128 devices in a mesh: strike: 32 (over y, z, core), depth: 4 (over x).
Axes of the slice: x: 4, y: 4, z: 4, core: 2. Of those that a mesh axis runs over, the one named last changes fastest.
Arguments:
- dofs: float32 [27, 20, 65536], P(None, None, ('strike', 'depth')), may hold values from -6 to 6
- star: float32 [3, 9, 9, 65536], P(None, None, None, ('strike', 'depth')), may hold values from -1.25 to 1.25
- kdiff: float32 [3, 20, 20], replicated, may hold values from -1.25 to 1.25
- couple: float32 [3, 6, 65536], P(None, None, ('strike', 'depth')), may hold values from 0.1 to 1
- omega: float32 [3, 65536], P(None, ('strike', 'depth')), may hold values from 0.2 to 2
- flux_minus: float32 [9, 9, 65536], P(None, None, ('strike', 'depth')), may hold values from -1.5 to 1.5
- flux_plus: float32 [9, 9, 65536], P(None, None, ('strike', 'depth')), may hold values from -1.5 to 1.5
- area: float32 [4, 65536], P(None, ('strike', 'depth')), may hold values from 0.5 to 2
- face_proj: float32 [4, 20, 16], replicated, may hold values from -1.25 to 1.25
- face_lift: float32 [4, 16, 20], replicated, may hold values from -0.75 to 0.75
- nbr_elem: int32 [4, 65536], P(None, ('strike', 'depth')), may hold values from 0 to 1023, as said below
- nbr_face: int32 [4, 65536], P(None, ('strike', 'depth')), may hold values from 0 to 3
- weight_class: int32 [65536], P(('strike', 'depth')), may hold values from 0 to 2
- send_rows: int32 [4, 16384], P(None, ('strike', 'depth')), may hold values from 0 to 511
- fault_send_elem: int32 [128, 2048], P(('strike', 'depth')), may hold values from 0 to 511
- fault_send_face: int32 [128, 2048], P(('strike', 'depth')), may hold values from 0 to 3
- fault_minus_elem: int32 [128, 2048], P(('strike', 'depth')), may hold values from 0 to 511
- fault_minus_face: int32 [128, 2048], P(('strike', 'depth')), may hold values from 0 to 3
- fault_live: int32 [128, 2048], P(('strike', 'depth')), may hold values from 0 to 1
- normal_load: float32 [128, 16, 2048], P(('strike', 'depth')), may hold values from 0.5 to 2
- state: float32 [128, 16, 2048], P(('strike', 'depth')), may hold values from 1 to 30
Outputs:
- dofs_next: float32 [27, 20, 65536], P(None, None, ('strike', 'depth'))
The draws below stay inside these ranges and needn't reach their ends.
Inputs may be any that keep to these rules, and one draw needn't show every extreme that they name: Where nbr_elem is 512 + k * 128 + b, nbr_face is k.
All inputs are finite; a program needn't handle non-finite values.
Results may differ from the reference program's by a relative error of at most 0.0003.
Values sent between devices are 32-bit elements; how exact they have to be, the bound alone decides.
No kernel may reach another device: no remote copies, remote signals or barrier semaphores. Data moves between devices by JAX's collectives and lax.ppermute only.
A program may use at most 256 MiB of HBM per device.

```python
import math
import jax
import jax.numpy as jnp
from jax import lax

NQ = 27
NE = 9
MECH = 3
NB = 20
NP = 16
ORDER = 4
NEWTON = 4
E_DEV = 512
CAP = 16
BND = 128
ELEMS = 65536
SLOTS = 2048
N_STRIKE = 32
N_DEPTH = 4
DEVICES = 128


def neighbour_table(key):
    keys = jax.random.split(key, 4)
    local = jax.random.randint(keys[0], (4, ELEMS), 0, E_DEV)
    rowpick = jax.random.randint(keys[1], (4, ELEMS), 0, BND)
    use_rim = jax.random.randint(keys[2], (4, ELEMS), 0, 8) == 0
    other = jax.random.randint(keys[3], (4, ELEMS), 0, 4)
    facing = jnp.broadcast_to(jnp.arange(4, dtype=jnp.int32)[:, None], (4, ELEMS))
    element = jnp.where(use_rim, E_DEV + facing * BND + rowpick, local)
    partner = jnp.where(use_rim, facing, other)
    return (element.astype(jnp.int32), partner.astype(jnp.int32))


def draw_nbr_elem(key, part):
    element, partner = neighbour_table(key)
    return element


def draw_nbr_face(key, part):
    element, partner = neighbour_table(key)
    return partner


def draw_fault_live(key, part):
    key = jax.random.fold_in(key, 5)
    receiver = jnp.arange(DEVICES, dtype=jnp.int32)[:, None] // N_DEPTH
    source = jnp.arange(DEVICES * CAP, dtype=jnp.int32)[None, :] // CAP // N_DEPTH
    near = jnp.abs(receiver - source) <= 1
    rolled = jax.random.randint(key, (DEVICES, DEVICES * CAP), 0, 16)
    return jnp.where(near, rolled < 15, rolled < 8).astype(jnp.int32)


def plant(values, stream_key, least, top_value):
    extent = values.shape
    spot = [jax.random.randint(jax.random.fold_in(stream_key, axis), (), 0, extent[axis]) for axis in range(len(extent))]
    values = values.at[tuple(spot)].set(least)
    longest = extent.index(max(extent))
    spot[longest] = (spot[longest] + 1) % extent[longest]
    return values.at[tuple(spot)].set(top_value)


def block_levels(stream_key, extent, pieces, least, top_value):
    level, own = 1.0, jax.random.fold_in(stream_key, 6)
    for axis_at, shards_of in pieces:
        draws = jnp.exp(jax.random.uniform(jax.random.fold_in(own, axis_at), (shards_of,), jnp.float32, least / len(pieces), top_value / len(pieces)))
        level = level * jnp.repeat(draws, extent[axis_at] // shards_of).reshape([-1 if axis == axis_at else 1 for axis in range(len(extent))])
    return level


def normal_values(rng, dims, spread, limit, pieces=(), kind=jnp.bfloat16):
    level = block_levels(rng, dims, pieces, -0.22, 0.18) if pieces else 1.0
    array = jax.random.normal(rng, dims, jnp.float32) * spread * level
    return jnp.minimum(jnp.maximum(array, -limit), limit).astype(kind)


def setup_inputs(seed: int = 0) -> dict:
    splits = jax.random.split(jax.random.key(seed), 22)
    return {
        "dofs": normal_values(splits[0], (NQ, NB, ELEMS), 1.0, 6.0, ((2, 128),), jnp.float32),
        "star": normal_values(splits[1], (3, NE, NE, ELEMS), (3 * NE) ** -0.5, 1.25, ((3, 128),), jnp.float32),
        "kdiff": normal_values(splits[2], (3, NB, NB), NB ** -0.5, 1.25, (), jnp.float32),
        "couple": jnp.clip(jnp.exp(math.log(1.0) - 2.3025851 * jax.random.uniform(splits[3], (MECH, 6, ELEMS), jnp.float32) ** block_levels(splits[3], (MECH, 6, ELEMS), ((2, 128),), -0.2, 0.2)), 0.1, 1.0),
        "omega": jnp.clip(jnp.exp(math.log(2.0) - 2.3025851 * jax.random.uniform(splits[4], (MECH, ELEMS), jnp.float32) ** block_levels(splits[4], (MECH, ELEMS), ((1, 128),), -0.2, 0.2)), 0.2, 2.0),
        "flux_minus": normal_values(splits[5], (NE, NE, ELEMS), (2 * NE) ** -0.5, 1.5, ((2, 128),), jnp.float32),
        "flux_plus": normal_values(splits[6], (NE, NE, ELEMS), (2 * NE) ** -0.5, 1.5, ((2, 128),), jnp.float32),
        "area": jnp.clip(jnp.exp(math.log(2.0) - 1.3862944 * jax.random.uniform(splits[7], (4, ELEMS), jnp.float32) ** block_levels(splits[7], (4, ELEMS), ((1, 128),), -0.2, 0.2)), 0.5, 2.0),
        "face_proj": normal_values(splits[8], (4, NB, NP), NB ** -0.5, 1.25, (), jnp.float32),
        "face_lift": normal_values(splits[9], (4, NP, NB), (4 * NP) ** -0.5, 0.75, (), jnp.float32),
        "nbr_elem": draw_nbr_elem(jax.random.fold_in(splits[21], 71), 0),
        "nbr_face": draw_nbr_face(jax.random.fold_in(splits[21], 71), 0),
        "weight_class": plant(jax.random.randint(splits[12], (ELEMS,), 0, 3), jax.random.fold_in(splits[12], 1), 0, 2).astype(jnp.int32),
        "send_rows": plant(jax.random.randint(splits[13], (4, BND * DEVICES), 0, E_DEV), jax.random.fold_in(splits[13], 1), 0, E_DEV - 1).astype(jnp.int32),
        "fault_send_elem": plant(jax.random.randint(splits[14], (DEVICES, SLOTS), 0, E_DEV), jax.random.fold_in(splits[14], 1), 0, E_DEV - 1).astype(jnp.int32),
        "fault_send_face": plant(jax.random.randint(splits[15], (DEVICES, SLOTS), 0, 4), jax.random.fold_in(splits[15], 1), 0, 3).astype(jnp.int32),
        "fault_minus_elem": plant(jax.random.randint(splits[16], (DEVICES, SLOTS), 0, E_DEV), jax.random.fold_in(splits[16], 1), 0, E_DEV - 1).astype(jnp.int32),
        "fault_minus_face": plant(jax.random.randint(splits[17], (DEVICES, SLOTS), 0, 4), jax.random.fold_in(splits[17], 1), 0, 3).astype(jnp.int32),
        "fault_live": draw_fault_live(jax.random.fold_in(splits[21], 71), 0),
        "normal_load": jnp.clip(jnp.exp(math.log(2.0) - 1.3862944 * jax.random.uniform(splits[19], (DEVICES, NP, SLOTS), jnp.float32) ** block_levels(splits[19], (DEVICES, NP, SLOTS), ((0, 128),), -0.2, 0.2)), 0.5, 2.0),
        "state": jnp.clip(jnp.exp(math.log(30.0) - 3.4011974 * jax.random.uniform(splits[20], (DEVICES, NP, SLOTS), jnp.float32) ** block_levels(splits[20], (DEVICES, NP, SLOTS), ((0, 128),), -0.2, 0.2)), 1.0, 30.0),
    }


ETA = 1.0
AFRIC = 0.5
HIGH = lax.Precision.HIGHEST

def inverse_sine(value):
    magnitude = jnp.abs(value)
    return jnp.sign(value) * jnp.log(magnitude + jnp.sqrt(1.0 + magnitude * magnitude))

def derive(field, star, kdiff, couple, omega):
    count = field.shape[-1]
    grads = jnp.einsum('jce,dcb->djbe', field[:NE], kdiff, precision=HIGH)
    stress = jnp.einsum('dije,djbe->ibe', star, grads, precision=HIGH)
    memory = field[NE:].reshape(MECH, 6, NB, count)
    relax = lax.optimization_barrier(jnp.sum(couple[:, :, None, :] * memory, axis=0))
    upper = stress[:6] - relax
    d_mem = omega[:, None, None, :] * (stress[None, :6] - memory)
    return jnp.concatenate([upper, stress[6:], d_mem.reshape(MECH * 6, NB, count)], 0)

def predict(dofs, star, kdiff, couple, omega, weight_class):
    step = 1.0 / (1.0 + weight_class.astype(dofs.dtype))
    term = dofs
    power = step
    integ = step * dofs
    for order in range(1, ORDER):
        term = derive(term, star, kdiff, couple, omega)
        power = power * step / (order + 1)
        integ = integ + power * term
    return integ

def friction(minus, plus, load, state):
    trial = 0.5 * (minus[..., 1, :, :] + plus[..., 1, :, :]) + 0.5 * ETA * (plus[..., 2, :, :] - minus[..., 2, :, :])
    sigma = load * (1.0 + 0.5 * jnp.tanh(0.5 * (minus[..., 0, :, :] + plus[..., 0, :, :])))
    slip = jnp.zeros_like(trial)
    for turn in range(NEWTON):
        scaled = state * slip
        resid = trial - ETA * slip - AFRIC * sigma * inverse_sine(scaled)
        slope = -ETA - AFRIC * sigma * state / jnp.sqrt(1.0 + scaled * scaled)
        slip = slip - resid / slope
    return (trial - ETA * slip, slip)

def reference(dofs, star, kdiff, couple, omega, flux_minus, flux_plus, area, face_proj, face_lift, nbr_elem, nbr_face, weight_class, send_rows, fault_send_elem, fault_send_face, fault_minus_elem, fault_minus_face, fault_live, normal_load, state):
    strike_n = N_STRIKE
    depth_n = N_DEPTH
    integ = predict(dofs, star, kdiff, couple, omega, weight_class)
    volume = derive(integ, star, kdiff, couple, omega)
    faces = jnp.einsum('ibe,fbp->fipe', integ[:NE], face_proj, precision=HIGH)
    grid = faces.reshape(4, NE, NP, strike_n, depth_n, E_DEV)
    rows = send_rows.reshape(4, strike_n, depth_n, BND)
    sent = []
    for k in range(4):
        index = jnp.broadcast_to(rows[k][None, None], (NE, NP, strike_n, depth_n, BND))
        sent.append(jnp.take_along_axis(grid[k], index, axis=-1))
    blank_s = jnp.zeros_like(sent[0][:, :, :1])
    blank_d = jnp.zeros_like(sent[0][:, :, :, :1])
    block0 = jnp.concatenate([blank_s, sent[0][:, :, :-1]], 2)
    block1 = jnp.concatenate([sent[1][:, :, 1:], blank_s], 2)
    block2 = jnp.concatenate([blank_d, sent[2][:, :, :, :-1]], 3)
    block3 = jnp.concatenate([sent[3][:, :, :, 1:], blank_d], 3)
    rim = jnp.stack([block0, block1, block2, block3], 0)
    table = jnp.concatenate([grid, rim], -1)
    span = E_DEV + BND
    table = jnp.transpose(table, (1, 2, 3, 4, 0, 5)).reshape(NE, NP, strike_n, depth_n, 4 * span)
    elem = nbr_elem.reshape(4, strike_n, depth_n, E_DEV)
    fidx = nbr_face.reshape(4, strike_n, depth_n, E_DEV)
    flat = fidx * span + jnp.where(elem < E_DEV, elem, elem - fidx * BND)
    flat = jnp.transpose(flat, (1, 2, 0, 3)).reshape(strike_n, depth_n, 4 * E_DEV)
    flat = jnp.broadcast_to(flat[None, None], (NE, NP, strike_n, depth_n, 4 * E_DEV)).astype(jnp.int32)
    neigh = jnp.take_along_axis(table, flat, axis=-1).reshape(NE, NP, strike_n, depth_n, 4, E_DEV)
    neigh = jnp.transpose(neigh, (4, 0, 1, 2, 3, 5)).reshape(4, NE, NP, ELEMS)
    mixed = jnp.einsum('ije,fjpe->fipe', flux_minus, faces, precision=HIGH) + jnp.einsum('ije,fjpe->fipe', flux_plus, neigh, precision=HIGH)
    flux = jnp.einsum('fe,fipe,fpb->ibe', area, mixed, face_lift, precision=HIGH)
    sel = faces[:, 0:7:3].reshape(4, 3, NP, DEVICES, E_DEV)
    lookup = jnp.transpose(sel, (3, 0, 4, 1, 2))
    dev = jnp.arange(DEVICES, dtype=jnp.int32)[:, None]
    plus_sent = lookup[dev, fault_send_face, fault_send_elem]
    plus_at = plus_sent.reshape(DEVICES, DEVICES, CAP, 3, NP).transpose(1, 0, 2, 3, 4).reshape(DEVICES, SLOTS, 3, NP)
    minus_at = lookup[dev, fault_minus_face, fault_minus_elem]
    minus = jnp.transpose(minus_at, (0, 2, 3, 1))
    plus = jnp.transpose(plus_at, (0, 2, 3, 1))
    traction, slip = friction(minus, plus, normal_load, state)
    live = fault_live.astype(dofs.dtype)[:, None, :]
    minus_term = jnp.stack([(traction - minus[:, 1]) * live, -0.5 * slip * live], 1)
    plus_term = jnp.stack([(traction - plus[:, 1]) * live, 0.5 * slip * live], 1)
    plus_home = plus_term.reshape(DEVICES, 2, NP, DEVICES, CAP).transpose(3, 1, 2, 0, 4).reshape(DEVICES, 2, NP, SLOTS)
    minus_add = jnp.einsum('dkps,dspb->kbds', minus_term, face_lift[fault_minus_face], precision=HIGH)
    plus_add = jnp.einsum('dkps,dspb->kbds', plus_home, face_lift[fault_send_face], precision=HIGH)
    delta = jnp.zeros((2, NB, DEVICES, E_DEV), dofs.dtype)
    delta = delta.at[:, :, dev, fault_minus_elem].add(minus_add)
    delta = delta.at[:, :, dev, fault_send_elem].add(plus_add)
    delta = delta.reshape(2, NB, ELEMS)
    elastic = dofs[:NE] + volume[:NE] + flux
    elastic = elastic.at[3].add(delta[0]).at[6].add(delta[1])
    return jnp.concatenate([elastic, dofs[NE:] + volume[NE:]], 0)
```

```python
import jax
import jax.numpy as jnp
from jax import lax
from jax.experimental import pallas as pl
from jax.experimental.pallas import tpu as pltpu
from jax.sharding import PartitionSpec as P

NQ = 27
NE = 9
MECH = 3
NB = 20
NP = 16
ORDER = 4
NEWTON = 4
ETA = 1.0
AFRIC = 0.5
E_DEV = 512
BND = 128
SLOTS = 2048
DEVICES = 128
NBP = 24
LANES = 128
CHUNKS = E_DEV // LANES
ROWS = 224
SC = 512
WIDTH = 12 * 128 + 16
F32 = jnp.float32
BF = jnp.bfloat16
VMEM = 56 * 1024 * 1024
FAULT_ROWS = (0, 3, 6)


def split(x):
    hi = x.astype(BF)
    return hi, (x - hi.astype(F32)).astype(BF)


def pad_rows(x, rows):
    extra = rows - x.shape[0]
    if extra == 0:
        return x
    return jnp.concatenate([x, jnp.zeros((extra,) + x.shape[1:], x.dtype)], axis=0)


def stack3(x):
    hi, lo = split(x)
    return jnp.concatenate([hi, hi, lo], axis=0)


def left3(scratch, parts, depth, rows):
    scratch[...] = jnp.zeros(scratch.shape, F32)
    for row, col, value in parts:
        scratch[row : row + value.shape[0], col : col + value.shape[1]] = value
    whole = scratch[0:depth, :]
    hi = whole.astype(BF).astype(F32)
    lo = whole - hi
    tall = jnp.concatenate([hi, lo, hi], axis=0)
    tall = pad_rows(tall, -(-tall.shape[0] // 128) * 128)
    return jnp.transpose(tall, (1, 0))[0:rows, 0 : 3 * depth].astype(BF)


def dot(a, b):
    return lax.dot_general(a, b, (((1,), (0,)), ((), ())), preferred_element_type=F32)


def dot_nt(a, b):
    return lax.dot_general(a, b, (((1,), (1,)), ((), ())), preferred_element_type=F32)


def one_hot(index, rows, base=0):
    row = lax.broadcasted_iota(jnp.int32, (rows, index.shape[1]), 0) + base
    return jnp.where(row == index, 1.0, 0.0).astype(BF)


def swap_blocks(x):
    x = pltpu.roll(x, 0, 1, stride=16, stride_axis=0)
    lane = lax.broadcasted_iota(jnp.int32, (8, LANES), 1)
    sub = lax.broadcasted_iota(jnp.int32, (8, LANES), 0)
    down = jnp.bitwise_and(lane // 16 - sub, 7)
    across = jnp.bitwise_and(lane + 16 * sub, LANES - 1)
    tiles = []
    for t in range(x.shape[0] // 8):
        y = jnp.take_along_axis(x[8 * t : 8 * t + 8], down, axis=0, mode="promise_in_bounds")
        tiles.append(jnp.take_along_axis(y, across, axis=1, mode="promise_in_bounds"))
    return jnp.concatenate(tiles, axis=0)


def to_blocks(x):
    return swap_blocks(
        jnp.concatenate([x[:, t * LANES : (t + 1) * LANES] for t in range(SC // LANES)], axis=0)
    )


def to_slots(x):
    x = swap_blocks(x)
    return jnp.concatenate([x[8 * t : 8 * t + 8] for t in range(SC // LANES)], axis=1)


def stress_of(get, star_ref, kd, grads):
    right = jnp.concatenate([stack3(pad_rows(get(j), 32)) for j in range(NE)], axis=1)
    grads[...] = dot(kd, right)
    acc = [None] * NE
    for d in range(3):
        for j in range(NE):
            g = grads[d * NBP : (d + 1) * NBP, j * LANES : (j + 1) * LANES]
            for i in range(NE):
                t = star_ref[d, i, j : j + 1, :] * g
                acc[i] = t if acc[i] is None else acc[i] + t
    return acc


def predict_kernel(
    dofs, star, couple, omega, wc, kdiff, proj, srow, fse, fsf, fme, fmf, live, load, state,
    integ, ihl, send0, send1, send2, send3, out, keep,
    term, grads, mat, kdw, fpw, fhl,
):
    c = pl.program_id(0)

    @pl.when(c == 0)
    def _():
        kdw[...] = left3(mat, [(0, d * NBP, kdiff[d]) for d in range(3)], 32, 80)
        fpw[...] = left3(mat, [(0, g * NP, proj[g]) for g in range(4)], 32, 64)
        term[...] = jnp.zeros(term.shape, F32)

    kd = kdw[...]
    step = 1.0 / (1.0 + wc[...].astype(F32))
    for q in range(NQ):
        term[q, 0:NB, :] = dofs[q]
    for q in range(NQ):
        integ[q] = step * term[q]

    def turn(order, power):
        acc = stress_of(lambda j: term[j], star, kd, grads)
        for q in range(6):
            old = [term[NE + 6 * l + q] for l in range(MECH)]
            relax = couple[0, q : q + 1, :] * old[0]
            for l in range(1, MECH):
                relax = relax + couple[l, q : q + 1, :] * old[l]
            term[q] = acc[q] - relax
            for l in range(MECH):
                term[NE + 6 * l + q] = omega[l : l + 1, :] * (acc[q] - old[l])
        for q in range(6, NE):
            term[q] = acc[q]
        power = power * step / (order + 2).astype(F32)
        for q in range(NQ):
            integ[q] += power * term[q]
        return power

    lax.fori_loop(0, ORDER - 1, turn, step)

    here = pl.ds(pl.multiple_of(c * LANES, LANES), LANES)
    flat = pad_rows(integ[0:NE].reshape(NE * NBP, LANES), ROWS)
    hi, lo = split(flat)
    ihl[0:ROWS, here] = hi
    ihl[ROWS : 2 * ROWS, here] = lo
    hi, lo = split(pad_rows(jnp.concatenate([integ[r] for r in FAULT_ROWS], axis=0), 80))
    fhl[0:80, here] = hi
    fhl[80:160, here] = lo

    @pl.when(c == CHUNKS - 1)
    def _():
        rows = jnp.concatenate([srow[k : k + 1, :] for k in range(4)], axis=1)
        got = dot(ihl[...], one_hot(rows, E_DEV))
        got = got[0:ROWS] + got[ROWS : 2 * ROWS]
        for k, ref in enumerate((send0, send1, send2, send3)):
            for j in range(NE):
                ref[j] = got[j * NBP : j * NBP + NB, k * BND : (k + 1) * BND]

        def fault_values(elem, face):
            x = dot(fhl[...], one_hot(elem, E_DEV))
            right = []
            for r in range(3):
                h = pad_rows(x[r * NBP : (r + 1) * NBP], 32).astype(BF)
                l = pad_rows(x[80 + r * NBP : 80 + (r + 1) * NBP], 32).astype(BF)
                right.append(jnp.concatenate([h, h, l], axis=0))
            points = dot(fpw[...], jnp.concatenate(right, axis=1))
            values = []
            for r in range(3):
                cols = slice(r * SC, (r + 1) * SC)
                v = points[0:NP, cols]
                for g in range(1, 4):
                    v = jnp.where(face == g, points[g * NP : (g + 1) * NP, cols], v)
                values.append(v)
            return values

        def chunk(s, carry):
            cols = pl.ds(pl.multiple_of(s * SC, SC), SC)
            lines = pl.ds(pl.multiple_of(s * (SC // 16), SC // 16), SC // 16)
            plus = fault_values(fse[:, cols], fsf[:, cols])
            minus = fault_values(fme[:, cols], fmf[:, cols])
            sent = (
                plus[1] + plus[2], plus[0], minus[1] - minus[2], minus[0],
                load[0, :, cols], state[0, :, cols],
            )
            for n, x in enumerate(sent):
                for g in range(2):
                    at = (2 * n + g) * LANES
                    out[lines, at : at + LANES] = to_blocks(x[8 * g : 8 * g + 8])
            for n, x in enumerate((plus[1], minus[1])):
                for g in range(2):
                    at = (2 * n + g) * LANES
                    keep[lines, at : at + LANES] = to_blocks(x[8 * g : 8 * g + 8])
            alive = jnp.broadcast_to(live[:, cols].astype(F32), (8, SC))
            out[lines, 12 * LANES : WIDTH] = to_blocks(alive)[:, 0:16]
            return carry

        lax.fori_loop(0, SLOTS // SC, chunk, 0)


def element_kernel(
    integ, dofs, star, couple, omega, fminus, fplus, area, nelem, nface, ihl, rim0, rim1, rim2, rim3,
    kdiff, proj, lift, base, grads, mat, kdw, fpw, ltw, plw, rhl, own, near,
):
    c = pl.program_id(0)

    @pl.when(c == 0)
    def _():
        kdw[...] = left3(mat, [(0, d * NBP, kdiff[d]) for d in range(3)], 32, 80)
        fpw[...] = left3(mat, [(0, g * NP, proj[g]) for g in range(4)], 32, 64)
        ltw[...] = left3(mat, [(f * NP, 0, lift[f]) for f in range(4)], 64, 32)
        both = [
            lax.dot_general(
                proj[f], lift[f], (((1,), (0,)), ((), ())),
                precision=lax.Precision.HIGHEST, preferred_element_type=F32,
            )
            for f in range(4)
        ]
        plw[...] = left3(mat, [(0, f * NBP, both[f]) for f in range(4)], 32, 96)
        for k, ref in enumerate((rim0, rim1, rim2, rim3)):
            flat = jnp.concatenate([pad_rows(ref[j], NBP) for j in range(NE)], axis=0)
            hi, lo = split(pad_rows(flat, ROWS))
            rhl[0:ROWS, k * BND : (k + 1) * BND] = hi
            rhl[ROWS : 2 * ROWS, k * BND : (k + 1) * BND] = lo

    elem = jnp.concatenate([nelem[f : f + 1, :] for f in range(4)], axis=1)
    face = jnp.concatenate([nface[f : f + 1, :] for f in range(4)], axis=1)
    scale = jnp.concatenate([area[f : f + 1, :] for f in range(4)], axis=1)
    got = dot(ihl[...], one_hot(elem, E_DEV)) + dot(rhl[...], one_hot(elem, 4 * BND, E_DEV))
    lifted = []
    for j in range(NE):
        h = pad_rows(got[j * NBP : (j + 1) * NBP], 32).astype(BF)
        l = pad_rows(got[ROWS + j * NBP : ROWS + (j + 1) * NBP], 32).astype(BF)
        points = dot(fpw[...], jnp.concatenate([h, h, l], axis=0))
        v = points[0:NP]
        for g in range(1, 4):
            v = jnp.where(face == g, points[g * NP : (g + 1) * NP], v)
        v = v * scale
        v = jnp.concatenate([v[:, f * LANES : (f + 1) * LANES] for f in range(4)], axis=0)
        lifted.append(stack3(v))
    near[...] = dot(ltw[...], jnp.concatenate(lifted, axis=1))

    right = jnp.concatenate([stack3(pad_rows(integ[j], 32)) for j in range(NE)], axis=1)
    folded = dot(plw[...], right)
    for j in range(NE):
        cols = slice(j * LANES, (j + 1) * LANES)
        w = area[0:1, :] * folded[0:NBP, cols]
        for f in range(1, 4):
            w = w + area[f : f + 1, :] * folded[f * NBP : (f + 1) * NBP, cols]
        own[:, cols] = w

    acc = stress_of(lambda j: integ[j], star, kdw[...], grads)
    total = []
    for q in range(6):
        old = [integ[NE + 6 * l + q] for l in range(MECH)]
        relax = couple[0, q : q + 1, :] * old[0]
        for l in range(1, MECH):
            relax = relax + couple[l, q : q + 1, :] * old[l]
        for l in range(MECH):
            at = NE + 6 * l + q
            base[at] = dofs[at] + (omega[l : l + 1, :] * (acc[q] - old[l]))[0:NB]
        total.append(acc[q] - relax)
    total = total + acc[6:]
    for j in range(NE):
        cols = slice(j * LANES, (j + 1) * LANES)
        w, v = own[:, cols], near[0:NBP, cols]
        for i in range(NE):
            total[i] = total[i] + (fminus[i, j : j + 1, :] * w + fplus[i, j : j + 1, :] * v)
    for i in range(NE):
        base[i] = dofs[i] + total[i][0:NB]


def friction(trial, pressure, load, state):
    sigma = load * (1.0 + 0.5 * jnp.tanh(0.5 * pressure))
    half = AFRIC * sigma
    slip = trial / (ETA + half * state)
    for turn in range(NEWTON - 1):
        scaled = state * slip
        size = jnp.abs(scaled)
        root = jnp.sqrt(1.0 + size * size)
        arc = jnp.log(size + root)
        arc = jnp.where(scaled < 0.0, -arc, arc)
        resid = trial - ETA * slip - half * arc
        slip = slip + resid * root / (ETA * root + half * state)
    return trial - ETA * slip, slip


def fault_kernel(
    base_in, mine, theirs, keep, fse, fsf, fme, fmf, live, lift,
    base, mat, lfw, acc, rows, sem,
):
    del base_in
    reads = [
        pltpu.make_async_copy(base.at[FAULT_ROWS[1 + k]], rows.at[k], sem.at[k]) for k in range(2)
    ]
    for copy in reads:
        copy.start()
    lfw[...] = left3(mat, [(0, f * NBP, lift[f]) for f in range(4)], 16, 96)
    acc[...] = jnp.zeros(acc.shape, F32)

    def chunk(s, carry):
        cols = pl.ds(pl.multiple_of(s * SC, SC), SC)
        lines = pl.ds(pl.multiple_of(s * (SC // 16), SC // 16), SC // 16)

        def pair(ref, n):
            return ref[lines, n * 256 : (n + 1) * 256]

        pull, slip = friction(
            0.5 * (pair(theirs, 0) + pair(mine, 2)), pair(mine, 3) + pair(theirs, 1),
            pair(mine, 4), pair(mine, 5),
        )
        terms = [pull - pair(keep, 1), -0.5 * slip]
        pull, slip = friction(
            0.5 * (pair(mine, 0) + pair(theirs, 2)), pair(theirs, 3) + pair(mine, 1),
            pair(theirs, 4), pair(theirs, 5),
        )
        terms += [pull - pair(keep, 0), 0.5 * slip]
        right = []
        for t in terms:
            x = jnp.concatenate([to_slots(t[:, 0:LANES]), to_slots(t[:, LANES:256])], axis=0)
            right.append(stack3(x))
        added = dot(lfw[...], jnp.concatenate(right, axis=1))
        far = jnp.concatenate(
            [theirs[lines, 12 * LANES : WIDTH], jnp.zeros((SC // 16, LANES - 16), F32)], axis=1
        )
        far = to_slots(far)[0:1]
        left = []
        for side, (alive, face) in enumerate(
            ((live[:, cols].astype(F32), fmf[:, cols]), (far, fsf[:, cols]))
        ):
            mask = [jnp.where(face == f, alive, 0.0) for f in range(4)]
            sums = []
            for k in range(2):
                at = slice((2 * side + k) * SC, (2 * side + k + 1) * SC)
                y = mask[0] * added[0:NBP, at]
                for f in range(1, 4):
                    y = y + mask[f] * added[f * NBP : (f + 1) * NBP, at]
                sums.append(y)
            hi, lo = split(jnp.concatenate(sums, axis=0))
            left.append(jnp.concatenate([hi, lo], axis=0))
        spots = jnp.concatenate([one_hot(fme[:, cols], E_DEV), one_hot(fse[:, cols], E_DEV)], axis=1)
        acc[...] += dot_nt(jnp.concatenate(left, axis=1), spots)
        return carry

    lax.fori_loop(0, SLOTS // SC, chunk, 0)
    delta = acc[0:48] + acc[48:96]
    for copy in reads:
        copy.wait()
    for k in range(2):
        rows[k] = rows[k] + delta[k * NBP : k * NBP + NB]
    writes = [
        pltpu.make_async_copy(rows.at[k], base.at[FAULT_ROWS[1 + k]], sem.at[k]) for k in range(2)
    ]
    for copy in writes:
        copy.start()
    for copy in writes:
        copy.wait()


def whole(shape):
    return pl.BlockSpec(shape, lambda *i: (0,) * len(shape))


def lanes(*lead):
    return pl.BlockSpec(lead + (LANES,), lambda c: (0,) * len(lead) + (c,))


def per_device(
    dofs, star, kdiff, couple, omega, flux_minus, flux_plus, area, face_proj, face_lift,
    nbr_elem, nbr_face, weight_class, send_rows, fault_send_elem, fault_send_face,
    fault_minus_elem, fault_minus_face, fault_live, normal_load, state,
):
    shape = jax.ShapeDtypeStruct
    wc = weight_class.reshape(1, E_DEV)
    slot = whole((1, SLOTS))
    point = whole((1, NP, SLOTS))
    rim = whole((NE, NB, BND))
    params = pltpu.CompilerParams(vmem_limit_bytes=VMEM)
    integ, ihl, s0, s1, s2, s3, out, keep = pl.pallas_call(
        predict_kernel,
        grid=(CHUNKS,),
        in_specs=[
            lanes(NQ, NB), lanes(3, NE, NE), lanes(MECH, 6), lanes(MECH), lanes(1),
            whole((3, NB, NB)), whole((4, NB, NP)), whole((4, BND)),
            slot, slot, slot, slot, slot, point, point,
        ],
        out_specs=[
            lanes(NQ, NBP), whole((2 * ROWS, E_DEV)), rim, rim, rim, rim,
            whole((DEVICES, WIDTH)), whole((DEVICES, 4 * LANES)),
        ],
        out_shape=[
            shape((NQ, NBP, E_DEV), F32), shape((2 * ROWS, E_DEV), BF),
            *[shape((NE, NB, BND), F32)] * 4,
            shape((DEVICES, WIDTH), F32), shape((DEVICES, 4 * LANES), F32),
        ],
        scratch_shapes=[
            pltpu.VMEM((NQ, NBP, LANES), F32), pltpu.VMEM((80, NE * LANES), F32),
            pltpu.VMEM((64, LANES), F32), pltpu.VMEM((80, 96), BF), pltpu.VMEM((64, 96), BF),
            pltpu.VMEM((160, E_DEV), BF),
        ],
        compiler_params=params,
        name="predict",
    )(
        dofs, star, couple, omega, wc, kdiff, face_proj, send_rows, fault_send_elem, fault_send_face,
        fault_minus_elem, fault_minus_face, fault_live, normal_load, state,
    )
    ns, nd = lax.axis_size("strike"), lax.axis_size("depth")

    def onward(n):
        return [(i, i + 1) for i in range(n - 1)]

    def back(n):
        return [(i + 1, i) for i in range(n - 1)]

    r0 = lax.ppermute(s0, "strike", onward(ns))
    r1 = lax.ppermute(s1, "strike", back(ns))
    r2 = lax.ppermute(s2, "depth", onward(nd))
    r3 = lax.ppermute(s3, "depth", back(nd))
    theirs = lax.all_to_all(out, ("strike", "depth"), split_axis=0, concat_axis=0, tiled=True)
    base = pl.pallas_call(
        element_kernel,
        grid=(CHUNKS,),
        in_specs=[
            lanes(NQ, NBP), lanes(NQ, NB), lanes(3, NE, NE), lanes(MECH, 6), lanes(MECH),
            lanes(NE, NE), lanes(NE, NE), lanes(4), lanes(4), lanes(4),
            whole((2 * ROWS, E_DEV)), rim, rim, rim, rim,
            whole((3, NB, NB)), whole((4, NB, NP)), whole((4, NP, NB)),
        ],
        out_specs=lanes(NQ, NB),
        out_shape=shape((NQ, NB, E_DEV), F32),
        scratch_shapes=[
            pltpu.VMEM((80, NE * LANES), F32), pltpu.VMEM((64, LANES), F32),
            pltpu.VMEM((80, 96), BF), pltpu.VMEM((64, 96), BF), pltpu.VMEM((32, 192), BF),
            pltpu.VMEM((96, 96), BF), pltpu.VMEM((2 * ROWS, 4 * BND), BF),
            pltpu.VMEM((NBP, NE * LANES), F32), pltpu.VMEM((32, NE * LANES), F32),
        ],
        compiler_params=params,
        name="elements",
    )(
        integ, dofs, star, couple, omega, flux_minus, flux_plus, area, nbr_elem, nbr_face,
        ihl, r0, r1, r2, r3, kdiff, face_proj, face_lift,
    )
    anywhere = pl.BlockSpec(memory_space=pl.ANY)
    local = pl.BlockSpec(memory_space=pltpu.VMEM)
    return pl.pallas_call(
        fault_kernel,
        in_specs=[anywhere] + [local] * 9,
        out_specs=anywhere,
        out_shape=shape((NQ, NB, E_DEV), F32),
        input_output_aliases={0: 0},
        scratch_shapes=[
            pltpu.VMEM((64, LANES), F32), pltpu.VMEM((96, 48), BF), pltpu.VMEM((96, E_DEV), F32),
            pltpu.VMEM((2, NB, E_DEV), F32), pltpu.SemaphoreType.DMA((2,)),
        ],
        compiler_params=params,
        name="fault",
    )(
        base, out, theirs, keep, fault_send_elem, fault_send_face, fault_minus_elem,
        fault_minus_face, fault_live, face_lift,
    )


def solution(mesh):
    both = ("strike", "depth")
    split_1, split_2, split_3 = P(None, both), P(None, None, both), P(None, None, None, both)
    in_specs = (
        split_2, split_3, P(), split_2, split_1, split_2, split_2, split_1, P(), P(),
        split_1, split_1, P(both), split_1,
        *[P(both, None)] * 5, P(both, None, None), P(both, None, None),
    )
    return jax.shard_map(
        per_device, mesh=mesh, in_specs=in_specs, out_specs=split_2, check_vma=False
    )
```

```python
import jax
import jax.numpy as jnp
from jax import lax
from jax.experimental import pallas as pl
from jax.experimental.pallas import tpu as pltpu
from jax.sharding import PartitionSpec as P

NQ = 27
NE = 9
MECH = 3
NB = 20
NP = 16
ORDER = 4
NEWTON = 4
ETA = 1.0
AFRIC = 0.5
E_DEV = 512
BND = 128
SLOTS = 2048
DEVICES = 128
NBP = 24
LANES = 128
CHUNKS = E_DEV // LANES
ROWS = 224
SC = 512
TILES = 13
F32 = jnp.float32
BF = jnp.bfloat16
VMEM = 56 * 1024 * 1024
FAULT_ROWS = (0, 3, 6)


def split(x):
    hi = x.astype(BF)
    return hi, (x - hi.astype(F32)).astype(BF)


def pad_rows(x, rows):
    extra = rows - x.shape[0]
    if extra == 0:
        return x
    return jnp.concatenate([x, jnp.zeros((extra,) + x.shape[1:], x.dtype)], axis=0)


def stack3(x):
    hi, lo = split(x)
    return jnp.concatenate([hi, hi, lo], axis=0)


def left3(scratch, parts, depth, rows):
    scratch[...] = jnp.zeros(scratch.shape, F32)
    for row, col, value in parts:
        scratch[row : row + value.shape[0], col : col + value.shape[1]] = value
    whole = scratch[0:depth, :]
    hi = whole.astype(BF).astype(F32)
    lo = whole - hi
    tall = jnp.concatenate([hi, lo, hi], axis=0)
    tall = pad_rows(tall, -(-tall.shape[0] // 128) * 128)
    return jnp.transpose(tall, (1, 0))[0:rows, 0 : 3 * depth].astype(BF)


def dot(a, b):
    return lax.dot_general(a, b, (((1,), (0,)), ((), ())), preferred_element_type=F32)


def dot_nt(a, b):
    return lax.dot_general(a, b, (((1,), (1,)), ((), ())), preferred_element_type=F32)


def one_hot(index, rows, base=0):
    row = lax.broadcasted_iota(jnp.int32, (rows, index.shape[1]), 0) + base
    return jnp.where(row == index, 1.0, 0.0).astype(BF)


def swap_blocks(x):
    x = pltpu.roll(x, 0, 1, stride=16, stride_axis=0)
    lane = lax.broadcasted_iota(jnp.int32, (8, LANES), 1)
    sub = lax.broadcasted_iota(jnp.int32, (8, LANES), 0)
    down = jnp.bitwise_and(lane // 16 - sub, 7)
    across = jnp.bitwise_and(lane + 16 * sub, LANES - 1)
    tiles = []
    for t in range(x.shape[0] // 8):
        y = jnp.take_along_axis(x[8 * t : 8 * t + 8], down, axis=0, mode="promise_in_bounds")
        tiles.append(jnp.take_along_axis(y, across, axis=1, mode="promise_in_bounds"))
    return jnp.concatenate(tiles, axis=0)


def to_blocks(x):
    return swap_blocks(
        jnp.concatenate([x[:, t * LANES : (t + 1) * LANES] for t in range(SC // LANES)], axis=0)
    )


def to_slots(x):
    x = swap_blocks(x)
    return jnp.concatenate([x[8 * t : 8 * t + 8] for t in range(SC // LANES)], axis=1)


def stress_of(get, star_ref, kd, grads):
    right = jnp.concatenate([stack3(pad_rows(get(j), 32)) for j in range(NE)], axis=1)
    grads[...] = dot(kd, right)
    acc = [None] * NE
    for d in range(3):
        for j in range(NE):
            g = grads[d * NBP : (d + 1) * NBP, j * LANES : (j + 1) * LANES]
            for i in range(NE):
                t = star_ref[i, j, d : d + 1, :] * g
                acc[i] = t if acc[i] is None else acc[i] + t
    return acc


def predict_kernel(
    dofs, star, couple, omega, wc, kdiff, srow,
    integ, ihl, fhl, send0, send1, send2, send3,
    term, grads, mat, kdw,
):
    c = pl.program_id(0)

    @pl.when(c == 0)
    def _():
        kdw[...] = left3(mat, [(0, d * NBP, kdiff[d]) for d in range(3)], 32, 80)
        term[...] = jnp.zeros(term.shape, F32)

    kd = kdw[...]
    step = 1.0 / (1.0 + wc[...].astype(F32))
    term[:, 0:NB, :] = jnp.transpose(dofs[...], (1, 0, 2))
    for q in range(NQ):
        integ[q] = step * term[q]

    def turn(order, power):
        acc = stress_of(lambda j: term[j], star, kd, grads)
        for q in range(6):
            old = [term[NE + 6 * l + q] for l in range(MECH)]
            relax = couple[0, q : q + 1, :] * old[0]
            for l in range(1, MECH):
                relax = relax + couple[l, q : q + 1, :] * old[l]
            term[q] = acc[q] - relax
            for l in range(MECH):
                term[NE + 6 * l + q] = omega[l : l + 1, :] * (acc[q] - old[l])
        for q in range(6, NE):
            term[q] = acc[q]
        power = power * step / (order + 2).astype(F32)
        for q in range(NQ):
            integ[q] += power * term[q]
        return power

    lax.fori_loop(0, ORDER - 1, turn, step)

    here = pl.ds(pl.multiple_of(c * LANES, LANES), LANES)
    flat = pad_rows(integ[0:NE].reshape(NE * NBP, LANES), ROWS)
    hi, lo = split(flat)
    ihl[0:ROWS, here] = hi
    ihl[ROWS : 2 * ROWS, here] = lo
    hi, lo = split(pad_rows(jnp.concatenate([integ[r] for r in FAULT_ROWS], axis=0), 80))
    fhl[0:80, here] = hi
    fhl[80:160, here] = lo

    @pl.when(c == CHUNKS - 1)
    def _():
        rows = []
        for axis, k in (("strike", 0), ("depth", 2)):
            even = lax.axis_index(axis) % 2 == 0
            ahead, behind = srow[k : k + 1, :], srow[k + 1 : k + 2, :]
            rows += [jnp.where(even, ahead, behind), jnp.where(even, behind, ahead)]
        rows = jnp.concatenate(rows, axis=1)
        got = dot(ihl[...], one_hot(rows, E_DEV))
        got = got[0:ROWS] + got[ROWS : 2 * ROWS]
        for k, ref in enumerate((send0, send1, send2, send3)):
            for j in range(NE):
                ref[j] = got[j * NBP : j * NBP + NB, k * BND : (k + 1) * BND]


def fault_values(fhl, fpw, elem, face):
    x = dot(fhl[...], one_hot(elem, E_DEV))
    right = []
    for r in range(3):
        h = pad_rows(x[r * NBP : (r + 1) * NBP], 32).astype(BF)
        l = pad_rows(x[80 + r * NBP : 80 + (r + 1) * NBP], 32).astype(BF)
        right.append(jnp.concatenate([h, h, l], axis=0))
    points = dot(fpw[...], jnp.concatenate(right, axis=1))
    values = []
    for r in range(3):
        cols = slice(r * SC, (r + 1) * SC)
        v = points[0:NP, cols]
        for g in range(1, 4):
            v = jnp.where(face == g, points[g * NP : (g + 1) * NP, cols], v)
        values.append(v)
    return values


def slot_kernel(fhl, proj, fse, fsf, fme, fmf, live, load, state, out, keep, mat, fpw):
    @pl.when(pl.program_id(0) == 0)
    def _():
        fpw[...] = left3(mat, [(0, g * NP, proj[g].T) for g in range(4)], 32, 64)

    def place(tile, x):
        out[pl.ds(tile, SC // 16, stride=TILES), :] = to_blocks(x)

    place(12, jnp.broadcast_to(live[...].astype(F32), (8, SC)))
    plus = fault_values(fhl, fpw, fse[...], fsf[...])
    minus = fault_values(fhl, fpw, fme[...], fmf[...])
    sent = (
        plus[1] + plus[2], plus[0], minus[1] - minus[2], minus[0], load[0], state[0],
    )
    for n, x in enumerate(sent):
        for g in range(2):
            place(2 * n + g, x[8 * g : 8 * g + 8])
    for n, x in enumerate((plus[1], minus[1])):
        for g in range(2):
            at = (2 * n + g) * LANES
            keep[:, at : at + LANES] = to_blocks(x[8 * g : 8 * g + 8])


def element_kernel(
    integ, dofs, star, couple, omega, fminus, fplus, area, nelem, nface, ihl, rim0, rim1, rim2, rim3,
    kdiff, proj, lift, base, grads, mat, kdw, fpw, ltw, plw, rhl, own, near, change,
):
    c = pl.program_id(0)

    def put_rim(k, fields):
        flat = jnp.concatenate([pad_rows(x, NBP) for x in fields], axis=0)
        hi, lo = split(pad_rows(flat, ROWS))
        rhl[0:ROWS, k * BND : (k + 1) * BND] = hi
        rhl[ROWS : 2 * ROWS, k * BND : (k + 1) * BND] = lo

    @pl.when(c == 0)
    def _():
        kdw[...] = left3(mat, [(0, d * NBP, kdiff[d]) for d in range(3)], 32, 80)
        fpw[...] = left3(mat, [(0, g * NP, proj[g].T) for g in range(4)], 32, 64)
        ltw[...] = left3(mat, [(f * NP, 0, lift[f]) for f in range(4)], 64, 32)
        both = [
            lax.dot_general(
                proj[f], lift[f], (((0,), (0,)), ((), ())),
                precision=lax.Precision.HIGHEST, preferred_element_type=F32,
            )
            for f in range(4)
        ]
        plw[...] = left3(mat, [(0, f * NBP, both[f]) for f in range(4)], 32, 96)
        for k, first, second, axis in ((0, rim0, rim1, "strike"), (2, rim2, rim3, "depth")):
            at = lax.axis_index(axis)
            even = (at % 2 == 0).astype(F32)
            odd = 1.0 - even
            before = (at > 0).astype(F32)
            after = (at < lax.axis_size(axis) - 1).astype(F32)
            for side, one, two in ((k, odd * before, even * before), (k + 1, even * after, odd * after)):
                put_rim(side, [one * first[j] + two * second[j] for j in range(NE)])
    elem = jnp.concatenate([nelem[f : f + 1, :] for f in range(4)], axis=1)
    face = jnp.concatenate([nface[f : f + 1, :] for f in range(4)], axis=1)
    scale = jnp.concatenate([area[f : f + 1, :] for f in range(4)], axis=1)
    got = dot(ihl[...], one_hot(elem, E_DEV)) + dot(rhl[...], one_hot(elem, 4 * BND, E_DEV))
    lifted = []
    for j in range(NE):
        h = pad_rows(got[j * NBP : (j + 1) * NBP], 32).astype(BF)
        l = pad_rows(got[ROWS + j * NBP : ROWS + (j + 1) * NBP], 32).astype(BF)
        points = dot(fpw[...], jnp.concatenate([h, h, l], axis=0))
        v = points[0:NP]
        for g in range(1, 4):
            v = jnp.where(face == g, points[g * NP : (g + 1) * NP], v)
        v = v * scale
        v = jnp.concatenate([v[:, f * LANES : (f + 1) * LANES] for f in range(4)], axis=0)
        lifted.append(stack3(v))
    near[...] = dot(ltw[...], jnp.concatenate(lifted, axis=1))

    right = jnp.concatenate([stack3(pad_rows(integ[j], 32)) for j in range(NE)], axis=1)
    folded = dot(plw[...], right)
    for j in range(NE):
        cols = slice(j * LANES, (j + 1) * LANES)
        w = area[0:1, :] * folded[0:NBP, cols]
        for f in range(1, 4):
            w = w + area[f : f + 1, :] * folded[f * NBP : (f + 1) * NBP, cols]
        own[:, cols] = w

    acc = stress_of(lambda j: integ[j], star, kdw[...], grads)
    total = []
    for q in range(6):
        old = [integ[NE + 6 * l + q] for l in range(MECH)]
        relax = couple[0, q : q + 1, :] * old[0]
        for l in range(1, MECH):
            relax = relax + couple[l, q : q + 1, :] * old[l]
        for l in range(MECH):
            at = NE + 6 * l + q
            change[at] = omega[l : l + 1, :] * (acc[q] - old[l])
        total.append(acc[q] - relax)
    total = total + acc[6:]
    for j in range(NE):
        cols = slice(j * LANES, (j + 1) * LANES)
        w, v = own[:, cols], near[0:NBP, cols]
        for i in range(NE):
            total[i] = total[i] + (fminus[i, j : j + 1, :] * w + fplus[i, j : j + 1, :] * v)
    for i in range(NE):
        change[i] = total[i]
    base[...] = dofs[...] + jnp.transpose(change[:, 0:NB, :], (1, 0, 2))


def friction(trial, pressure, load, state):
    sigma = load * (1.0 + 0.5 * jnp.tanh(0.5 * pressure))
    half = AFRIC * sigma
    steep = half * state
    size = jnp.abs(trial)
    slip = size / (ETA + steep)
    for turn in range(NEWTON - 1):
        scaled = state * slip
        square = 1.0 + scaled * scaled
        inverse = lax.rsqrt(square)
        resid = size - ETA * slip - half * jnp.log(scaled + square * inverse)
        slope = ETA + steep * inverse
        guess = pl.reciprocal(slope, approx=True)
        slip = slip + resid * (guess * (2.0 - slope * guess))
    slip = jnp.where(trial < 0.0, -slip, slip)
    return trial - ETA * slip, slip


def fault_kernel(
    base_in, mine, theirs, keep, fse, fsf, fme, fmf, live, lift,
    base, mat, lfw, acc, slab, sem,
):
    del base_in
    s = pl.program_id(0)
    window = base.at[:, 0:8, :]

    @pl.when(s == 0)
    def _():
        pltpu.make_async_copy(window, slab, sem).start()
        lfw[...] = left3(mat, [(0, f * NBP, lift[f]) for f in range(4)], 16, 96)

    def tile(ref, n):
        return ref[pl.ds(n, SC // 16, stride=TILES), :]

    def pair(ref, n):
        return jnp.concatenate([tile(ref, 2 * n), tile(ref, 2 * n + 1)], axis=1)

    pull, slip = friction(
        0.5 * (pair(theirs, 0) + pair(mine, 2)), pair(mine, 3) + pair(theirs, 1),
        pair(mine, 4), pair(mine, 5),
    )
    terms = [pull - keep[:, 256:512], -0.5 * slip]
    pull, slip = friction(
        0.5 * (pair(mine, 0) + pair(theirs, 2)), pair(theirs, 3) + pair(mine, 1),
        pair(theirs, 4), pair(theirs, 5),
    )
    terms += [pull - keep[:, 0:256], 0.5 * slip]
    right = []
    for t in terms:
        x = jnp.concatenate([to_slots(t[:, 0:LANES]), to_slots(t[:, LANES:256])], axis=0)
        right.append(stack3(x))
    added = dot(lfw[...], jnp.concatenate(right, axis=1))
    far = to_slots(tile(theirs, 12))[0:1]
    left = []
    for side, (alive, face) in enumerate(((live[...].astype(F32), fmf[...]), (far, fsf[...]))):
        mask = [jnp.where(face == f, alive, 0.0) for f in range(4)]
        sums = []
        for k in range(2):
            at = slice((2 * side + k) * SC, (2 * side + k + 1) * SC)
            y = mask[0] * added[0:NBP, at]
            for f in range(1, 4):
                y = y + mask[f] * added[f * NBP : (f + 1) * NBP, at]
            sums.append(y)
        hi, lo = split(jnp.concatenate(sums, axis=0))
        left.append(jnp.concatenate([hi, lo], axis=0))
    spots = jnp.concatenate([one_hot(fme[...], E_DEV), one_hot(fse[...], E_DEV)], axis=1)
    acc[s] = dot_nt(jnp.concatenate(left, axis=1), spots)

    @pl.when(s == SLOTS // SC - 1)
    def _():
        total = acc[0]
        for part in range(1, SLOTS // SC):
            total = total + acc[part]
        acc[0, 0:48, :] = total[0:48] + total[48:96]
        pltpu.make_async_copy(window, slab, sem).wait()
        for b in range(NB):
            for k in range(2):
                row = slice(FAULT_ROWS[1 + k], FAULT_ROWS[1 + k] + 1)
                slab[b, row, :] = slab[b, row, :] + acc[0, k * NBP + b : k * NBP + b + 1, :]
        copy = pltpu.make_async_copy(slab, window, sem)
        copy.start()
        copy.wait()


def whole(shape):
    return pl.BlockSpec(shape, lambda *i: (0,) * len(shape))


def lanes(*lead):
    return pl.BlockSpec(lead + (LANES,), lambda c: (0,) * len(lead) + (c,))


def per_device(
    dofs, star, kdiff, couple, omega, flux_minus, flux_plus, area, face_proj, face_lift,
    nbr_elem, nbr_face, weight_class, send_rows, fault_send_elem, fault_send_face,
    fault_minus_elem, fault_minus_face, fault_live, normal_load, state,
):
    shape = jax.ShapeDtypeStruct
    wc = weight_class.reshape(1, E_DEV)
    dofs = jnp.transpose(dofs, (1, 0, 2))
    star = jnp.transpose(star, (1, 2, 0, 3))
    face_proj = jnp.transpose(face_proj, (0, 2, 1))
    rim = whole((NE, NB, BND))
    lines = pl.BlockSpec((SC // 16 * TILES, LANES), lambda c: (c, 0))
    kept = pl.BlockSpec((SC // 16, 4 * LANES), lambda c: (c, 0))
    slots = pl.BlockSpec((1, SC), lambda c: (0, c))
    points = pl.BlockSpec((1, NP, SC), lambda c: (0, 0, c))
    params = pltpu.CompilerParams(vmem_limit_bytes=VMEM)
    integ, ihl, fhl, s0, s1, s2, s3 = pl.pallas_call(
        predict_kernel,
        grid=(CHUNKS,),
        in_specs=[
            lanes(NB, NQ), lanes(NE, NE, 3), lanes(MECH, 6), lanes(MECH), lanes(1),
            whole((3, NB, NB)), whole((4, BND)),
        ],
        out_specs=[
            lanes(NQ, NBP), whole((2 * ROWS, E_DEV)), whole((160, E_DEV)), rim, rim, rim, rim,
        ],
        out_shape=[
            shape((NQ, NBP, E_DEV), F32), shape((2 * ROWS, E_DEV), BF), shape((160, E_DEV), BF),
            *[shape((NE, NB, BND), F32)] * 4,
        ],
        scratch_shapes=[
            pltpu.VMEM((NQ, NBP, LANES), F32), pltpu.VMEM((80, NE * LANES), F32),
            pltpu.VMEM((64, LANES), F32), pltpu.VMEM((80, 96), BF),
        ],
        compiler_params=params,
        name="predict",
    )(dofs, star, couple, omega, wc, kdiff, send_rows)
    out, keep = pl.pallas_call(
        slot_kernel,
        grid=(SLOTS // SC,),
        in_specs=[whole((160, E_DEV)), whole((4, NP, NB)), *[slots] * 5, points, points],
        out_specs=[lines, kept],
        out_shape=[shape((DEVICES * TILES, LANES), F32), shape((DEVICES, 4 * LANES), F32)],
        scratch_shapes=[pltpu.VMEM((64, LANES), F32), pltpu.VMEM((64, 96), BF)],
        compiler_params=params,
        name="slots",
    )(
        fhl, face_proj, fault_send_elem, fault_send_face, fault_minus_elem, fault_minus_face,
        fault_live, normal_load, state,
    )
    ns, nd = lax.axis_size("strike"), lax.axis_size("depth")

    def swap(x, axis, n, first):
        ends = [(i, (i + 1) % n) for i in range(first, n, 2)]
        return lax.ppermute(x, axis, ends + [(j, i) for i, j in ends])

    r0 = swap(s0, "strike", ns, 0)
    r1 = swap(s1, "strike", ns, 1)
    r2 = swap(s2, "depth", nd, 0)
    r3 = swap(s3, "depth", nd, 1)
    theirs = lax.all_to_all(
        out.reshape(DEVICES, 1, TILES * LANES), ("strike", "depth"), split_axis=0, concat_axis=0, tiled=True
    ).reshape(DEVICES * TILES, LANES)
    base = pl.pallas_call(
        element_kernel,
        grid=(CHUNKS,),
        in_specs=[
            lanes(NQ, NBP), lanes(NB, NQ), lanes(NE, NE, 3), lanes(MECH, 6), lanes(MECH),
            lanes(NE, NE), lanes(NE, NE), lanes(4), lanes(4), lanes(4),
            whole((2 * ROWS, E_DEV)), rim, rim, rim, rim,
            whole((3, NB, NB)), whole((4, NP, NB)), whole((4, NP, NB)),
        ],
        out_specs=lanes(NB, NQ),
        out_shape=shape((NB, NQ, E_DEV), F32),
        scratch_shapes=[
            pltpu.VMEM((80, NE * LANES), F32), pltpu.VMEM((64, LANES), F32),
            pltpu.VMEM((80, 96), BF), pltpu.VMEM((64, 96), BF), pltpu.VMEM((32, 192), BF),
            pltpu.VMEM((96, 96), BF), pltpu.VMEM((2 * ROWS, 4 * BND), BF),
            pltpu.VMEM((NBP, NE * LANES), F32), pltpu.VMEM((32, NE * LANES), F32),
            pltpu.VMEM((NQ, NBP, LANES), F32),
        ],
        compiler_params=params,
        name="elements",
    )(
        integ, dofs, star, couple, omega, flux_minus, flux_plus, area, nbr_elem, nbr_face,
        ihl, r0, r1, r2, r3, kdiff, face_proj, face_lift,
    )
    anywhere = pl.BlockSpec(memory_space=pl.ANY)
    result = pl.pallas_call(
        fault_kernel,
        grid=(SLOTS // SC,),
        in_specs=[
            anywhere, lines, lines, kept,
            slots, slots, slots, slots, slots, whole((4, NP, NB)),
        ],
        out_specs=anywhere,
        out_shape=shape((NB, NQ, E_DEV), F32),
        input_output_aliases={0: 0},
        scratch_shapes=[
            pltpu.VMEM((64, LANES), F32), pltpu.VMEM((96, 48), BF), pltpu.VMEM((SLOTS // SC, 96, E_DEV), F32),
            pltpu.VMEM((NB, 8, E_DEV), F32), pltpu.SemaphoreType.DMA,
        ],
        compiler_params=params,
        name="fault",
    )(
        base, out, theirs, keep, fault_send_elem, fault_send_face, fault_minus_elem,
        fault_minus_face, fault_live, face_lift,
    )
    return jnp.transpose(result, (1, 0, 2))


def solution(mesh):
    both = ("strike", "depth")
    split_1, split_2, split_3 = P(None, both), P(None, None, both), P(None, None, None, both)
    in_specs = (
        split_2, split_3, P(), split_2, split_1, split_2, split_2, split_1, P(), P(),
        split_1, split_1, P(both), split_1,
        *[P(both, None)] * 5, P(both, None, None), P(both, None, None),
    )
    return jax.shard_map(
        per_device, mesh=mesh, in_specs=in_specs, out_specs=split_2, check_vma=False
    )
```

```python
import jax
import jax.numpy as jnp
from jax import lax
from jax.experimental import pallas as pl
from jax.experimental.pallas import tpu as pltpu
from jax.sharding import PartitionSpec as P

NQ = 27
NE = 9
MECH = 3
NB = 20
NP = 16
ORDER = 4
NEWTON = 4
ETA = 1.0
AFRIC = 0.5
E_DEV = 512
BND = 128
SLOTS = 2048
DEVICES = 128
NBP = 24
LANES = 128
CHUNKS = E_DEV // LANES
ROWS = 224
SC = 512
TILES = 13
F32 = jnp.float32
BF = jnp.bfloat16
VMEM = 56 * 1024 * 1024
FAULT_ROWS = (0, 3, 6)


def split(x):
    hi = x.astype(BF)
    return hi, (x - hi.astype(F32)).astype(BF)


def pad_rows(x, rows):
    extra = rows - x.shape[0]
    if extra == 0:
        return x
    return jnp.concatenate([x, jnp.zeros((extra,) + x.shape[1:], x.dtype)], axis=0)


def stack3(x):
    hi, lo = split(x)
    return jnp.concatenate([hi, hi, lo], axis=0)


def left3(scratch, parts, depth, rows):
    scratch[...] = jnp.zeros(scratch.shape, F32)
    for row, col, value in parts:
        scratch[row : row + value.shape[0], col : col + value.shape[1]] = value
    whole = scratch[0:depth, :]
    hi = whole.astype(BF).astype(F32)
    lo = whole - hi
    tall = jnp.concatenate([hi, lo, hi], axis=0)
    tall = pad_rows(tall, -(-tall.shape[0] // 128) * 128)
    return jnp.transpose(tall, (1, 0))[0:rows, 0 : 3 * depth].astype(BF)


def dot(a, b):
    return lax.dot_general(a, b, (((1,), (0,)), ((), ())), preferred_element_type=F32)


def dot_nt(a, b):
    return lax.dot_general(a, b, (((1,), (1,)), ((), ())), preferred_element_type=F32)


def one_hot(index, rows, base=0):
    row = lax.broadcasted_iota(jnp.int32, (rows, LANES), 0).astype(jnp.int16)
    index = jnp.broadcast_to(index - base, (16, index.shape[1])).astype(jnp.int16)
    out = []
    for t in range(index.shape[1] // LANES):
        here = jnp.concatenate([index[:, t * LANES : (t + 1) * LANES]] * (rows // 16), axis=0)
        out.append(jnp.where(row == here, jnp.ones((), BF), jnp.zeros((), BF)))
    return jnp.concatenate(out, axis=1)


def swap_blocks(x):
    x = pltpu.roll(x, 0, 1, stride=16, stride_axis=0)
    lane = lax.broadcasted_iota(jnp.int32, (8, LANES), 1)
    sub = lax.broadcasted_iota(jnp.int32, (8, LANES), 0)
    down = jnp.bitwise_and(lane // 16 - sub, 7)
    across = jnp.bitwise_and(lane + 16 * sub, LANES - 1)
    tiles = []
    for t in range(x.shape[0] // 8):
        y = jnp.take_along_axis(x[8 * t : 8 * t + 8], down, axis=0, mode="promise_in_bounds")
        tiles.append(jnp.take_along_axis(y, across, axis=1, mode="promise_in_bounds"))
    return jnp.concatenate(tiles, axis=0)


def to_blocks(x):
    return swap_blocks(
        jnp.concatenate([x[:, t * LANES : (t + 1) * LANES] for t in range(SC // LANES)], axis=0)
    )


def to_slots(x):
    x = swap_blocks(x)
    return jnp.concatenate([x[8 * t : 8 * t + 8] for t in range(SC // LANES)], axis=1)


def stress_of(get, star_ref, kd, rows=range(NE)):
    fields = [get(j) for j in range(NE)]
    out = []
    for i in rows:
        mixed = []
        for d in range(3):
            t = star_ref[i, 0, d : d + 1, :] * fields[0]
            for j in range(1, NE):
                t = t + star_ref[i, j, d : d + 1, :] * fields[j]
            mixed.append(t)
        out.append(dot(kd, stack3(pad_rows(jnp.concatenate(mixed, axis=0), 80)))[0:NBP])
    return out


def predict_kernel(
    dofs, star, couple, omega, wc, kdiff, srow,
    integ, ihl, fhl, send0, send1, send2, send3,
    term, mat, kdw,
):
    c = pl.program_id(0)

    @pl.when(c == 0)
    def _():
        kdw[...] = left3(mat, [(d * NBP, 0, kdiff[d]) for d in range(3)], 80, 32)
        term[...] = jnp.zeros(term.shape, F32)

    kd = kdw[...]
    step = 1.0 / (1.0 + wc[...].astype(F32))
    term[:, 0:NB, :] = jnp.transpose(dofs[...], (1, 0, 2))
    for q in range(NQ):
        integ[q] = step * term[q]

    def turn(order, power):
        acc = stress_of(lambda j: term[j], star, kd)
        for q in range(6):
            old = [term[NE + 6 * l + q] for l in range(MECH)]
            relax = couple[0, q : q + 1, :] * old[0]
            for l in range(1, MECH):
                relax = relax + couple[l, q : q + 1, :] * old[l]
            term[q] = acc[q] - relax
            for l in range(MECH):
                term[NE + 6 * l + q] = omega[l : l + 1, :] * (acc[q] - old[l])
        for q in range(6, NE):
            term[q] = acc[q]
        power = power * step / (order + 2).astype(F32)
        for q in range(NQ):
            integ[q] += power * term[q]
        return power

    lax.fori_loop(0, ORDER - 1, turn, step)

    here = pl.ds(pl.multiple_of(c * LANES, LANES), LANES)
    flat = pad_rows(integ[0:NE].reshape(NE * NBP, LANES), ROWS)
    hi, lo = split(flat)
    ihl[0:ROWS, here] = hi
    ihl[ROWS : 2 * ROWS, here] = lo
    hi, lo = split(pad_rows(jnp.concatenate([integ[r] for r in FAULT_ROWS], axis=0), 80))
    fhl[0:80, here] = hi
    fhl[80:160, here] = lo

    @pl.when(c == CHUNKS - 1)
    def _():
        rows = []
        for axis, k in (("strike", 0), ("depth", 2)):
            even = lax.axis_index(axis) % 2 == 0
            ahead, behind = srow[k : k + 1, :], srow[k + 1 : k + 2, :]
            rows += [jnp.where(even, ahead, behind), jnp.where(even, behind, ahead)]
        rows = jnp.concatenate(rows, axis=1)
        got = dot(ihl[...], one_hot(rows, E_DEV))
        got = got[0:ROWS] + got[ROWS : 2 * ROWS]
        for k, ref in enumerate((send0, send1, send2, send3)):
            for j in range(NE):
                ref[j] = got[j * NBP : j * NBP + NB, k * BND : (k + 1) * BND]


def fault_values(fhl, fpw, elem, face):
    x = dot(fhl[...], one_hot(elem, E_DEV))
    right = []
    for r in range(3):
        h = pad_rows(x[r * NBP : (r + 1) * NBP], 32).astype(BF)
        l = pad_rows(x[80 + r * NBP : 80 + (r + 1) * NBP], 32).astype(BF)
        right.append(jnp.concatenate([h, h, l], axis=0))
    points = dot(fpw[...], jnp.concatenate(right, axis=1))
    values = []
    for r in range(3):
        cols = slice(r * SC, (r + 1) * SC)
        v = points[0:NP, cols]
        for g in range(1, 4):
            v = jnp.where(face == g, points[g * NP : (g + 1) * NP, cols], v)
        values.append(v)
    return values


def slot_kernel(fhl, proj, fse, fsf, fme, fmf, live, load, state, out, keep, mat, fpw):
    @pl.when(pl.program_id(0) == 0)
    def _():
        fpw[...] = left3(mat, [(0, g * NP, proj[g].T) for g in range(4)], 32, 64)

    def place(tile, x):
        out[pl.ds(tile, SC // 16, stride=TILES), :] = to_blocks(x)

    place(12, jnp.broadcast_to(live[...].astype(F32), (8, SC)))
    plus = fault_values(fhl, fpw, fse[...], fsf[...])
    minus = fault_values(fhl, fpw, fme[...], fmf[...])
    sent = (
        plus[1] + plus[2], plus[0], minus[1] - minus[2], minus[0], load[0], state[0],
    )
    for n, x in enumerate(sent):
        for g in range(2):
            place(2 * n + g, x[8 * g : 8 * g + 8])
    for n, x in enumerate((plus[1], minus[1])):
        for g in range(2):
            at = (2 * n + g) * LANES
            keep[:, at : at + LANES] = to_blocks(x[8 * g : 8 * g + 8])


def element_kernel(
    integ, dofs, star, couple, omega, fminus, fplus, area, nelem, nface, ihl, rim0, rim1, rim2, rim3,
    kdiff, proj, lift, base, mat, kdw, fpw, ltw, plw, rhl, change,
):
    c = pl.program_id(0)

    def put_rim(k, fields):
        flat = jnp.concatenate([pad_rows(x, NBP) for x in fields], axis=0)
        hi, lo = split(pad_rows(flat, ROWS))
        rhl[0:ROWS, k * BND : (k + 1) * BND] = hi
        rhl[ROWS : 2 * ROWS, k * BND : (k + 1) * BND] = lo

    @pl.when(c == 0)
    def _():
        kdw[...] = left3(mat, [(d * NBP, 0, kdiff[d]) for d in range(3)], 80, 32)
        fpw[...] = left3(mat, [(0, g * NP, proj[g].T) for g in range(4)], 32, 64)
        ltw[...] = left3(mat, [(f * NP, 0, lift[f]) for f in range(4)], 64, 32)
        both = [
            lax.dot_general(
                proj[f], lift[f], (((0,), (0,)), ((), ())),
                precision=lax.Precision.HIGHEST, preferred_element_type=F32,
            )
            for f in range(4)
        ]
        plw[...] = left3(mat, [(0, f * NBP, both[f]) for f in range(4)], 32, 96)
        for k, first, second, axis in ((0, rim0, rim1, "strike"), (2, rim2, rim3, "depth")):
            at = lax.axis_index(axis)
            even = (at % 2 == 0).astype(F32)
            odd = 1.0 - even
            before = (at > 0).astype(F32)
            after = (at < lax.axis_size(axis) - 1).astype(F32)
            for side, one, two in ((k, odd * before, even * before), (k + 1, even * after, odd * after)):
                put_rim(side, [one * first[j] + two * second[j] for j in range(NE)])
    def spread(ref):
        return jnp.concatenate([ref[f : f + 1, :] for f in range(4)], axis=1)

    def gather():
        elem = spread(nelem)
        return dot(ihl[...], one_hot(elem, E_DEV)) + dot(rhl[...], one_hot(elem, 4 * BND, E_DEV))

    def project(got):
        right = []
        for j in range(NE):
            hi = pad_rows(got[j * NBP : (j + 1) * NBP], 32).astype(BF)
            lo = pad_rows(got[ROWS + j * NBP : ROWS + (j + 1) * NBP], 32).astype(BF)
            right.append(jnp.concatenate([hi, hi, lo], axis=0))
        return dot(fpw[...], jnp.concatenate(right, axis=1))

    def choose(points):
        face, scale = spread(nface), spread(area)
        out = []
        for j in range(NE):
            cols = slice(j * E_DEV, (j + 1) * E_DEV)
            v = points[0:NP, cols]
            for g in range(1, 4):
                v = jnp.where(face == g, points[g * NP : (g + 1) * NP, cols], v)
            v = v * scale
            out.append(jnp.concatenate([v[:, f * LANES : (f + 1) * LANES] for f in range(4)], axis=0))
        return out

    kd = kdw[...]
    got = gather()
    acc = stress_of(lambda j: integ[j], star, kd)
    folded = dot(plw[...], jnp.concatenate([stack3(pad_rows(integ[j], 32)) for j in range(NE)], axis=1))
    points = project(got)
    for q in range(6):
        old = [integ[NE + 6 * l + q] for l in range(MECH)]
        relax = couple[0, q : q + 1, :] * old[0]
        for l in range(1, MECH):
            relax = relax + couple[l, q : q + 1, :] * old[l]
        for l in range(MECH):
            change[NE + 6 * l + q] = omega[l : l + 1, :] * (acc[q] - old[l])
        change[q] = acc[q] - relax
    for q in range(6, NE):
        change[q] = acc[q]
    total = [None] * NE
    for j in range(NE):
        cols = slice(j * LANES, (j + 1) * LANES)
        w = area[0:1, :] * folded[0:NBP, cols]
        for f in range(1, 4):
            w = w + area[f : f + 1, :] * folded[f * NBP : (f + 1) * NBP, cols]
        for i in range(NE):
            t = fminus[i, j : j + 1, :] * w
            total[i] = t if j == 0 else total[i] + t
    for i in range(NE):
        change[i] += total[i]
    lifted = dot(ltw[...], jnp.concatenate([stack3(v) for v in choose(points)], axis=1))
    for i in range(NE):
        t = change[i]
        for j in range(NE):
            t = t + fplus[i, j : j + 1, :] * lifted[0:NBP, j * LANES : (j + 1) * LANES]
        change[i] = t
    base[...] = dofs[...] + jnp.transpose(change[:, 0:NB, :], (1, 0, 2))


def friction(trial, pressure, load, state):
    sigma = load * (1.0 + 0.5 * jnp.tanh(0.5 * pressure))
    half = AFRIC * sigma
    steep = half * state
    size = jnp.abs(trial)
    slip = size / (ETA + steep)
    for turn in range(NEWTON - 1):
        scaled = state * slip
        square = 1.0 + scaled * scaled
        inverse = lax.rsqrt(square)
        resid = size - ETA * slip - half * jnp.log(scaled + square * inverse)
        slope = ETA + steep * inverse
        guess = pl.reciprocal(slope, approx=True)
        slip = slip + resid * (guess * (2.0 - slope * guess))
    slip = jnp.where(trial < 0.0, -slip, slip)
    return trial - ETA * slip, slip


def fault_kernel(
    base_in, mine, theirs, keep, fse, fsf, fme, fmf, live, lift,
    base, mat, lfw, acc, slab, sem,
):
    del base_in
    s = pl.program_id(0)
    window = base.at[:, 0:8, :]

    @pl.when(s == 0)
    def _():
        pltpu.make_async_copy(window, slab, sem).start()
        lfw[...] = left3(mat, [(0, f * NBP, lift[f]) for f in range(4)], 16, 96)

    def tile(ref, n):
        return ref[pl.ds(n, SC // 16, stride=TILES), :]

    def pair(ref, n):
        return jnp.concatenate([tile(ref, 2 * n), tile(ref, 2 * n + 1)], axis=1)

    pull, slip = friction(
        0.5 * (pair(theirs, 0) + pair(mine, 2)), pair(mine, 3) + pair(theirs, 1),
        pair(mine, 4), pair(mine, 5),
    )
    terms = [pull - keep[:, 256:512], -0.5 * slip]
    pull, slip = friction(
        0.5 * (pair(mine, 0) + pair(theirs, 2)), pair(theirs, 3) + pair(mine, 1),
        pair(theirs, 4), pair(theirs, 5),
    )
    terms += [pull - keep[:, 0:256], 0.5 * slip]
    right = []
    for t in terms:
        x = jnp.concatenate([to_slots(t[:, 0:LANES]), to_slots(t[:, LANES:256])], axis=0)
        right.append(stack3(x))
    added = dot(lfw[...], jnp.concatenate(right, axis=1))
    far = to_slots(tile(theirs, 12))[0:1]
    left = []
    for side, (alive, face) in enumerate(((live[...].astype(F32), fmf[...]), (far, fsf[...]))):
        mask = [jnp.where(face == f, alive, 0.0) for f in range(4)]
        sums = []
        for k in range(2):
            at = slice((2 * side + k) * SC, (2 * side + k + 1) * SC)
            y = mask[0] * added[0:NBP, at]
            for f in range(1, 4):
                y = y + mask[f] * added[f * NBP : (f + 1) * NBP, at]
            sums.append(y)
        hi, lo = split(jnp.concatenate(sums, axis=0))
        left.append(jnp.concatenate([hi, lo], axis=0))
    spots = jnp.concatenate([one_hot(fme[...], E_DEV), one_hot(fse[...], E_DEV)], axis=1)
    acc[s] = dot_nt(jnp.concatenate(left, axis=1), spots)

    @pl.when(s == SLOTS // SC - 1)
    def _():
        total = acc[0]
        for part in range(1, SLOTS // SC):
            total = total + acc[part]
        acc[0, 0:48, :] = total[0:48] + total[48:96]
        pltpu.make_async_copy(window, slab, sem).wait()
        for b in range(NB):
            for k in range(2):
                row = slice(FAULT_ROWS[1 + k], FAULT_ROWS[1 + k] + 1)
                slab[b, row, :] = slab[b, row, :] + acc[0, k * NBP + b : k * NBP + b + 1, :]
        copy = pltpu.make_async_copy(slab, window, sem)
        copy.start()
        copy.wait()


def whole(shape):
    return pl.BlockSpec(shape, lambda *i: (0,) * len(shape))


def lanes(*lead):
    return pl.BlockSpec(lead + (LANES,), lambda c: (0,) * len(lead) + (c,))


def per_device(
    dofs, star, kdiff, couple, omega, flux_minus, flux_plus, area, face_proj, face_lift,
    nbr_elem, nbr_face, weight_class, send_rows, fault_send_elem, fault_send_face,
    fault_minus_elem, fault_minus_face, fault_live, normal_load, state,
):
    shape = jax.ShapeDtypeStruct
    wc = weight_class.reshape(1, E_DEV)
    dofs = jnp.transpose(dofs, (1, 0, 2))
    star = jnp.transpose(star, (1, 2, 0, 3))
    face_proj = jnp.transpose(face_proj, (0, 2, 1))
    rim = whole((NE, NB, BND))
    lines = pl.BlockSpec((SC // 16 * TILES, LANES), lambda c: (c, 0))
    kept = pl.BlockSpec((SC // 16, 4 * LANES), lambda c: (c, 0))
    slots = pl.BlockSpec((1, SC), lambda c: (0, c))
    points = pl.BlockSpec((1, NP, SC), lambda c: (0, 0, c))
    params = pltpu.CompilerParams(vmem_limit_bytes=VMEM)
    integ, ihl, fhl, s0, s1, s2, s3 = pl.pallas_call(
        predict_kernel,
        grid=(CHUNKS,),
        in_specs=[
            lanes(NB, NQ), lanes(NE, NE, 3), lanes(MECH, 6), lanes(MECH), lanes(1),
            whole((3, NB, NB)), whole((4, BND)),
        ],
        out_specs=[
            lanes(NQ, NBP), whole((2 * ROWS, E_DEV)), whole((160, E_DEV)), rim, rim, rim, rim,
        ],
        out_shape=[
            shape((NQ, NBP, E_DEV), F32), shape((2 * ROWS, E_DEV), BF), shape((160, E_DEV), BF),
            *[pltpu.HBM((NE, NB, BND), F32)] * 4,
        ],
        scratch_shapes=[
            pltpu.VMEM((NQ, NBP, LANES), F32), pltpu.VMEM((80, LANES), F32),
            pltpu.VMEM((32, 240), BF),
        ],
        compiler_params=params,
        name="predict",
    )(dofs, star, couple, omega, wc, kdiff, send_rows)
    out, keep = pl.pallas_call(
        slot_kernel,
        grid=(SLOTS // SC,),
        in_specs=[whole((160, E_DEV)), whole((4, NP, NB)), *[slots] * 5, points, points],
        out_specs=[lines, kept],
        out_shape=[shape((DEVICES * TILES, LANES), F32), shape((DEVICES, 4 * LANES), F32)],
        scratch_shapes=[pltpu.VMEM((64, LANES), F32), pltpu.VMEM((64, 96), BF)],
        compiler_params=params,
        name="slots",
    )(
        fhl, face_proj, fault_send_elem, fault_send_face, fault_minus_elem, fault_minus_face,
        fault_live, normal_load, state,
    )
    ns, nd = lax.axis_size("strike"), lax.axis_size("depth")

    def swap(x, axis, n, first):
        ends = [(i, (i + 1) % n) for i in range(first, n, 2)]
        return lax.ppermute(x, axis, ends + [(j, i) for i, j in ends])

    r0 = swap(s0, "strike", ns, 0)
    r1 = swap(s1, "strike", ns, 1)
    r2 = swap(s2, "depth", nd, 0)
    r3 = swap(s3, "depth", nd, 1)
    r0, r1, r2, r3, sent = lax.optimization_barrier((r0, r1, r2, r3, out))
    theirs = lax.all_to_all(
        sent.reshape(DEVICES, 1, TILES * LANES), ("strike", "depth"), split_axis=0, concat_axis=0, tiled=True
    ).reshape(DEVICES * TILES, LANES)
    base = pl.pallas_call(
        element_kernel,
        grid=(CHUNKS,),
        in_specs=[
            lanes(NQ, NBP), lanes(NB, NQ), lanes(NE, NE, 3), lanes(MECH, 6), lanes(MECH),
            lanes(NE, NE), lanes(NE, NE), lanes(4), lanes(4), lanes(4),
            whole((2 * ROWS, E_DEV)), rim, rim, rim, rim,
            whole((3, NB, NB)), whole((4, NP, NB)), whole((4, NP, NB)),
        ],
        out_specs=lanes(NB, NQ),
        out_shape=pltpu.HBM((NB, NQ, E_DEV), F32),
        scratch_shapes=[
            pltpu.VMEM((80, LANES), F32),
            pltpu.VMEM((32, 240), BF), pltpu.VMEM((64, 96), BF), pltpu.VMEM((32, 192), BF),
            pltpu.VMEM((96, 96), BF), pltpu.VMEM((2 * ROWS, 4 * BND), BF),
            pltpu.VMEM((NQ, NBP, LANES), F32),
        ],
        compiler_params=params,
        name="elements",
    )(
        integ, dofs, star, couple, omega, flux_minus, flux_plus, area, nbr_elem, nbr_face,
        ihl, r0, r1, r2, r3, kdiff, face_proj, face_lift,
    )
    anywhere = pl.BlockSpec(memory_space=pl.ANY)
    result = pl.pallas_call(
        fault_kernel,
        grid=(SLOTS // SC,),
        in_specs=[
            anywhere, lines, lines, kept,
            slots, slots, slots, slots, slots, whole((4, NP, NB)),
        ],
        out_specs=anywhere,
        out_shape=shape((NB, NQ, E_DEV), F32),
        input_output_aliases={0: 0},
        scratch_shapes=[
            pltpu.VMEM((64, LANES), F32), pltpu.VMEM((96, 48), BF), pltpu.VMEM((SLOTS // SC, 96, E_DEV), F32),
            pltpu.VMEM((NB, 8, E_DEV), F32), pltpu.SemaphoreType.DMA,
        ],
        compiler_params=params,
        name="fault",
    )(
        base, sent, theirs, keep, fault_send_elem, fault_send_face, fault_minus_elem,
        fault_minus_face, fault_live, face_lift,
    )
    return jnp.transpose(result, (1, 0, 2))


def solution(mesh):
    both = ("strike", "depth")
    split_1, split_2, split_3 = P(None, both), P(None, None, both), P(None, None, None, both)
    in_specs = (
        split_2, split_3, P(), split_2, split_1, split_2, split_2, split_1, P(), P(),
        split_1, split_1, P(both), split_1,
        *[P(both, None)] * 5, P(both, None, None), P(both, None, None),
    )
    return jax.shard_map(
        per_device, mesh=mesh, in_specs=in_specs, out_specs=split_2, check_vma=False
    )
```

```python
import jax
import jax.numpy as jnp
from jax import lax
from jax.experimental import pallas as pl
from jax.experimental.pallas import tpu as pltpu
from jax.sharding import PartitionSpec as P

NQ = 27
NE = 9
MECH = 3
NB = 20
NP = 16
ORDER = 4
NEWTON = 4
ETA = 1.0
AFRIC = 0.5
E_DEV = 512
BND = 128
SLOTS = 2048
DEVICES = 128
NBP = 24
LANES = 128
CHUNKS = E_DEV // LANES
PAIR = 2
WIDE = PAIR * LANES
ROWS = 224
SC = 2048
TILES = 13
F32 = jnp.float32
BF = jnp.bfloat16
VMEM = 56 * 1024 * 1024
FAULT_ROWS = (0, 3, 6)


def split(x):
    hi = x.astype(BF)
    return hi, (x - hi.astype(F32)).astype(BF)


def pad_rows(x, rows):
    extra = rows - x.shape[0]
    if extra == 0:
        return x
    return jnp.concatenate([x, jnp.zeros((extra,) + x.shape[1:], x.dtype)], axis=0)


def stack3(x):
    hi, lo = split(x)
    return jnp.concatenate([hi, hi, lo], axis=0)


def left3(scratch, parts, depth, rows):
    scratch[...] = jnp.zeros(scratch.shape, F32)
    for row, col, value in parts:
        scratch[row : row + value.shape[0], col : col + value.shape[1]] = value
    whole = scratch[0:depth, :]
    hi = whole.astype(BF).astype(F32)
    lo = whole - hi
    tall = jnp.concatenate([hi, lo, hi], axis=0)
    tall = pad_rows(tall, -(-tall.shape[0] // 128) * 128)
    return jnp.transpose(tall, (1, 0))[0:rows, 0 : 3 * depth].astype(BF)


def dot(a, b):
    return lax.dot_general(a, b, (((1,), (0,)), ((), ())), preferred_element_type=F32)


def dot_nt(a, b):
    return lax.dot_general(a, b, (((1,), (1,)), ((), ())), preferred_element_type=F32)


def one_hot(index, rows, base=0):
    row = lax.broadcasted_iota(jnp.int32, (rows, LANES), 0).astype(jnp.int16)
    index = jnp.broadcast_to(index - base, (16, index.shape[1])).astype(jnp.int16)
    out = []
    for t in range(index.shape[1] // LANES):
        here = jnp.concatenate([index[:, t * LANES : (t + 1) * LANES]] * (rows // 16), axis=0)
        out.append(jnp.where(row == here, jnp.ones((), BF), jnp.zeros((), BF)))
    return jnp.concatenate(out, axis=1)


def swap_blocks(x):
    x = pltpu.roll(x, 0, 1, stride=16, stride_axis=0)
    lane = lax.broadcasted_iota(jnp.int32, (8, LANES), 1)
    sub = lax.broadcasted_iota(jnp.int32, (8, LANES), 0)
    down = jnp.bitwise_and(lane // 16 - sub, 7)
    across = jnp.bitwise_and(lane + 16 * sub, LANES - 1)
    tiles = []
    for t in range(x.shape[0] // 8):
        y = jnp.take_along_axis(x[8 * t : 8 * t + 8], down, axis=0, mode="promise_in_bounds")
        tiles.append(jnp.take_along_axis(y, across, axis=1, mode="promise_in_bounds"))
    return jnp.concatenate(tiles, axis=0)


def to_blocks(x):
    return swap_blocks(
        jnp.concatenate([x[:, t * LANES : (t + 1) * LANES] for t in range(SC // LANES)], axis=0)
    )


def to_slots(x):
    x = swap_blocks(x)
    return jnp.concatenate([x[8 * t : 8 * t + 8] for t in range(SC // LANES)], axis=1)


def stress_of(get, star_ref, kd, rows=range(NE)):
    fields = [get(j) for j in range(NE)]
    out = []
    for i in rows:
        mixed = []
        for d in range(3):
            t = star_ref[i, 0, d : d + 1, :] * fields[0]
            for j in range(1, NE):
                t = t + star_ref[i, j, d : d + 1, :] * fields[j]
            mixed.append(t)
        out.append(dot(kd, stack3(pad_rows(jnp.concatenate(mixed, axis=0), 80)))[0:NBP])
    return out


def predict_kernel(
    dofs, star, couple, omega, wc, kdiff, srow,
    integ, ihl, fhl, send0, send1, send2, send3,
    term, mat, kdw,
):
    c = pl.program_id(0)

    @pl.when(c == 0)
    def _():
        kdw[...] = left3(mat, [(d * NBP, 0, kdiff[d]) for d in range(3)], 80, 32)
        term[...] = jnp.zeros(term.shape, F32)

    kd = kdw[...]
    step = 1.0 / (1.0 + wc[...].astype(F32))
    term[:, 0:NB, :] = jnp.transpose(dofs[...], (1, 0, 2))
    for q in range(NQ):
        integ[q] = step * term[q]

    def derive(cols, power):
        acc = stress_of(lambda j: term[j, :, cols], star.at[:, :, :, cols], kd)
        for q in range(6):
            old = [term[NE + 6 * l + q, :, cols] for l in range(MECH)]
            relax = couple[0, q : q + 1, cols] * old[0]
            for l in range(1, MECH):
                relax = relax + couple[l, q : q + 1, cols] * old[l]
            new = acc[q] - relax
            term[q, :, cols] = new
            integ[q, :, cols] += power * new
            for l in range(MECH):
                new = omega[l : l + 1, cols] * (acc[q] - old[l])
                term[NE + 6 * l + q, :, cols] = new
                integ[NE + 6 * l + q, :, cols] += power * new
        for q in range(6, NE):
            term[q, :, cols] = acc[q]
            integ[q, :, cols] += power * acc[q]

    def turn(order, power):
        power = power * step / (order + 2).astype(F32)
        for half in range(PAIR):
            cols = slice(half * LANES, (half + 1) * LANES)
            derive(cols, power[:, cols])
        return power

    lax.fori_loop(0, ORDER - 1, turn, step)

    here = pl.ds(pl.multiple_of(c * WIDE, WIDE), WIDE)
    flat = pad_rows(integ[0:NE].reshape(NE * NBP, WIDE), ROWS)
    hi, lo = split(flat)
    ihl[0:ROWS, here] = hi
    ihl[ROWS : 2 * ROWS, here] = lo
    hi, lo = split(pad_rows(jnp.concatenate([integ[r] for r in FAULT_ROWS], axis=0), 80))
    fhl[0:80, here] = hi
    fhl[80:160, here] = lo

    @pl.when(c == CHUNKS // PAIR - 1)
    def _():
        rows = []
        for axis, k in (("strike", 0), ("depth", 2)):
            even = lax.axis_index(axis) % 2 == 0
            ahead, behind = srow[k : k + 1, :], srow[k + 1 : k + 2, :]
            rows += [jnp.where(even, ahead, behind), jnp.where(even, behind, ahead)]
        rows = jnp.concatenate(rows, axis=1)
        got = dot(ihl[...], one_hot(rows, E_DEV))
        got = got[0:ROWS] + got[ROWS : 2 * ROWS]
        for k, ref in enumerate((send0, send1, send2, send3)):
            for j in range(NE):
                ref[j] = got[j * NBP : j * NBP + NB, k * BND : (k + 1) * BND]


def fault_values(fhl, fpw, elem, face):
    count = elem.shape[1]
    x = dot(fhl[...], one_hot(elem, E_DEV))
    right = []
    for r in range(3):
        h = pad_rows(x[r * NBP : (r + 1) * NBP], 32).astype(BF)
        l = pad_rows(x[80 + r * NBP : 80 + (r + 1) * NBP], 32).astype(BF)
        right.append(jnp.concatenate([h, h, l], axis=0))
    points = dot(fpw[...], jnp.concatenate(right, axis=1))
    values = []
    for r in range(3):
        cols = slice(r * count, (r + 1) * count)
        v = points[0:NP, cols]
        for g in range(1, 4):
            v = jnp.where(face == g, points[g * NP : (g + 1) * NP, cols], v)
        values.append(v)
    return values


def slot_kernel(fhl, proj, fse, fsf, fme, fmf, live, load, state, out, keep, mat, fpw):
    @pl.when(pl.program_id(0) == 0)
    def _():
        fpw[...] = left3(mat, [(0, g * NP, proj[g].T) for g in range(4)], 32, 64)

    def place(tile, x):
        out[pl.ds(tile, SC // 16, stride=TILES), :] = to_blocks(x)

    def place_points(n, x):
        for g in range(2):
            place(2 * n + g, x[8 * g : 8 * g + 8])

    place(12, jnp.broadcast_to(live[...].astype(F32), (8, SC)))
    place_points(4, load[0])
    place_points(5, state[0])
    values = fault_values(
        fhl, fpw, jnp.concatenate([fse[...], fme[...]], axis=1), jnp.concatenate([fsf[...], fmf[...]], axis=1)
    )
    plus, minus = [v[:, 0:SC] for v in values], [v[:, SC : 2 * SC] for v in values]
    for n, x in enumerate((plus[1] + plus[2], plus[0], minus[1] - minus[2], minus[0])):
        place_points(n, x)
    for n, x in enumerate((plus[1], minus[1])):
        for g in range(2):
            at = (2 * n + g) * LANES
            keep[:, at : at + LANES] = to_blocks(x[8 * g : 8 * g + 8])


def element_kernel(
    integ, dofs, star, couple, omega, fminus, fplus, area, nelem, nface, ihl, rim0, rim1, rim2, rim3,
    kdiff, proj, lift, base, mat, kdw, fpw, ltw, plw, rhl, change,
):
    c = pl.program_id(0)

    def put_rim(k, fields):
        flat = jnp.concatenate([pad_rows(x, NBP) for x in fields], axis=0)
        hi, lo = split(pad_rows(flat, ROWS))
        rhl[0:ROWS, k * BND : (k + 1) * BND] = hi
        rhl[ROWS : 2 * ROWS, k * BND : (k + 1) * BND] = lo

    @pl.when(c == 0)
    def _():
        kdw[...] = left3(mat, [(d * NBP, 0, kdiff[d]) for d in range(3)], 80, 32)
        fpw[...] = left3(mat, [(0, g * NP, proj[g].T) for g in range(4)], 32, 64)
        ltw[...] = left3(mat, [(f * NP, 0, lift[f]) for f in range(4)], 64, 32)
        both = [
            lax.dot_general(
                proj[f], lift[f], (((0,), (0,)), ((), ())),
                precision=lax.Precision.HIGHEST, preferred_element_type=F32,
            )
            for f in range(4)
        ]
        plw[...] = left3(mat, [(0, f * NBP, both[f]) for f in range(4)], 32, 96)
        for k, first, second, axis in ((0, rim0, rim1, "strike"), (2, rim2, rim3, "depth")):
            at = lax.axis_index(axis)
            even = (at % 2 == 0).astype(F32)
            odd = 1.0 - even
            before = (at > 0).astype(F32)
            after = (at < lax.axis_size(axis) - 1).astype(F32)
            for side, one, two in ((k, odd * before, even * before), (k + 1, even * after, odd * after)):
                put_rim(side, [one * first[j] + two * second[j] for j in range(NE)])
    def spread(ref):
        return jnp.concatenate([ref[f : f + 1, :] for f in range(4)], axis=1)

    def gather():
        elem = spread(nelem)
        return dot(ihl[...], one_hot(elem, E_DEV)) + dot(rhl[...], one_hot(elem, 4 * BND, E_DEV))

    def project(got):
        right = []
        for j in range(NE):
            hi = pad_rows(got[j * NBP : (j + 1) * NBP], 32).astype(BF)
            lo = pad_rows(got[ROWS + j * NBP : ROWS + (j + 1) * NBP], 32).astype(BF)
            right.append(jnp.concatenate([hi, hi, lo], axis=0))
        return dot(fpw[...], jnp.concatenate(right, axis=1))

    def choose(points):
        face, scale = spread(nface), spread(area)
        out = []
        for j in range(NE):
            cols = slice(j * E_DEV, (j + 1) * E_DEV)
            v = points[0:NP, cols]
            for g in range(1, 4):
                v = jnp.where(face == g, points[g * NP : (g + 1) * NP, cols], v)
            v = v * scale
            out.append(jnp.concatenate([v[:, f * LANES : (f + 1) * LANES] for f in range(4)], axis=0))
        return out

    kd = kdw[...]
    got = gather()
    acc = stress_of(lambda j: integ[j], star, kd)
    folded = dot(plw[...], jnp.concatenate([stack3(pad_rows(integ[j], 32)) for j in range(NE)], axis=1))
    points = project(got)
    for q in range(6):
        old = [integ[NE + 6 * l + q] for l in range(MECH)]
        relax = couple[0, q : q + 1, :] * old[0]
        for l in range(1, MECH):
            relax = relax + couple[l, q : q + 1, :] * old[l]
        for l in range(MECH):
            change[NE + 6 * l + q] = omega[l : l + 1, :] * (acc[q] - old[l])
        change[q] = acc[q] - relax
    for q in range(6, NE):
        change[q] = acc[q]
    total = [None] * NE
    for j in range(NE):
        cols = slice(j * LANES, (j + 1) * LANES)
        w = area[0:1, :] * folded[0:NBP, cols]
        for f in range(1, 4):
            w = w + area[f : f + 1, :] * folded[f * NBP : (f + 1) * NBP, cols]
        for i in range(NE):
            t = fminus[i, j : j + 1, :] * w
            total[i] = t if j == 0 else total[i] + t
    for i in range(NE):
        change[i] += total[i]
    lifted = dot(ltw[...], jnp.concatenate([stack3(v) for v in choose(points)], axis=1))
    for i in range(NE):
        t = change[i]
        for j in range(NE):
            t = t + fplus[i, j : j + 1, :] * lifted[0:NBP, j * LANES : (j + 1) * LANES]
        change[i] = t
    base[...] = dofs[...] + jnp.transpose(change[:, 0:NB, :], (1, 0, 2))


def friction(trial, pressure, load, state):
    sigma = load * (1.0 + 0.5 * jnp.tanh(0.5 * pressure))
    half = AFRIC * sigma
    steep = half * state
    size = jnp.abs(trial)
    slip = size / (ETA + steep)
    for turn in range(NEWTON - 1):
        scaled = state * slip
        square = 1.0 + scaled * scaled
        inverse = lax.rsqrt(square)
        resid = size - ETA * slip - half * jnp.log(scaled + square * inverse)
        slope = ETA + steep * inverse
        guess = pl.reciprocal(slope, approx=True)
        slip = slip + resid * (guess * (2.0 - slope * guess))
    slip = jnp.where(trial < 0.0, -slip, slip)
    return trial - ETA * slip, slip


def fault_kernel(
    base_in, mine, theirs, keep, fse, fsf, fme, fmf, live, lift,
    base, mat, lfw, acc, slab, sem,
):
    del base_in
    s = pl.program_id(0)
    window = base.at[:, 0:8, :]

    @pl.when(s == 0)
    def _():
        pltpu.make_async_copy(window, slab, sem).start()
        lfw[...] = left3(mat, [(0, f * NBP, lift[f]) for f in range(4)], 16, 96)

    def tile(ref, n):
        return ref[pl.ds(s * (SC // 16 * TILES) + n, SC // 16, stride=TILES), :]

    def pair(ref, n):
        return jnp.concatenate([tile(ref, 2 * n), tile(ref, 2 * n + 1)], axis=1)

    pull, slip = friction(
        0.5 * (pair(theirs, 0) + pair(mine, 2)), pair(mine, 3) + pair(theirs, 1),
        pair(mine, 4), pair(mine, 5),
    )
    terms = [pull - keep[:, 256:512], -0.5 * slip]
    pull, slip = friction(
        0.5 * (pair(mine, 0) + pair(theirs, 2)), pair(theirs, 3) + pair(mine, 1),
        pair(theirs, 4), pair(theirs, 5),
    )
    terms += [pull - keep[:, 0:256], 0.5 * slip]
    right = []
    for t in terms:
        x = jnp.concatenate([to_slots(t[:, 0:LANES]), to_slots(t[:, LANES:256])], axis=0)
        right.append(stack3(x))
    added = dot(lfw[...], jnp.concatenate(right, axis=1))
    far = to_slots(tile(theirs, 12))[0:1]
    left = []
    for side, (alive, face) in enumerate(((live[...].astype(F32), fmf[...]), (far, fsf[...]))):
        sums = []
        for k in range(2):
            at = slice((2 * side + k) * SC, (2 * side + k + 1) * SC)
            y = added[0:NBP, at]
            for f in range(1, 4):
                y = jnp.where(face == f, added[f * NBP : (f + 1) * NBP, at], y)
            sums.append(y * alive)
        hi, lo = split(jnp.concatenate(sums, axis=0))
        left.append(jnp.concatenate([hi, lo], axis=0))
    spots = jnp.concatenate([one_hot(fme[...], E_DEV), one_hot(fse[...], E_DEV)], axis=1)
    acc[s] = dot_nt(jnp.concatenate(left, axis=1), spots)

    @pl.when(s == SLOTS // SC - 1)
    def _():
        total = acc[0]
        for part in range(1, SLOTS // SC):
            total = total + acc[part]
        acc[0, 0:48, :] = total[0:48] + total[48:96]
        pltpu.make_async_copy(window, slab, sem).wait()
        for b in range(NB):
            for k in range(2):
                row = slice(FAULT_ROWS[1 + k], FAULT_ROWS[1 + k] + 1)
                slab[b, row, :] = slab[b, row, :] + acc[0, k * NBP + b : k * NBP + b + 1, :]
        copy = pltpu.make_async_copy(slab, window, sem)
        copy.start()
        copy.wait()


def whole(shape):
    return pl.BlockSpec(shape, lambda *i: (0,) * len(shape))


def lanes(*lead, width=LANES):
    return pl.BlockSpec(lead + (width,), lambda c: (0,) * len(lead) + (c,))


def wide(*lead):
    return lanes(*lead, width=WIDE)


def per_device(
    dofs, star, kdiff, couple, omega, flux_minus, flux_plus, area, face_proj, face_lift,
    nbr_elem, nbr_face, weight_class, send_rows, fault_send_elem, fault_send_face,
    fault_minus_elem, fault_minus_face, fault_live, normal_load, state,
):
    shape = jax.ShapeDtypeStruct
    wc = weight_class.reshape(1, E_DEV)
    dofs = jnp.transpose(dofs, (1, 0, 2))
    star = jnp.transpose(star, (1, 2, 0, 3))
    face_proj = jnp.transpose(face_proj, (0, 2, 1))
    rim = whole((NE, NB, BND))
    lines = pl.BlockSpec((SC // 16 * TILES, LANES), lambda c: (c, 0))
    kept = pl.BlockSpec((SC // 16, 4 * LANES), lambda c: (c, 0))
    slots = pl.BlockSpec((1, SC), lambda c: (0, c))
    points = pl.BlockSpec((1, NP, SC), lambda c: (0, 0, c))
    params = pltpu.CompilerParams(vmem_limit_bytes=VMEM)
    integ, ihl, fhl, s0, s1, s2, s3 = pl.pallas_call(
        predict_kernel,
        grid=(CHUNKS // PAIR,),
        in_specs=[
            wide(NB, NQ), wide(NE, NE, 3), wide(MECH, 6), wide(MECH), wide(1),
            whole((3, NB, NB)), whole((4, BND)),
        ],
        out_specs=[
            wide(NQ, NBP), whole((2 * ROWS, E_DEV)), whole((160, E_DEV)), rim, rim, rim, rim,
        ],
        out_shape=[
            shape((NQ, NBP, E_DEV), F32), shape((2 * ROWS, E_DEV), BF), shape((160, E_DEV), BF),
            *[pltpu.HBM((NE, NB, BND), F32)] * 4,
        ],
        scratch_shapes=[
            pltpu.VMEM((NQ, NBP, WIDE), F32), pltpu.VMEM((80, LANES), F32),
            pltpu.VMEM((32, 240), BF),
        ],
        compiler_params=params,
        name="predict",
    )(dofs, star, couple, omega, wc, kdiff, send_rows)
    out, keep = pl.pallas_call(
        slot_kernel,
        grid=(SLOTS // SC,),
        in_specs=[whole((160, E_DEV)), whole((4, NP, NB)), *[slots] * 5, points, points],
        out_specs=[lines, kept],
        out_shape=[shape((DEVICES * TILES, LANES), F32), shape((DEVICES, 4 * LANES), F32)],
        scratch_shapes=[pltpu.VMEM((64, LANES), F32), pltpu.VMEM((64, 96), BF)],
        compiler_params=params,
        name="slots",
    )(
        fhl, face_proj, fault_send_elem, fault_send_face, fault_minus_elem, fault_minus_face,
        fault_live, normal_load, state,
    )
    ns, nd = lax.axis_size("strike"), lax.axis_size("depth")

    def swap(x, axis, n, first):
        ends = [(i, (i + 1) % n) for i in range(first, n, 2)]
        return lax.ppermute(x, axis, ends + [(j, i) for i, j in ends])

    r0 = swap(s0, "strike", ns, 0)
    r1 = swap(s1, "strike", ns, 1)
    r2 = swap(s2, "depth", nd, 0)
    r3 = swap(s3, "depth", nd, 1)
    r0, r1, r2, r3, sent = lax.optimization_barrier((r0, r1, r2, r3, out))
    theirs = lax.all_to_all(
        sent.reshape(DEVICES, 1, TILES * LANES), ("strike", "depth"), split_axis=0, concat_axis=0, tiled=True
    ).reshape(DEVICES * TILES, LANES)
    base = pl.pallas_call(
        element_kernel,
        grid=(CHUNKS,),
        in_specs=[
            lanes(NQ, NBP), lanes(NB, NQ), lanes(NE, NE, 3), lanes(MECH, 6), lanes(MECH),
            lanes(NE, NE), lanes(NE, NE), lanes(4), lanes(4), lanes(4),
            whole((2 * ROWS, E_DEV)), rim, rim, rim, rim,
            whole((3, NB, NB)), whole((4, NP, NB)), whole((4, NP, NB)),
        ],
        out_specs=lanes(NB, NQ),
        out_shape=pltpu.HBM((NB, NQ, E_DEV), F32),
        scratch_shapes=[
            pltpu.VMEM((80, LANES), F32),
            pltpu.VMEM((32, 240), BF), pltpu.VMEM((64, 96), BF), pltpu.VMEM((32, 192), BF),
            pltpu.VMEM((96, 96), BF), pltpu.VMEM((2 * ROWS, 4 * BND), BF),
            pltpu.VMEM((NQ, NBP, LANES), F32),
        ],
        compiler_params=params,
        name="elements",
    )(
        integ, dofs, star, couple, omega, flux_minus, flux_plus, area, nbr_elem, nbr_face,
        ihl, r0, r1, r2, r3, kdiff, face_proj, face_lift,
    )
    anywhere = pl.BlockSpec(memory_space=pl.ANY)
    resident = pl.BlockSpec(memory_space=pltpu.VMEM)
    result = pl.pallas_call(
        fault_kernel,
        grid=(SLOTS // SC,),
        in_specs=[
            anywhere, resident, resident, kept,
            slots, slots, slots, slots, slots, whole((4, NP, NB)),
        ],
        out_specs=anywhere,
        out_shape=shape((NB, NQ, E_DEV), F32),
        input_output_aliases={0: 0},
        scratch_shapes=[
            pltpu.VMEM((64, LANES), F32), pltpu.VMEM((96, 48), BF), pltpu.VMEM((SLOTS // SC, 96, E_DEV), F32),
            pltpu.VMEM((NB, 8, E_DEV), F32), pltpu.SemaphoreType.DMA,
        ],
        compiler_params=params,
        name="fault",
    )(
        base, sent, theirs, keep, fault_send_elem, fault_send_face, fault_minus_elem,
        fault_minus_face, fault_live, face_lift,
    )
    return jnp.transpose(result, (1, 0, 2))


def solution(mesh):
    both = ("strike", "depth")
    split_1, split_2, split_3 = P(None, both), P(None, None, both), P(None, None, None, both)
    in_specs = (
        split_2, split_3, P(), split_2, split_1, split_2, split_2, split_1, P(), P(),
        split_1, split_1, P(both), split_1,
        *[P(both, None)] * 5, P(both, None, None), P(both, None, None),
    )
    return jax.shard_map(
        per_device, mesh=mesh, in_specs=in_specs, out_specs=split_2, check_vma=False
    )
```

```python
import jax
import jax.numpy as jnp
from jax import lax
from jax.experimental import pallas as pl
from jax.experimental.pallas import tpu as pltpu
from jax.sharding import PartitionSpec as P

NQ = 27
NE = 9
MECH = 3
NB = 20
NP = 16
ORDER = 4
NEWTON = 4
ETA = 1.0
AFRIC = 0.5
E_DEV = 512
BND = 128
SLOTS = 2048
DEVICES = 128
NBP = 24
LANES = 128
CHUNKS = E_DEV // LANES
PAIR = 2
WIDE = PAIR * LANES
ROWS = 224
TILES = 13
F32 = jnp.float32
BF = jnp.bfloat16
VMEM = 56 * 1024 * 1024
VMEM_SMALL = 40 * 1024 * 1024
FAULT_ROWS = (0, 3, 6)


def split(x):
    hi = x.astype(BF)
    return hi, (x - hi.astype(F32)).astype(BF)


def pad_rows(x, rows):
    extra = rows - x.shape[0]
    if extra == 0:
        return x
    return jnp.concatenate([x, jnp.zeros((extra,) + x.shape[1:], x.dtype)], axis=0)


def stack3(x):
    hi, lo = split(x)
    return jnp.concatenate([hi, hi, lo], axis=0)


def left3(scratch, parts, depth, rows):
    scratch[...] = jnp.zeros(scratch.shape, F32)
    for row, col, value in parts:
        scratch[row : row + value.shape[0], col : col + value.shape[1]] = value
    whole = scratch[0:depth, :]
    hi = whole.astype(BF).astype(F32)
    lo = whole - hi
    tall = jnp.concatenate([hi, lo, hi], axis=0)
    tall = pad_rows(tall, -(-tall.shape[0] // 128) * 128)
    return jnp.transpose(tall, (1, 0))[0:rows, 0 : 3 * depth].astype(BF)


def dot(a, b):
    return lax.dot_general(a, b, (((1,), (0,)), ((), ())), preferred_element_type=F32)


def dot_nt(a, b):
    return lax.dot_general(a, b, (((1,), (1,)), ((), ())), preferred_element_type=F32)


def one_hot(index, rows, base=0):
    row = lax.broadcasted_iota(jnp.int32, (rows, LANES), 0).astype(jnp.int16)
    index = jnp.broadcast_to(index - base, (16, index.shape[1])).astype(jnp.int16)
    out = []
    for t in range(index.shape[1] // LANES):
        here = jnp.concatenate([index[:, t * LANES : (t + 1) * LANES]] * (rows // 16), axis=0)
        out.append(jnp.where(row == here, jnp.ones((), BF), jnp.zeros((), BF)))
    return jnp.concatenate(out, axis=1)


def swap_blocks(x):
    x = pltpu.roll(x, 0, 1, stride=16, stride_axis=0)
    lane = lax.broadcasted_iota(jnp.int32, (8, LANES), 1)
    sub = lax.broadcasted_iota(jnp.int32, (8, LANES), 0)
    down = jnp.bitwise_and(lane // 16 - sub, 7)
    across = jnp.bitwise_and(lane + 16 * sub, LANES - 1)
    tiles = []
    for t in range(x.shape[0] // 8):
        y = jnp.take_along_axis(x[8 * t : 8 * t + 8], down, axis=0, mode="promise_in_bounds")
        tiles.append(jnp.take_along_axis(y, across, axis=1, mode="promise_in_bounds"))
    return jnp.concatenate(tiles, axis=0)


def to_blocks(x):
    return swap_blocks(
        jnp.concatenate([x[:, t * LANES : (t + 1) * LANES] for t in range(SLOTS // LANES)], axis=0)
    )


def to_slots(x):
    x = swap_blocks(x)
    return jnp.concatenate([x[8 * t : 8 * t + 8] for t in range(SLOTS // LANES)], axis=1)


def stress_of(get, star_ref, kd, rows=range(NE)):
    fields = [get(j) for j in range(NE)]
    out = []
    for i in rows:
        mixed = []
        for d in range(3):
            t = star_ref[i, 0, d : d + 1, :] * fields[0]
            for j in range(1, NE):
                t = t + star_ref[i, j, d : d + 1, :] * fields[j]
            mixed.append(t)
        out.append(dot(kd, stack3(pad_rows(jnp.concatenate(mixed, axis=0), 80)))[0:NBP])
    return out


def predict_kernel(
    dofs, star, couple, omega, wc, kdiff, srow,
    integ, ihl, fhl, send0, send1, send2, send3,
    term, mat, kdw,
):
    c = pl.program_id(0)

    @pl.when(c == 0)
    def _():
        kdw[...] = left3(mat, [(d * NBP, 0, kdiff[d]) for d in range(3)], 80, 32)
        term[...] = jnp.zeros(term.shape, F32)

    kd = kdw[...]
    step = 1.0 / (1.0 + wc[...].astype(F32))
    term[:, 0:NB, :] = jnp.transpose(dofs[...], (1, 0, 2))
    for q in range(NQ):
        integ[q] = step * term[q]

    def derive(cols, power):
        acc = stress_of(lambda j: term[j, :, cols], star.at[:, :, :, cols], kd)
        for q in range(6):
            old = [term[NE + 6 * l + q, :, cols] for l in range(MECH)]
            relax = couple[0, q : q + 1, cols] * old[0]
            for l in range(1, MECH):
                relax = relax + couple[l, q : q + 1, cols] * old[l]
            new = acc[q] - relax
            term[q, :, cols] = new
            integ[q, :, cols] += power * new
            for l in range(MECH):
                new = omega[l : l + 1, cols] * (acc[q] - old[l])
                term[NE + 6 * l + q, :, cols] = new
                integ[NE + 6 * l + q, :, cols] += power * new
        for q in range(6, NE):
            term[q, :, cols] = acc[q]
            integ[q, :, cols] += power * acc[q]

    def turn(order, power):
        power = power * step / (order + 2).astype(F32)
        for half in range(PAIR):
            cols = slice(half * LANES, (half + 1) * LANES)
            derive(cols, power[:, cols])
        return power

    lax.fori_loop(0, ORDER - 1, turn, step)

    here = pl.ds(pl.multiple_of(c * WIDE, WIDE), WIDE)
    flat = pad_rows(integ[0:NE].reshape(NE * NBP, WIDE), ROWS)
    hi, lo = split(flat)
    ihl[0:ROWS, here] = hi
    ihl[ROWS : 2 * ROWS, here] = lo
    hi, lo = split(pad_rows(jnp.concatenate([integ[r] for r in FAULT_ROWS], axis=0), 80))
    fhl[0:80, here] = hi
    fhl[80:160, here] = lo

    @pl.when(c == CHUNKS // PAIR - 1)
    def _():
        rows = []
        for axis, k in (("strike", 0), ("depth", 2)):
            even = lax.axis_index(axis) % 2 == 0
            ahead, behind = srow[k : k + 1, :], srow[k + 1 : k + 2, :]
            rows += [jnp.where(even, ahead, behind), jnp.where(even, behind, ahead)]
        rows = jnp.concatenate(rows, axis=1)
        got = dot(ihl[...], one_hot(rows, E_DEV))
        got = got[0:ROWS] + got[ROWS : 2 * ROWS]
        for k, ref in enumerate((send0, send1, send2, send3)):
            for j in range(NE):
                ref[j] = got[j * NBP : j * NBP + NB, k * BND : (k + 1) * BND]


def fault_values(fhl, fpw, elem, face):
    count = elem.shape[1]
    x = dot(fhl[...], one_hot(elem, E_DEV))
    right = []
    for r in range(3):
        h = pad_rows(x[r * NBP : (r + 1) * NBP], 32).astype(BF)
        l = pad_rows(x[80 + r * NBP : 80 + (r + 1) * NBP], 32).astype(BF)
        right.append(jnp.concatenate([h, h, l], axis=0))
    points = dot(fpw[...], jnp.concatenate(right, axis=1))
    values = []
    for r in range(3):
        cols = slice(r * count, (r + 1) * count)
        v = points[0:NP, cols]
        for g in range(1, 4):
            v = jnp.where(face == g, points[g * NP : (g + 1) * NP, cols], v)
        values.append(v)
    return values


def slot_kernel(fhl, proj, fse, fsf, fme, fmf, live, load, state, out, keep, mat, fpw):
    fpw[...] = left3(mat, [(0, g * NP, proj[g].T) for g in range(4)], 32, 64)

    def place(tile, x):
        out[pl.ds(tile, DEVICES, stride=TILES), :] = to_blocks(x)

    def place_points(n, x):
        for g in range(2):
            place(2 * n + g, x[8 * g : 8 * g + 8])

    place(12, jnp.broadcast_to(live[...].astype(F32), (8, SLOTS)))
    place_points(4, load[0])
    place_points(5, state[0])
    values = fault_values(
        fhl, fpw, jnp.concatenate([fse[...], fme[...]], axis=1), jnp.concatenate([fsf[...], fmf[...]], axis=1)
    )
    plus, minus = [v[:, 0:SLOTS] for v in values], [v[:, SLOTS : 2 * SLOTS] for v in values]
    for n, x in enumerate((plus[1] + plus[2], plus[0], minus[1] - minus[2], minus[0])):
        place_points(n, x)
    for n, x in enumerate((plus[1], minus[1])):
        for g in range(2):
            at = (2 * n + g) * LANES
            keep[:, at : at + LANES] = to_blocks(x[8 * g : 8 * g + 8])


def element_kernel(
    integ, dofs, star, couple, omega, fminus, fplus, area, nelem, nface, ihl, rim0, rim1, rim2, rim3,
    kdiff, proj, lift, base, mat, kdw, fpw, ltw, plw, rhl, change,
):
    c = pl.program_id(0)

    def put_rim(k, fields):
        flat = jnp.concatenate([pad_rows(x, NBP) for x in fields], axis=0)
        hi, lo = split(pad_rows(flat, ROWS))
        rhl[0:ROWS, k * BND : (k + 1) * BND] = hi
        rhl[ROWS : 2 * ROWS, k * BND : (k + 1) * BND] = lo

    @pl.when(c == 0)
    def _():
        kdw[...] = left3(mat, [(d * NBP, 0, kdiff[d]) for d in range(3)], 80, 32)
        fpw[...] = left3(mat, [(0, g * NP, proj[g].T) for g in range(4)], 32, 64)
        ltw[...] = left3(mat, [(f * NP, 0, lift[f]) for f in range(4)], 64, 32)
        both = [
            lax.dot_general(
                proj[f], lift[f], (((0,), (0,)), ((), ())),
                precision=lax.Precision.HIGHEST, preferred_element_type=F32,
            )
            for f in range(4)
        ]
        plw[...] = left3(mat, [(0, f * NBP, both[f]) for f in range(4)], 32, 96)
        for k, first, second, axis in ((0, rim0, rim1, "strike"), (2, rim2, rim3, "depth")):
            at = lax.axis_index(axis)
            even = (at % 2 == 0).astype(F32)
            odd = 1.0 - even
            before = (at > 0).astype(F32)
            after = (at < lax.axis_size(axis) - 1).astype(F32)
            for side, one, two in ((k, odd * before, even * before), (k + 1, even * after, odd * after)):
                put_rim(side, [one * first[j] + two * second[j] for j in range(NE)])
    def spread(ref):
        return jnp.concatenate([ref[f : f + 1, :] for f in range(4)], axis=1)

    def gather():
        elem = spread(nelem)
        return dot(ihl[...], one_hot(elem, E_DEV)) + dot(rhl[...], one_hot(elem, 4 * BND, E_DEV))

    def project(got):
        right = []
        for j in range(NE):
            hi = pad_rows(got[j * NBP : (j + 1) * NBP], 32).astype(BF)
            lo = pad_rows(got[ROWS + j * NBP : ROWS + (j + 1) * NBP], 32).astype(BF)
            right.append(jnp.concatenate([hi, hi, lo], axis=0))
        return dot(fpw[...], jnp.concatenate(right, axis=1))

    def choose(points):
        face, scale = spread(nface), spread(area)
        out = []
        for j in range(NE):
            cols = slice(j * E_DEV, (j + 1) * E_DEV)
            v = points[0:NP, cols]
            for g in range(1, 4):
                v = jnp.where(face == g, points[g * NP : (g + 1) * NP, cols], v)
            v = v * scale
            out.append(jnp.concatenate([v[:, f * LANES : (f + 1) * LANES] for f in range(4)], axis=0))
        return out

    kd = kdw[...]
    got = gather()
    acc = stress_of(lambda j: integ[j], star, kd)
    folded = dot(plw[...], jnp.concatenate([stack3(pad_rows(integ[j], 32)) for j in range(NE)], axis=1))
    points = project(got)
    for q in range(6):
        old = [integ[NE + 6 * l + q] for l in range(MECH)]
        relax = couple[0, q : q + 1, :] * old[0]
        for l in range(1, MECH):
            relax = relax + couple[l, q : q + 1, :] * old[l]
        for l in range(MECH):
            change[NE + 6 * l + q] = omega[l : l + 1, :] * (acc[q] - old[l])
        change[q] = acc[q] - relax
    for q in range(6, NE):
        change[q] = acc[q]
    total = [None] * NE
    for j in range(NE):
        cols = slice(j * LANES, (j + 1) * LANES)
        w = area[0:1, :] * folded[0:NBP, cols]
        for f in range(1, 4):
            w = w + area[f : f + 1, :] * folded[f * NBP : (f + 1) * NBP, cols]
        for i in range(NE):
            t = fminus[i, j : j + 1, :] * w
            total[i] = t if j == 0 else total[i] + t
    for i in range(NE):
        change[i] += total[i]
    lifted = dot(ltw[...], jnp.concatenate([stack3(v) for v in choose(points)], axis=1))
    for i in range(NE):
        t = change[i]
        for j in range(NE):
            t = t + fplus[i, j : j + 1, :] * lifted[0:NBP, j * LANES : (j + 1) * LANES]
        change[i] = t
    base[...] = dofs[...] + jnp.transpose(change[:, 0:NB, :], (1, 0, 2))


def inverse_of(x):
    guess = pl.reciprocal(x, approx=True)
    return guess * (2.0 - x * guess)


def friction(trial, pressure, load, state):
    sigma = load * (1.0 + 0.5 * jnp.tanh(0.5 * pressure))
    half = AFRIC * sigma
    steep = half * state
    size = jnp.abs(trial)
    slip = size * inverse_of(ETA + steep)
    for turn in range(NEWTON - 1):
        scaled = state * slip
        square = 1.0 + scaled * scaled
        inverse = lax.rsqrt(square)
        resid = size - ETA * slip - half * jnp.log(scaled + square * inverse)
        slip = slip + resid * inverse_of(ETA + steep * inverse)
    slip = jnp.where(trial < 0.0, -slip, slip)
    return trial - ETA * slip, slip


def fault_kernel(
    base_in, mine, theirs, keep, fse, fsf, fme, fmf, live, lift,
    base, mat, lfw, slab, sem,
):
    del base_in
    window = base.at[:, 0:8, :]
    read_slab = pltpu.make_async_copy(window, slab, sem)
    read_slab.start()
    lfw[...] = left3(mat, [(0, f * NBP, lift[f]) for f in range(4)], 16, 96)

    def tile(ref, n):
        return ref[pl.ds(n, DEVICES, stride=TILES), :]

    def pair(ref, n):
        return jnp.concatenate([tile(ref, 2 * n), tile(ref, 2 * n + 1)], axis=1)

    def side(one, other, load, state, kept, sign, alive, face, elem):
        pull, slip = friction(0.5 * (pair(theirs, other[0]) + pair(mine, one[0])), pair(mine, one[1]) + pair(theirs, other[1]), load, state)
        right = []
        for t in (pull - kept, sign * slip):
            x = jnp.concatenate([to_slots(t[:, 0:LANES]), to_slots(t[:, LANES:256])], axis=0)
            right.append(stack3(x))
        added = dot(lfw[...], jnp.concatenate(right, axis=1))
        sums = []
        for k in range(2):
            at = slice(k * SLOTS, (k + 1) * SLOTS)
            y = added[0:NBP, at]
            for f in range(1, 4):
                y = jnp.where(face == f, added[f * NBP : (f + 1) * NBP, at], y)
            sums.append(y * alive)
        hi, lo = split(jnp.concatenate(sums, axis=0))
        return dot_nt(jnp.concatenate([hi, lo], axis=0), one_hot(elem, E_DEV))

    minus = side(
        (2, 3), (0, 1), pair(mine, 4), pair(mine, 5), keep[:, 256:512], -0.5,
        live[...].astype(F32), fmf[...], fme[...],
    )
    far = to_slots(tile(theirs, 12))[0:1]
    plus = side(
        (0, 1), (2, 3), pair(theirs, 4), pair(theirs, 5), keep[:, 0:256], 0.5,
        far, fsf[...], fse[...],
    )
    both = minus + plus
    delta = both[0:48] + both[48:96]
    read_slab.wait()
    for b in range(NB):
        for k in range(2):
            row = slice(FAULT_ROWS[1 + k], FAULT_ROWS[1 + k] + 1)
            slab[b, row, :] = slab[b, row, :] + delta[k * NBP + b : k * NBP + b + 1, :]
    write = pltpu.make_async_copy(slab, window, sem)
    write.start()
    write.wait()


def whole(shape):
    return pl.BlockSpec(shape, lambda *i: (0,) * len(shape))


def lanes(*lead, width=LANES):
    return pl.BlockSpec(lead + (width,), lambda c: (0,) * len(lead) + (c,))


def wide(*lead):
    return lanes(*lead, width=WIDE)


def per_device(
    dofs, star, kdiff, couple, omega, flux_minus, flux_plus, area, face_proj, face_lift,
    nbr_elem, nbr_face, weight_class, send_rows, fault_send_elem, fault_send_face,
    fault_minus_elem, fault_minus_face, fault_live, normal_load, state,
):
    shape = jax.ShapeDtypeStruct
    wc = weight_class.reshape(1, E_DEV)
    dofs = jnp.transpose(dofs, (1, 0, 2))
    star = jnp.transpose(star, (1, 2, 0, 3))
    face_proj = jnp.transpose(face_proj, (0, 2, 1))
    rim = whole((NE, NB, BND))
    resident = pl.BlockSpec(memory_space=pltpu.VMEM)
    params = pltpu.CompilerParams(vmem_limit_bytes=VMEM)
    small = pltpu.CompilerParams(vmem_limit_bytes=VMEM_SMALL)
    integ, ihl, fhl, s0, s1, s2, s3 = pl.pallas_call(
        predict_kernel,
        grid=(CHUNKS // PAIR,),
        in_specs=[
            wide(NB, NQ), wide(NE, NE, 3), wide(MECH, 6), wide(MECH), wide(1),
            whole((3, NB, NB)), whole((4, BND)),
        ],
        out_specs=[
            wide(NQ, NBP), whole((2 * ROWS, E_DEV)), whole((160, E_DEV)), rim, rim, rim, rim,
        ],
        out_shape=[
            shape((NQ, NBP, E_DEV), F32), shape((2 * ROWS, E_DEV), BF), shape((160, E_DEV), BF),
            *[pltpu.HBM((NE, NB, BND), F32)] * 4,
        ],
        scratch_shapes=[
            pltpu.VMEM((NQ, NBP, WIDE), F32), pltpu.VMEM((80, LANES), F32),
            pltpu.VMEM((32, 240), BF),
        ],
        compiler_params=params,
        name="predict",
    )(dofs, star, couple, omega, wc, kdiff, send_rows)
    out, keep = pl.pallas_call(
        slot_kernel,
        in_specs=[resident] * 9,
        out_specs=[resident] * 2,
        out_shape=[shape((DEVICES * TILES, LANES), F32), shape((DEVICES, 4 * LANES), F32)],
        scratch_shapes=[pltpu.VMEM((64, LANES), F32), pltpu.VMEM((64, 96), BF)],
        compiler_params=small,
        name="slots",
    )(
        fhl, face_proj, fault_send_elem, fault_send_face, fault_minus_elem, fault_minus_face,
        fault_live, normal_load, state,
    )
    ns, nd = lax.axis_size("strike"), lax.axis_size("depth")

    def swap(x, axis, n, first):
        ends = [(i, (i + 1) % n) for i in range(first, n, 2)]
        return lax.ppermute(x, axis, ends + [(j, i) for i, j in ends])

    r0 = swap(s0, "strike", ns, 0)
    r1 = swap(s1, "strike", ns, 1)
    r2 = swap(s2, "depth", nd, 0)
    r3 = swap(s3, "depth", nd, 1)
    r0, r1, r2, r3, sent = lax.optimization_barrier((r0, r1, r2, r3, out))
    theirs = lax.all_to_all(
        sent.reshape(DEVICES, 1, TILES * LANES), ("strike", "depth"), split_axis=0, concat_axis=0, tiled=True
    ).reshape(DEVICES * TILES, LANES)
    base = pl.pallas_call(
        element_kernel,
        grid=(CHUNKS,),
        in_specs=[
            lanes(NQ, NBP), lanes(NB, NQ), lanes(NE, NE, 3), lanes(MECH, 6), lanes(MECH),
            lanes(NE, NE), lanes(NE, NE), lanes(4), lanes(4), lanes(4),
            whole((2 * ROWS, E_DEV)), rim, rim, rim, rim,
            whole((3, NB, NB)), whole((4, NP, NB)), whole((4, NP, NB)),
        ],
        out_specs=lanes(NB, NQ),
        out_shape=pltpu.HBM((NB, NQ, E_DEV), F32),
        scratch_shapes=[
            pltpu.VMEM((80, LANES), F32),
            pltpu.VMEM((32, 240), BF), pltpu.VMEM((64, 96), BF), pltpu.VMEM((32, 192), BF),
            pltpu.VMEM((96, 96), BF), pltpu.VMEM((2 * ROWS, 4 * BND), BF),
            pltpu.VMEM((NQ, NBP, LANES), F32),
        ],
        compiler_params=small,
        name="elements",
    )(
        integ, dofs, star, couple, omega, flux_minus, flux_plus, area, nbr_elem, nbr_face,
        ihl, r0, r1, r2, r3, kdiff, face_proj, face_lift,
    )
    anywhere = pl.BlockSpec(memory_space=pl.ANY)
    result = pl.pallas_call(
        fault_kernel,
        in_specs=[anywhere] + [resident] * 9,
        out_specs=anywhere,
        out_shape=shape((NB, NQ, E_DEV), F32),
        input_output_aliases={0: 0},
        scratch_shapes=[
            pltpu.VMEM((64, LANES), F32), pltpu.VMEM((96, 48), BF),
            pltpu.VMEM((NB, 8, E_DEV), F32), pltpu.SemaphoreType.DMA,
        ],
        compiler_params=small,
        name="fault",
    )(
        base, sent, theirs, keep, fault_send_elem, fault_send_face, fault_minus_elem, fault_minus_face,
        fault_live, face_lift,
    )
    return jnp.transpose(result, (1, 0, 2))


def solution(mesh):
    both = ("strike", "depth")
    split_1, split_2, split_3 = P(None, both), P(None, None, both), P(None, None, None, both)
    in_specs = (
        split_2, split_3, P(), split_2, split_1, split_2, split_2, split_1, P(), P(),
        split_1, split_1, P(both), split_1,
        *[P(both, None)] * 5, P(both, None, None), P(both, None, None),
    )
    return jax.shard_map(
        per_device, mesh=mesh, in_specs=in_specs, out_specs=split_2, check_vma=False
    )
```

```python
import jax
import jax.numpy as jnp
from jax import lax
from jax.experimental import pallas as pl
from jax.experimental.pallas import tpu as pltpu
from jax.sharding import PartitionSpec as P

NQ = 27
NE = 9
MECH = 3
NB = 20
NP = 16
ORDER = 4
NEWTON = 4
ETA = 1.0
AFRIC = 0.5
E_DEV = 512
BND = 128
SLOTS = 2048
DEVICES = 128
NBP = 24
LANES = 128
CHUNKS = E_DEV // LANES
PAIR = 2
WIDE = PAIR * LANES
ROWS = 224
TILES = 13
F32 = jnp.float32
BF = jnp.bfloat16
VMEM = 56 * 1024 * 1024
VMEM_SMALL = 56 * 1024 * 1024
FAULT_ROWS = (0, 3, 6)


def split(x):
    hi = x.astype(BF)
    return hi, (x - hi.astype(F32)).astype(BF)


def pad_rows(x, rows):
    extra = rows - x.shape[0]
    if extra == 0:
        return x
    return jnp.concatenate([x, jnp.zeros((extra,) + x.shape[1:], x.dtype)], axis=0)


def stack3(x):
    hi, lo = split(x)
    return jnp.concatenate([hi, hi, lo], axis=0)


def left3(scratch, parts, depth, rows):
    scratch[...] = jnp.zeros(scratch.shape, F32)
    for row, col, value in parts:
        scratch[row : row + value.shape[0], col : col + value.shape[1]] = value
    whole = scratch[0:depth, :]
    hi = whole.astype(BF).astype(F32)
    lo = whole - hi
    tall = jnp.concatenate([hi, lo, hi], axis=0)
    tall = pad_rows(tall, -(-tall.shape[0] // 128) * 128)
    return jnp.transpose(tall, (1, 0))[0:rows, 0 : 3 * depth].astype(BF)


def dot(a, b):
    return lax.dot_general(a, b, (((1,), (0,)), ((), ())), preferred_element_type=F32)


def dot_nt(a, b):
    return lax.dot_general(a, b, (((1,), (1,)), ((), ())), preferred_element_type=F32)


def one_hot(index, rows, base=0):
    row = lax.broadcasted_iota(jnp.int32, (rows, LANES), 0).astype(jnp.int16)
    index = jnp.broadcast_to(index - base, (16, index.shape[1])).astype(jnp.int16)
    out = []
    for t in range(index.shape[1] // LANES):
        here = jnp.concatenate([index[:, t * LANES : (t + 1) * LANES]] * (rows // 16), axis=0)
        out.append(jnp.where(row == here, jnp.ones((), BF), jnp.zeros((), BF)))
    return jnp.concatenate(out, axis=1)


def one_hot_t(index, columns):
    column = lax.broadcasted_iota(jnp.int32, (16, columns), 1).astype(jnp.int16)
    column = jnp.concatenate([column] * (LANES // 16), axis=0)
    out = []
    for t in range(index.shape[1] // LANES):
        here = jnp.broadcast_to(index[:, t * LANES : (t + 1) * LANES], (LANES, LANES))
        here = jnp.transpose(here, (1, 0)).astype(jnp.int16)
        here = jnp.concatenate([here] * (columns // LANES), axis=1)
        out.append(jnp.where(column == here, jnp.ones((), BF), jnp.zeros((), BF)))
    return jnp.concatenate(out, axis=0)


def fetches(sources, held, sems):
    copies = [
        pltpu.make_async_copy(source, place, sems.at[n])
        for n, (source, place) in enumerate(zip(sources, held))
    ]
    for copy in copies:
        copy.start()
    return copies


def swap_blocks(x):
    x = pltpu.roll(x, 0, 1, stride=16, stride_axis=0)
    lane = lax.broadcasted_iota(jnp.int32, (8, LANES), 1)
    sub = lax.broadcasted_iota(jnp.int32, (8, LANES), 0)
    down = jnp.bitwise_and(lane // 16 - sub, 7)
    across = jnp.bitwise_and(lane + 16 * sub, LANES - 1)
    tiles = []
    for t in range(x.shape[0] // 8):
        y = jnp.take_along_axis(x[8 * t : 8 * t + 8], down, axis=0, mode="promise_in_bounds")
        tiles.append(jnp.take_along_axis(y, across, axis=1, mode="promise_in_bounds"))
    return jnp.concatenate(tiles, axis=0)


def to_blocks(x):
    return swap_blocks(
        jnp.concatenate([x[:, t * LANES : (t + 1) * LANES] for t in range(SLOTS // LANES)], axis=0)
    )


def to_slots(x):
    x = swap_blocks(x)
    return jnp.concatenate([x[8 * t : 8 * t + 8] for t in range(SLOTS // LANES)], axis=1)


def stress_of(get, star_ref, kd, rows=range(NE)):
    fields = [get(j) for j in range(NE)]
    out = []
    for i in rows:
        mixed = []
        for d in range(3):
            t = star_ref[i, 0, d : d + 1, :] * fields[0]
            for j in range(1, NE):
                t = t + star_ref[i, j, d : d + 1, :] * fields[j]
            mixed.append(t)
        out.append(dot(kd, stack3(pad_rows(jnp.concatenate(mixed, axis=0), 80)))[0:NBP])
    return out


def predict_kernel(
    dofs, star, couple, omega, wc, kdiff, srow,
    integ, ihl, fhl, send0, send1, send2, send3,
    term, mat, kdw,
):
    c = pl.program_id(0)

    @pl.when(c == 0)
    def _():
        kdw[...] = left3(mat, [(d * NBP, 0, kdiff[d]) for d in range(3)], 80, 32)
        term[...] = jnp.zeros(term.shape, F32)

    kd = kdw[...]
    step = 1.0 / (1.0 + wc[...].astype(F32))
    term[:, 0:NB, :] = jnp.transpose(dofs[...], (1, 0, 2))
    for q in range(NQ):
        integ[q] = step * term[q]

    def derive(cols, power):
        acc = stress_of(lambda j: term[j, :, cols], star.at[:, :, :, cols], kd)
        for q in range(6):
            old = [term[NE + 6 * l + q, :, cols] for l in range(MECH)]
            relax = couple[0, q : q + 1, cols] * old[0]
            for l in range(1, MECH):
                relax = relax + couple[l, q : q + 1, cols] * old[l]
            new = acc[q] - relax
            term[q, :, cols] = new
            integ[q, :, cols] += power * new
            for l in range(MECH):
                new = omega[l : l + 1, cols] * (acc[q] - old[l])
                term[NE + 6 * l + q, :, cols] = new
                integ[NE + 6 * l + q, :, cols] += power * new
        for q in range(6, NE):
            term[q, :, cols] = acc[q]
            integ[q, :, cols] += power * acc[q]

    def turn(order, power):
        power = power * step / (order + 2).astype(F32)
        for half in range(PAIR):
            cols = slice(half * LANES, (half + 1) * LANES)
            derive(cols, power[:, cols])
        return power

    lax.fori_loop(0, ORDER - 1, turn, step)

    here = pl.ds(pl.multiple_of(c * WIDE, WIDE), WIDE)
    flat = pad_rows(integ[0:NE].reshape(NE * NBP, WIDE), ROWS)
    hi, lo = split(flat)
    ihl[0:ROWS, here] = hi
    ihl[ROWS : 2 * ROWS, here] = lo
    hi, lo = split(pad_rows(jnp.concatenate([integ[r] for r in FAULT_ROWS], axis=0), 80))
    fhl[0:80, here] = hi
    fhl[80:160, here] = lo

    @pl.when(c == CHUNKS // PAIR - 1)
    def _():
        rows = []
        for axis, k in (("strike", 0), ("depth", 2)):
            even = lax.axis_index(axis) % 2 == 0
            ahead, behind = srow[k : k + 1, :], srow[k + 1 : k + 2, :]
            rows += [jnp.where(even, ahead, behind), jnp.where(even, behind, ahead)]
        rows = jnp.concatenate(rows, axis=1)
        got = dot(ihl[...], one_hot(rows, E_DEV))
        got = got[0:ROWS] + got[ROWS : 2 * ROWS]
        for k, ref in enumerate((send0, send1, send2, send3)):
            for j in range(NE):
                ref[j] = got[j * NBP : j * NBP + NB, k * BND : (k + 1) * BND]


def fault_values(fhl, fpw, elem, face):
    count = elem.shape[1]
    x = dot(fhl[...], one_hot(elem, E_DEV))
    right = []
    for r in range(3):
        h = pad_rows(x[r * NBP : (r + 1) * NBP], 32).astype(BF)
        l = pad_rows(x[80 + r * NBP : 80 + (r + 1) * NBP], 32).astype(BF)
        right.append(jnp.concatenate([h, h, l], axis=0))
    points = dot(fpw[...], jnp.concatenate(right, axis=1))
    values = []
    for r in range(3):
        cols = slice(r * count, (r + 1) * count)
        v = points[0:NP, cols]
        for g in range(1, 4):
            v = jnp.where(face == g, points[g * NP : (g + 1) * NP, cols], v)
        values.append(v)
    return values


SLOT_SHAPES = ((4, NP, NB), (160, E_DEV), *[(1, SLOTS)] * 5, (1, NP, SLOTS), (1, NP, SLOTS))
SLOT_TYPES = (F32, BF, *[jnp.int32] * 5, F32, F32)


def slot_kernel(*refs):
    count = len(SLOT_SHAPES)
    sources, (out_to, keep_to, mat, fpw, out, keep) = refs[:count], refs[count : count + 6]
    held, sems = refs[count + 6 : -1], refs[-1]
    fetch = fetches(sources, held, sems)
    proj, fhl, fse, fsf, fme, fmf, live, load, state = held
    fetch[0].wait()
    fpw[...] = left3(mat, [(0, g * NP, proj[g].T) for g in range(4)], 32, 64)
    for copy in fetch[1:]:
        copy.wait()

    def place(tile, x):
        out[pl.ds(tile, DEVICES, stride=TILES), :] = to_blocks(x)

    def place_points(n, x):
        for g in range(2):
            place(2 * n + g, x[8 * g : 8 * g + 8])

    place(12, jnp.broadcast_to(live[...].astype(F32), (8, SLOTS)))
    place_points(4, load[0])
    place_points(5, state[0])
    values = fault_values(
        fhl, fpw, jnp.concatenate([fse[...], fme[...]], axis=1), jnp.concatenate([fsf[...], fmf[...]], axis=1)
    )
    plus, minus = [v[:, 0:SLOTS] for v in values], [v[:, SLOTS : 2 * SLOTS] for v in values]
    for n, x in enumerate((plus[1] + plus[2], plus[0], minus[1] - minus[2], minus[0])):
        place_points(n, x)
    for n, x in enumerate((plus[1], minus[1])):
        for g in range(2):
            at = (2 * n + g) * LANES
            keep[:, at : at + LANES] = to_blocks(x[8 * g : 8 * g + 8])
    writes = fetches((out, keep), (out_to, keep_to), sems)
    for copy in writes:
        copy.wait()


def element_kernel(
    integ, dofs, star, couple, omega, fminus, fplus, area, nelem, nface, ihl, rim0, rim1, rim2, rim3,
    kdiff, proj, lift, base, mat, kdw, fpw, ltw, plw, rhl, change,
):
    c = pl.program_id(0)

    def put_rim(k, fields):
        flat = jnp.concatenate([pad_rows(x, NBP) for x in fields], axis=0)
        hi, lo = split(pad_rows(flat, ROWS))
        rhl[0:ROWS, k * BND : (k + 1) * BND] = hi
        rhl[ROWS : 2 * ROWS, k * BND : (k + 1) * BND] = lo

    @pl.when(c == 0)
    def _():
        kdw[...] = left3(mat, [(d * NBP, 0, kdiff[d]) for d in range(3)], 80, 32)
        fpw[...] = left3(mat, [(0, g * NP, proj[g].T) for g in range(4)], 32, 64)
        ltw[...] = left3(mat, [(f * NP, 0, lift[f]) for f in range(4)], 64, 32)
        both = [
            lax.dot_general(
                proj[f], lift[f], (((0,), (0,)), ((), ())),
                precision=lax.Precision.HIGHEST, preferred_element_type=F32,
            )
            for f in range(4)
        ]
        plw[...] = left3(mat, [(0, f * NBP, both[f]) for f in range(4)], 32, 96)
        for k, first, second, axis in ((0, rim0, rim1, "strike"), (2, rim2, rim3, "depth")):
            at = lax.axis_index(axis)
            even = (at % 2 == 0).astype(F32)
            odd = 1.0 - even
            before = (at > 0).astype(F32)
            after = (at < lax.axis_size(axis) - 1).astype(F32)
            for side, one, two in ((k, odd * before, even * before), (k + 1, even * after, odd * after)):
                put_rim(side, [one * first[j] + two * second[j] for j in range(NE)])
    def spread(ref):
        return jnp.concatenate([ref[f : f + 1, :] for f in range(4)], axis=1)

    def gather():
        elem = spread(nelem)
        return dot(ihl[...], one_hot(elem, E_DEV)) + dot(rhl[...], one_hot(elem, 4 * BND, E_DEV))

    def project(got):
        right = []
        for j in range(NE):
            hi = pad_rows(got[j * NBP : (j + 1) * NBP], 32).astype(BF)
            lo = pad_rows(got[ROWS + j * NBP : ROWS + (j + 1) * NBP], 32).astype(BF)
            right.append(jnp.concatenate([hi, hi, lo], axis=0))
        return dot(fpw[...], jnp.concatenate(right, axis=1))

    def choose(points):
        face, scale = spread(nface), spread(area)
        out = []
        for j in range(NE):
            cols = slice(j * E_DEV, (j + 1) * E_DEV)
            v = points[0:NP, cols]
            for g in range(1, 4):
                v = jnp.where(face == g, points[g * NP : (g + 1) * NP, cols], v)
            v = v * scale
            out.append(jnp.concatenate([v[:, f * LANES : (f + 1) * LANES] for f in range(4)], axis=0))
        return out

    kd = kdw[...]
    got = gather()
    acc = stress_of(lambda j: integ[j], star, kd)
    folded = dot(plw[...], jnp.concatenate([stack3(pad_rows(integ[j], 32)) for j in range(NE)], axis=1))
    points = project(got)
    for q in range(6):
        old = [integ[NE + 6 * l + q] for l in range(MECH)]
        relax = couple[0, q : q + 1, :] * old[0]
        for l in range(1, MECH):
            relax = relax + couple[l, q : q + 1, :] * old[l]
        for l in range(MECH):
            change[NE + 6 * l + q] = omega[l : l + 1, :] * (acc[q] - old[l])
        change[q] = acc[q] - relax
    for q in range(6, NE):
        change[q] = acc[q]
    total = [None] * NE
    for j in range(NE):
        cols = slice(j * LANES, (j + 1) * LANES)
        w = area[0:1, :] * folded[0:NBP, cols]
        for f in range(1, 4):
            w = w + area[f : f + 1, :] * folded[f * NBP : (f + 1) * NBP, cols]
        for i in range(NE):
            t = fminus[i, j : j + 1, :] * w
            total[i] = t if j == 0 else total[i] + t
    for i in range(NE):
        change[i] += total[i]
    lifted = dot(ltw[...], jnp.concatenate([stack3(v) for v in choose(points)], axis=1))
    for i in range(NE):
        t = change[i]
        for j in range(NE):
            t = t + fplus[i, j : j + 1, :] * lifted[0:NBP, j * LANES : (j + 1) * LANES]
        change[i] = t
    base[...] = dofs[...] + jnp.transpose(change[:, 0:NB, :], (1, 0, 2))


def inverse_of(x):
    guess = pl.reciprocal(x, approx=True)
    return guess * (2.0 - x * guess)


def friction(trial, pressure, load, state):
    sigma = load * (1.0 + 0.5 * jnp.tanh(0.5 * pressure))
    half = AFRIC * sigma
    steep = half * state
    size = jnp.abs(trial)
    slip = size * inverse_of(ETA + steep)
    for turn in range(NEWTON - 1):
        scaled = state * slip
        square = 1.0 + scaled * scaled
        inverse = lax.rsqrt(square)
        resid = size - ETA * slip - half * jnp.log(scaled + square * inverse)
        slip = slip + resid * inverse_of(ETA + steep * inverse)
    slip = jnp.where(trial < 0.0, -slip, slip)
    return trial - ETA * slip, slip


FAULT_SHAPES = (
    (4, NP, NB), (1, SLOTS), (1, SLOTS), *[(DEVICES * TILES, LANES)] * 2, (DEVICES, 4 * LANES), *[(1, SLOTS)] * 3,
)
FAULT_TYPES = (F32, jnp.int32, jnp.int32, F32, F32, F32, *[jnp.int32] * 3)


def fault_kernel(
    base_in, *refs
):
    del base_in
    count = len(FAULT_SHAPES)
    sources, (base, mat, lfw, slab, spots) = refs[:count], refs[count : count + 5]
    held = refs[count + 5 : -1]
    sem = refs[-1].at[count]
    fetch = fetches(sources, held, refs[-1])
    lift, fme, fse, theirs, mine, keep, fmf, live, fsf = held
    window = base.at[:, 0:8, :]
    read_slab = pltpu.make_async_copy(window, slab, sem)
    read_slab.start()
    fetch[0].wait()
    lfw[...] = left3(mat, [(0, f * NBP, lift[f]) for f in range(4)], 16, 96)
    for n, elem in enumerate((fme, fse)):
        fetch[1 + n].wait()
        spots[n * SLOTS : (n + 1) * SLOTS, :] = one_hot_t(elem[...], E_DEV)
    for copy in fetch[3:]:
        copy.wait()

    def tile(ref, n):
        return ref[pl.ds(n, DEVICES, stride=TILES), :]

    def pair(ref, n):
        return jnp.concatenate([tile(ref, 2 * n), tile(ref, 2 * n + 1)], axis=1)

    def side(one, other, load, state, kept, sign, alive, face, rows):
        pull, slip = friction(0.5 * (pair(theirs, other[0]) + pair(mine, one[0])), pair(mine, one[1]) + pair(theirs, other[1]), load, state)
        right = []
        for t in (pull - kept, sign * slip):
            x = jnp.concatenate([to_slots(t[:, 0:LANES]), to_slots(t[:, LANES:256])], axis=0)
            right.append(stack3(x))
        added = dot(lfw[...], jnp.concatenate(right, axis=1))
        sums = []
        for k in range(2):
            at = slice(k * SLOTS, (k + 1) * SLOTS)
            y = added[0:NBP, at]
            for f in range(1, 4):
                y = jnp.where(face == f, added[f * NBP : (f + 1) * NBP, at], y)
            sums.append(y * alive)
        hi, lo = split(jnp.concatenate(sums, axis=0))
        return dot(jnp.concatenate([hi, lo], axis=0), spots[rows, :])

    minus = side(
        (2, 3), (0, 1), pair(mine, 4), pair(mine, 5), keep[:, 256:512], -0.5,
        live[...].astype(F32), fmf[...], slice(0, SLOTS),
    )
    far = to_slots(tile(theirs, 12))[0:1]
    plus = side(
        (0, 1), (2, 3), pair(theirs, 4), pair(theirs, 5), keep[:, 0:256], 0.5,
        far, fsf[...], slice(SLOTS, 2 * SLOTS),
    )
    both = minus + plus
    delta = both[0:48] + both[48:96]
    read_slab.wait()
    for b in range(NB):
        for k in range(2):
            row = slice(FAULT_ROWS[1 + k], FAULT_ROWS[1 + k] + 1)
            slab[b, row, :] = slab[b, row, :] + delta[k * NBP + b : k * NBP + b + 1, :]
    write = pltpu.make_async_copy(slab, window, sem)
    write.start()
    write.wait()


def whole(shape):
    return pl.BlockSpec(shape, lambda *i: (0,) * len(shape))


def lanes(*lead, width=LANES):
    return pl.BlockSpec(lead + (width,), lambda c: (0,) * len(lead) + (c,))


def wide(*lead):
    return lanes(*lead, width=WIDE)


def per_device(
    dofs, star, kdiff, couple, omega, flux_minus, flux_plus, area, face_proj, face_lift,
    nbr_elem, nbr_face, weight_class, send_rows, fault_send_elem, fault_send_face,
    fault_minus_elem, fault_minus_face, fault_live, normal_load, state,
):
    shape = jax.ShapeDtypeStruct
    wc = weight_class.reshape(1, E_DEV)
    dofs = jnp.transpose(dofs, (1, 0, 2))
    star = jnp.transpose(star, (1, 2, 0, 3))
    face_proj = jnp.transpose(face_proj, (0, 2, 1))
    rim = whole((NE, NB, BND))
    anywhere = pl.BlockSpec(memory_space=pl.ANY)
    params = pltpu.CompilerParams(vmem_limit_bytes=VMEM)
    small = pltpu.CompilerParams(vmem_limit_bytes=VMEM_SMALL)
    integ, ihl, fhl, s0, s1, s2, s3 = pl.pallas_call(
        predict_kernel,
        grid=(CHUNKS // PAIR,),
        in_specs=[
            wide(NB, NQ), wide(NE, NE, 3), wide(MECH, 6), wide(MECH), wide(1),
            whole((3, NB, NB)), whole((4, BND)),
        ],
        out_specs=[
            wide(NQ, NBP), whole((2 * ROWS, E_DEV)), whole((160, E_DEV)), rim, rim, rim, rim,
        ],
        out_shape=[
            shape((NQ, NBP, E_DEV), F32), shape((2 * ROWS, E_DEV), BF), shape((160, E_DEV), BF),
            *[pltpu.HBM((NE, NB, BND), F32)] * 4,
        ],
        scratch_shapes=[
            pltpu.VMEM((NQ, NBP, WIDE), F32), pltpu.VMEM((80, LANES), F32),
            pltpu.VMEM((32, 240), BF),
        ],
        compiler_params=params,
        name="predict",
    )(dofs, star, couple, omega, wc, kdiff, send_rows)
    out, keep = pl.pallas_call(
        slot_kernel,
        in_specs=[anywhere] * len(SLOT_SHAPES),
        out_specs=[anywhere] * 2,
        out_shape=[shape((DEVICES * TILES, LANES), F32), shape((DEVICES, 4 * LANES), F32)],
        scratch_shapes=[
            pltpu.VMEM((64, LANES), F32), pltpu.VMEM((64, 96), BF),
            pltpu.VMEM((DEVICES * TILES, LANES), F32), pltpu.VMEM((DEVICES, 4 * LANES), F32),
            *[pltpu.VMEM(n, t) for n, t in zip(SLOT_SHAPES, SLOT_TYPES)],
            pltpu.SemaphoreType.DMA((len(SLOT_SHAPES),)),
        ],
        compiler_params=small,
        name="slots",
    )(
        face_proj, fhl, fault_send_elem, fault_send_face, fault_minus_elem, fault_minus_face,
        fault_live, normal_load, state,
    )
    ns, nd = lax.axis_size("strike"), lax.axis_size("depth")

    def swap(x, axis, n, first):
        ends = [(i, (i + 1) % n) for i in range(first, n, 2)]
        return lax.ppermute(x, axis, ends + [(j, i) for i, j in ends])

    r0 = swap(s0, "strike", ns, 0)
    r1 = swap(s1, "strike", ns, 1)
    r2 = swap(s2, "depth", nd, 0)
    r3 = swap(s3, "depth", nd, 1)
    r0, r1, r2, r3, sent = lax.optimization_barrier((r0, r1, r2, r3, out))
    theirs = lax.all_to_all(
        sent.reshape(DEVICES, 1, TILES * LANES), ("strike", "depth"), split_axis=0, concat_axis=0, tiled=True
    ).reshape(DEVICES * TILES, LANES)
    base = pl.pallas_call(
        element_kernel,
        grid=(CHUNKS,),
        in_specs=[
            lanes(NQ, NBP), lanes(NB, NQ), lanes(NE, NE, 3), lanes(MECH, 6), lanes(MECH),
            lanes(NE, NE), lanes(NE, NE), lanes(4), lanes(4), lanes(4),
            whole((2 * ROWS, E_DEV)), rim, rim, rim, rim,
            whole((3, NB, NB)), whole((4, NP, NB)), whole((4, NP, NB)),
        ],
        out_specs=lanes(NB, NQ),
        out_shape=pltpu.HBM((NB, NQ, E_DEV), F32),
        scratch_shapes=[
            pltpu.VMEM((80, LANES), F32),
            pltpu.VMEM((32, 240), BF), pltpu.VMEM((64, 96), BF), pltpu.VMEM((32, 192), BF),
            pltpu.VMEM((96, 96), BF), pltpu.VMEM((2 * ROWS, 4 * BND), BF),
            pltpu.VMEM((NQ, NBP, LANES), F32),
        ],
        compiler_params=small,
        name="elements",
    )(
        integ, dofs, star, couple, omega, flux_minus, flux_plus, area, nbr_elem, nbr_face,
        ihl, r0, r1, r2, r3, kdiff, face_proj, face_lift,
    )
    result = pl.pallas_call(
        fault_kernel,
        in_specs=[anywhere] * (1 + len(FAULT_SHAPES)),
        out_specs=anywhere,
        out_shape=shape((NB, NQ, E_DEV), F32),
        input_output_aliases={0: 0},
        scratch_shapes=[
            pltpu.VMEM((64, LANES), F32), pltpu.VMEM((96, 48), BF),
            pltpu.VMEM((NB, 8, E_DEV), F32), pltpu.VMEM((2 * SLOTS, E_DEV), BF),
            *[pltpu.VMEM(n, t) for n, t in zip(FAULT_SHAPES, FAULT_TYPES)],
            pltpu.SemaphoreType.DMA((len(FAULT_SHAPES) + 1,)),
        ],
        compiler_params=small,
        name="fault",
    )(
        base, face_lift, fault_minus_elem, fault_send_elem, theirs, sent, keep, fault_minus_face,
        fault_live, fault_send_face,
    )
    return jnp.transpose(result, (1, 0, 2))


def solution(mesh):
    both = ("strike", "depth")
    split_1, split_2, split_3 = P(None, both), P(None, None, both), P(None, None, None, both)
    in_specs = (
        split_2, split_3, P(), split_2, split_1, split_2, split_2, split_1, P(), P(),
        split_1, split_1, P(both), split_1,
        *[P(both, None)] * 5, P(both, None, None), P(both, None, None),
    )
    return jax.shard_map(
        per_device, mesh=mesh, in_specs=in_specs, out_specs=split_2, check_vma=False
    )
```

```python
import jax
import jax.numpy as jnp
from jax import lax
from jax.experimental import pallas as pl
from jax.experimental.pallas import tpu as pltpu
from jax.sharding import PartitionSpec as P

NQ = 27
NE = 9
MECH = 3
NB = 20
NP = 16
ORDER = 4
NEWTON = 4
ETA = 1.0
AFRIC = 0.5
E_DEV = 512
BND = 128
SLOTS = 2048
DEVICES = 128
NBP = 24
LANES = 128
CHUNKS = E_DEV // LANES
PAIR = 2
WIDE = PAIR * LANES
ROWS = 224
TILES = 13
F32 = jnp.float32
BF = jnp.bfloat16
VMEM = 56 * 1024 * 1024
VMEM_SMALL = 56 * 1024 * 1024
FAULT_ROWS = (0, 3, 6)


def split(x):
    hi = x.astype(BF)
    return hi, (x - hi.astype(F32)).astype(BF)


def pad_rows(x, rows):
    extra = rows - x.shape[0]
    if extra == 0:
        return x
    return jnp.concatenate([x, jnp.zeros((extra,) + x.shape[1:], x.dtype)], axis=0)


def stack3(x):
    hi, lo = split(x)
    return jnp.concatenate([hi, hi, lo], axis=0)


def left3(scratch, parts, depth, rows):
    scratch[...] = jnp.zeros(scratch.shape, F32)
    for row, col, value in parts:
        scratch[row : row + value.shape[0], col : col + value.shape[1]] = value
    whole = scratch[0:depth, :]
    hi = whole.astype(BF).astype(F32)
    lo = whole - hi
    tall = jnp.concatenate([hi, lo, hi], axis=0)
    tall = pad_rows(tall, -(-tall.shape[0] // 128) * 128)
    return jnp.transpose(tall, (1, 0))[0:rows, 0 : 3 * depth].astype(BF)


def dot(a, b):
    return lax.dot_general(a, b, (((1,), (0,)), ((), ())), preferred_element_type=F32)


def dot_nt(a, b):
    return lax.dot_general(a, b, (((1,), (1,)), ((), ())), preferred_element_type=F32)


def one_hot(index, rows, base=0):
    row = lax.broadcasted_iota(jnp.int32, (rows, LANES), 0).astype(jnp.int16)
    index = jnp.broadcast_to(index - base, (16, index.shape[1])).astype(jnp.int16)
    out = []
    for t in range(index.shape[1] // LANES):
        here = jnp.concatenate([index[:, t * LANES : (t + 1) * LANES]] * (rows // 16), axis=0)
        out.append(jnp.where(row == here, jnp.ones((), BF), jnp.zeros((), BF)))
    return jnp.concatenate(out, axis=1)


def one_hot_t(index, columns):
    column = lax.broadcasted_iota(jnp.int32, (16, columns), 1).astype(jnp.int16)
    column = jnp.concatenate([column] * (LANES // 16), axis=0)
    out = []
    for t in range(index.shape[1] // LANES):
        here = jnp.broadcast_to(index[:, t * LANES : (t + 1) * LANES], (LANES, LANES))
        here = jnp.transpose(here, (1, 0)).astype(jnp.int16)
        here = jnp.concatenate([here] * (columns // LANES), axis=1)
        out.append(jnp.where(column == here, jnp.ones((), BF), jnp.zeros((), BF)))
    return jnp.concatenate(out, axis=0)


def fetches(sources, held, sems):
    copies = [
        pltpu.make_async_copy(source, place, sems.at[n])
        for n, (source, place) in enumerate(zip(sources, held))
    ]
    for copy in copies:
        copy.start()
    return copies


def swap_blocks(x):
    x = pltpu.roll(x, 0, 1, stride=16, stride_axis=0)
    lane = lax.broadcasted_iota(jnp.int32, (8, LANES), 1)
    sub = lax.broadcasted_iota(jnp.int32, (8, LANES), 0)
    down = jnp.bitwise_and(lane // 16 - sub, 7)
    across = jnp.bitwise_and(lane + 16 * sub, LANES - 1)
    tiles = []
    for t in range(x.shape[0] // 8):
        y = jnp.take_along_axis(x[8 * t : 8 * t + 8], down, axis=0, mode="promise_in_bounds")
        tiles.append(jnp.take_along_axis(y, across, axis=1, mode="promise_in_bounds"))
    return jnp.concatenate(tiles, axis=0)


def to_blocks(x):
    return swap_blocks(
        jnp.concatenate([x[:, t * LANES : (t + 1) * LANES] for t in range(SLOTS // LANES)], axis=0)
    )


def to_slots(x):
    x = swap_blocks(x)
    return jnp.concatenate([x[8 * t : 8 * t + 8] for t in range(SLOTS // LANES)], axis=1)


def stress_of(get, star_ref, kd, rows=range(NE)):
    fields = [get(j) for j in range(NE)]
    out = []
    for i in rows:
        mixed = []
        for d in range(3):
            t = star_ref[i, 0, d : d + 1, :] * fields[0]
            for j in range(1, NE):
                t = t + star_ref[i, j, d : d + 1, :] * fields[j]
            mixed.append(t)
        out.append(dot(kd, stack3(pad_rows(jnp.concatenate(mixed, axis=0), 80)))[0:NBP])
    return out


def predict_kernel(
    dofs, star, couple, omega, wc, kdiff, srow,
    integ, ihl, fhl, send0, send1, send2, send3,
    term, mat, kdw,
):
    c = pl.program_id(0)

    @pl.when(c == 0)
    def _():
        kdw[...] = left3(mat, [(d * NBP, 0, kdiff[d]) for d in range(3)], 80, 32)
        term[...] = jnp.zeros(term.shape, F32)

    kd = kdw[...]
    step = 1.0 / (1.0 + wc[...].astype(F32))
    term[:, 0:NB, :] = jnp.transpose(dofs[...], (1, 0, 2))
    for q in range(NQ):
        integ[q] = step * term[q]

    def derive(cols, power):
        acc = stress_of(lambda j: term[j, :, cols], star.at[:, :, :, cols], kd)
        for q in range(6):
            old = [term[NE + 6 * l + q, :, cols] for l in range(MECH)]
            relax = couple[0, q : q + 1, cols] * old[0]
            for l in range(1, MECH):
                relax = relax + couple[l, q : q + 1, cols] * old[l]
            new = acc[q] - relax
            term[q, :, cols] = new
            integ[q, :, cols] += power * new
            for l in range(MECH):
                new = omega[l : l + 1, cols] * (acc[q] - old[l])
                term[NE + 6 * l + q, :, cols] = new
                integ[NE + 6 * l + q, :, cols] += power * new
        for q in range(6, NE):
            term[q, :, cols] = acc[q]
            integ[q, :, cols] += power * acc[q]

    def turn(order, power):
        power = power * step / (order + 2).astype(F32)
        for half in range(PAIR):
            cols = slice(half * LANES, (half + 1) * LANES)
            derive(cols, power[:, cols])
        return power

    lax.fori_loop(0, ORDER - 1, turn, step)

    here = pl.ds(pl.multiple_of(c * WIDE, WIDE), WIDE)
    flat = pad_rows(integ[0:NE].reshape(NE * NBP, WIDE), ROWS)
    hi, lo = split(flat)
    ihl[0:ROWS, here] = hi
    ihl[ROWS : 2 * ROWS, here] = lo
    hi, lo = split(pad_rows(jnp.concatenate([integ[r] for r in FAULT_ROWS], axis=0), 80))
    fhl[0:80, here] = hi
    fhl[80:160, here] = lo

    @pl.when(c == CHUNKS // PAIR - 1)
    def _():
        rows = []
        for axis, k in (("strike", 0), ("depth", 2)):
            even = lax.axis_index(axis) % 2 == 0
            ahead, behind = srow[k : k + 1, :], srow[k + 1 : k + 2, :]
            rows += [jnp.where(even, ahead, behind), jnp.where(even, behind, ahead)]
        rows = jnp.concatenate(rows, axis=1)
        got = dot(ihl[...], one_hot(rows, E_DEV))
        got = got[0:ROWS] + got[ROWS : 2 * ROWS]
        for k, ref in enumerate((send0, send1, send2, send3)):
            for j in range(NE):
                ref[j] = got[j * NBP : j * NBP + NB, k * BND : (k + 1) * BND]


def fault_values(fhl, fpw, elem, face):
    count = elem.shape[1]
    x = dot(fhl[...], one_hot(elem, E_DEV))
    right = []
    for r in range(3):
        h = pad_rows(x[r * NBP : (r + 1) * NBP], 32).astype(BF)
        l = pad_rows(x[80 + r * NBP : 80 + (r + 1) * NBP], 32).astype(BF)
        right.append(jnp.concatenate([h, h, l], axis=0))
    points = dot(fpw[...], jnp.concatenate(right, axis=1))
    values = []
    for r in range(3):
        cols = slice(r * count, (r + 1) * count)
        v = points[0:NP, cols]
        for g in range(1, 4):
            v = jnp.where(face == g, points[g * NP : (g + 1) * NP, cols], v)
        values.append(v)
    return values


SLOT_SHAPES = ((4, NP, NB), (160, E_DEV), *[(1, SLOTS)] * 5, (1, NP, SLOTS), (1, NP, SLOTS))
SLOT_TYPES = (F32, BF, *[jnp.int32] * 5, F32, F32)


def slot_kernel(*refs):
    count = len(SLOT_SHAPES)
    sources, (out_to, keep_to, mat, fpw, out, keep) = refs[:count], refs[count : count + 6]
    held, sems = refs[count + 6 : -1], refs[-1]
    fetch = fetches(sources, held, sems)
    proj, fhl, fse, fsf, fme, fmf, live, load, state = held
    fetch[0].wait()
    fpw[...] = left3(mat, [(0, g * NP, proj[g].T) for g in range(4)], 32, 64)
    for copy in fetch[1:]:
        copy.wait()

    def place(tile, x):
        out[pl.ds(tile, DEVICES, stride=TILES), :] = to_blocks(x)

    def place_points(n, x):
        for g in range(2):
            place(2 * n + g, x[8 * g : 8 * g + 8])

    place(12, jnp.broadcast_to(live[...].astype(F32), (8, SLOTS)))
    place_points(4, load[0])
    place_points(5, state[0])
    values = fault_values(
        fhl, fpw, jnp.concatenate([fse[...], fme[...]], axis=1), jnp.concatenate([fsf[...], fmf[...]], axis=1)
    )
    plus, minus = [v[:, 0:SLOTS] for v in values], [v[:, SLOTS : 2 * SLOTS] for v in values]
    for n, x in enumerate((plus[1] + plus[2], plus[0], minus[1] - minus[2], minus[0])):
        place_points(n, x)
    for n, x in enumerate((plus[1], minus[1])):
        for g in range(2):
            at = (2 * n + g) * LANES
            keep[:, at : at + LANES] = to_blocks(x[8 * g : 8 * g + 8])
    writes = fetches((out, keep), (out_to, keep_to), sems)
    for copy in writes:
        copy.wait()


def element_kernel(
    integ, dofs, star, couple, omega, fminus, fplus, area, nelem, nface, ihl, rim0, rim1, rim2, rim3,
    kdiff, proj, lift, base, mat, kdw, fpw, ltw, plw, rhl, change,
):
    c = pl.program_id(0)

    def put_rim(k, fields):
        flat = jnp.concatenate([pad_rows(x, NBP) for x in fields], axis=0)
        hi, lo = split(pad_rows(flat, ROWS))
        rhl[0:ROWS, k * BND : (k + 1) * BND] = hi
        rhl[ROWS : 2 * ROWS, k * BND : (k + 1) * BND] = lo

    @pl.when(c == 0)
    def _():
        kdw[...] = left3(mat, [(d * NBP, 0, kdiff[d]) for d in range(3)], 80, 32)
        fpw[...] = left3(mat, [(0, g * NP, proj[g].T) for g in range(4)], 32, 64)
        ltw[...] = left3(mat, [(f * NP, 0, lift[f]) for f in range(4)], 64, 32)
        both = [
            lax.dot_general(
                proj[f], lift[f], (((0,), (0,)), ((), ())),
                precision=lax.Precision.HIGHEST, preferred_element_type=F32,
            )
            for f in range(4)
        ]
        plw[...] = left3(mat, [(0, f * NBP, both[f]) for f in range(4)], 32, 96)
        for k, first, second, axis in ((0, rim0, rim1, "strike"), (2, rim2, rim3, "depth")):
            at = lax.axis_index(axis)
            even = (at % 2 == 0).astype(F32)
            odd = 1.0 - even
            before = (at > 0).astype(F32)
            after = (at < lax.axis_size(axis) - 1).astype(F32)
            for side, one, two in ((k, odd * before, even * before), (k + 1, even * after, odd * after)):
                put_rim(side, [one * first[j] + two * second[j] for j in range(NE)])
    def spread(ref):
        return jnp.concatenate([ref[f : f + 1, :] for f in range(4)], axis=1)

    def gather():
        elem = spread(nelem)
        return dot(ihl[...], one_hot(elem, E_DEV)) + dot(rhl[...], one_hot(elem, 4 * BND, E_DEV))

    def project(got):
        right = []
        for j in range(NE):
            hi = pad_rows(got[j * NBP : (j + 1) * NBP], 32).astype(BF)
            lo = pad_rows(got[ROWS + j * NBP : ROWS + (j + 1) * NBP], 32).astype(BF)
            right.append(jnp.concatenate([hi, hi, lo], axis=0))
        return dot(fpw[...], jnp.concatenate(right, axis=1))

    def choose(points):
        face, scale = spread(nface), spread(area)
        out = []
        for j in range(NE):
            cols = slice(j * E_DEV, (j + 1) * E_DEV)
            v = points[0:NP, cols]
            for g in range(1, 4):
                v = jnp.where(face == g, points[g * NP : (g + 1) * NP, cols], v)
            v = v * scale
            out.append(jnp.concatenate([v[:, f * LANES : (f + 1) * LANES] for f in range(4)], axis=0))
        return out

    kd = kdw[...]
    got = gather()
    acc = stress_of(lambda j: integ[j], star, kd)
    folded = dot(plw[...], jnp.concatenate([stack3(pad_rows(integ[j], 32)) for j in range(NE)], axis=1))
    points = project(got)
    for q in range(6):
        old = [integ[NE + 6 * l + q] for l in range(MECH)]
        relax = couple[0, q : q + 1, :] * old[0]
        for l in range(1, MECH):
            relax = relax + couple[l, q : q + 1, :] * old[l]
        for l in range(MECH):
            change[NE + 6 * l + q] = omega[l : l + 1, :] * (acc[q] - old[l])
        change[q] = acc[q] - relax
    for q in range(6, NE):
        change[q] = acc[q]
    total = [None] * NE
    for j in range(NE):
        cols = slice(j * LANES, (j + 1) * LANES)
        w = area[0:1, :] * folded[0:NBP, cols]
        for f in range(1, 4):
            w = w + area[f : f + 1, :] * folded[f * NBP : (f + 1) * NBP, cols]
        for i in range(NE):
            t = fminus[i, j : j + 1, :] * w
            total[i] = t if j == 0 else total[i] + t
    for i in range(NE):
        change[i] += total[i]
    lifted = dot(ltw[...], jnp.concatenate([stack3(v) for v in choose(points)], axis=1))
    for i in range(NE):
        t = change[i]
        for j in range(NE):
            t = t + fplus[i, j : j + 1, :] * lifted[0:NBP, j * LANES : (j + 1) * LANES]
        change[i] = t
    base[...] = dofs[...] + jnp.transpose(change[:, 0:NB, :], (1, 0, 2))


def inverse_of(x):
    guess = pl.reciprocal(x, approx=True)
    return guess * (2.0 - x * guess)


def friction(trial, pressure, load, state):
    sigma = load * (1.0 + 0.5 * jnp.tanh(0.5 * pressure))
    half = AFRIC * sigma
    steep = half * state
    size = jnp.abs(trial)
    slip = size * inverse_of(ETA + steep)
    for turn in range(NEWTON - 1):
        scaled = state * slip
        square = 1.0 + scaled * scaled
        inverse = lax.rsqrt(square)
        resid = size - ETA * slip - half * jnp.log(scaled + square * inverse)
        slip = slip + resid * inverse_of(ETA + steep * inverse)
    slip = jnp.where(trial < 0.0, -slip, slip)
    return trial - ETA * slip, slip


FAULT_SHAPES = (
    (4, NP, NB), (1, SLOTS), (1, SLOTS), (DEVICES * TILES, LANES), (DEVICES, 4 * LANES), *[(1, SLOTS)] * 3,
)
FAULT_TYPES = (F32, jnp.int32, jnp.int32, F32, F32, *[jnp.int32] * 3)


def fault_kernel(
    base_in, theirs, *refs
):
    del base_in
    count = len(FAULT_SHAPES)
    sources, (base, mat, lfw, slab, spots) = refs[:count], refs[count : count + 5]
    held = refs[count + 5 : -1]
    sem = refs[-1].at[count]
    fetch = fetches(sources, held, refs[-1])
    lift, fme, fse, mine, keep, fmf, live, fsf = held
    window = base.at[:, 0:8, :]
    read_slab = pltpu.make_async_copy(window, slab, sem)
    read_slab.start()
    fetch[0].wait()
    lfw[...] = left3(mat, [(0, f * NBP, lift[f]) for f in range(4)], 16, 96)
    for n, elem in enumerate((fme, fse)):
        fetch[1 + n].wait()
        spots[n * SLOTS : (n + 1) * SLOTS, :] = one_hot_t(elem[...], E_DEV)
    for copy in fetch[3:]:
        copy.wait()

    def tile(ref, n):
        return ref[pl.ds(n, DEVICES, stride=TILES), :]

    def pair(ref, n):
        return jnp.concatenate([tile(ref, 2 * n), tile(ref, 2 * n + 1)], axis=1)

    def side(one, other, load, state, kept, sign, alive, face, rows):
        pull, slip = friction(0.5 * (pair(theirs, other[0]) + pair(mine, one[0])), pair(mine, one[1]) + pair(theirs, other[1]), load, state)
        right = []
        for t in (pull - kept, sign * slip):
            x = jnp.concatenate([to_slots(t[:, 0:LANES]), to_slots(t[:, LANES:256])], axis=0)
            right.append(stack3(x))
        added = dot(lfw[...], jnp.concatenate(right, axis=1))
        sums = []
        for k in range(2):
            at = slice(k * SLOTS, (k + 1) * SLOTS)
            y = added[0:NBP, at]
            for f in range(1, 4):
                y = jnp.where(face == f, added[f * NBP : (f + 1) * NBP, at], y)
            sums.append(y * alive)
        hi, lo = split(jnp.concatenate(sums, axis=0))
        return dot(jnp.concatenate([hi, lo], axis=0), spots[rows, :])

    minus = side(
        (2, 3), (0, 1), pair(mine, 4), pair(mine, 5), keep[:, 256:512], -0.5,
        live[...].astype(F32), fmf[...], slice(0, SLOTS),
    )
    far = to_slots(tile(theirs, 12))[0:1]
    plus = side(
        (0, 1), (2, 3), pair(theirs, 4), pair(theirs, 5), keep[:, 0:256], 0.5,
        far, fsf[...], slice(SLOTS, 2 * SLOTS),
    )
    both = minus + plus
    delta = both[0:48] + both[48:96]
    read_slab.wait()
    for b in range(NB):
        for k in range(2):
            row = slice(FAULT_ROWS[1 + k], FAULT_ROWS[1 + k] + 1)
            slab[b, row, :] = slab[b, row, :] + delta[k * NBP + b : k * NBP + b + 1, :]
    write = pltpu.make_async_copy(slab, window, sem)
    write.start()
    write.wait()


def whole(shape):
    return pl.BlockSpec(shape, lambda *i: (0,) * len(shape))


def lanes(*lead, width=LANES):
    return pl.BlockSpec(lead + (width,), lambda c: (0,) * len(lead) + (c,))


def wide(*lead):
    return lanes(*lead, width=WIDE)


def per_device(
    dofs, star, kdiff, couple, omega, flux_minus, flux_plus, area, face_proj, face_lift,
    nbr_elem, nbr_face, weight_class, send_rows, fault_send_elem, fault_send_face,
    fault_minus_elem, fault_minus_face, fault_live, normal_load, state,
):
    shape = jax.ShapeDtypeStruct
    wc = weight_class.reshape(1, E_DEV)
    dofs = jnp.transpose(dofs, (1, 0, 2))
    star = jnp.transpose(star, (1, 2, 0, 3))
    face_proj = jnp.transpose(face_proj, (0, 2, 1))
    rim = whole((NE, NB, BND))
    anywhere = pl.BlockSpec(memory_space=pl.ANY)
    params = pltpu.CompilerParams(vmem_limit_bytes=VMEM)
    small = pltpu.CompilerParams(vmem_limit_bytes=VMEM_SMALL)
    integ, ihl, fhl, s0, s1, s2, s3 = pl.pallas_call(
        predict_kernel,
        grid=(CHUNKS // PAIR,),
        in_specs=[
            wide(NB, NQ), wide(NE, NE, 3), wide(MECH, 6), wide(MECH), wide(1),
            whole((3, NB, NB)), whole((4, BND)),
        ],
        out_specs=[
            wide(NQ, NBP), whole((2 * ROWS, E_DEV)), whole((160, E_DEV)), rim, rim, rim, rim,
        ],
        out_shape=[
            shape((NQ, NBP, E_DEV), F32), shape((2 * ROWS, E_DEV), BF), shape((160, E_DEV), BF),
            *[pltpu.HBM((NE, NB, BND), F32)] * 4,
        ],
        scratch_shapes=[
            pltpu.VMEM((NQ, NBP, WIDE), F32), pltpu.VMEM((80, LANES), F32),
            pltpu.VMEM((32, 240), BF),
        ],
        compiler_params=params,
        name="predict",
    )(dofs, star, couple, omega, wc, kdiff, send_rows)
    out, keep = pl.pallas_call(
        slot_kernel,
        in_specs=[anywhere] * len(SLOT_SHAPES),
        out_specs=[anywhere] * 2,
        out_shape=[shape((DEVICES * TILES, LANES), F32), shape((DEVICES, 4 * LANES), F32)],
        scratch_shapes=[
            pltpu.VMEM((64, LANES), F32), pltpu.VMEM((64, 96), BF),
            pltpu.VMEM((DEVICES * TILES, LANES), F32), pltpu.VMEM((DEVICES, 4 * LANES), F32),
            *[pltpu.VMEM(n, t) for n, t in zip(SLOT_SHAPES, SLOT_TYPES)],
            pltpu.SemaphoreType.DMA((len(SLOT_SHAPES),)),
        ],
        compiler_params=small,
        name="slots",
    )(
        face_proj, fhl, fault_send_elem, fault_send_face, fault_minus_elem, fault_minus_face,
        fault_live, normal_load, state,
    )
    ns, nd = lax.axis_size("strike"), lax.axis_size("depth")

    def swap(x, axis, n, first):
        ends = [(i, (i + 1) % n) for i in range(first, n, 2)]
        return lax.ppermute(x, axis, ends + [(j, i) for i, j in ends])

    r0 = swap(s0, "strike", ns, 0)
    r1 = swap(s1, "strike", ns, 1)
    r2 = swap(s2, "depth", nd, 0)
    r3 = swap(s3, "depth", nd, 1)
    r0, r1, r2, r3, sent = lax.optimization_barrier((r0, r1, r2, r3, out))
    theirs = lax.all_to_all(
        sent.reshape(DEVICES, 1, TILES * LANES), ("strike", "depth"), split_axis=0, concat_axis=0, tiled=True
    ).reshape(DEVICES * TILES, LANES)
    base = pl.pallas_call(
        element_kernel,
        grid=(CHUNKS,),
        in_specs=[
            lanes(NQ, NBP), lanes(NB, NQ), lanes(NE, NE, 3), lanes(MECH, 6), lanes(MECH),
            lanes(NE, NE), lanes(NE, NE), lanes(4), lanes(4), lanes(4),
            whole((2 * ROWS, E_DEV)), rim, rim, rim, rim,
            whole((3, NB, NB)), whole((4, NP, NB)), whole((4, NP, NB)),
        ],
        out_specs=lanes(NB, NQ),
        out_shape=pltpu.HBM((NB, NQ, E_DEV), F32),
        scratch_shapes=[
            pltpu.VMEM((80, LANES), F32),
            pltpu.VMEM((32, 240), BF), pltpu.VMEM((64, 96), BF), pltpu.VMEM((32, 192), BF),
            pltpu.VMEM((96, 96), BF), pltpu.VMEM((2 * ROWS, 4 * BND), BF),
            pltpu.VMEM((NQ, NBP, LANES), F32),
        ],
        compiler_params=small,
        name="elements",
    )(
        integ, dofs, star, couple, omega, flux_minus, flux_plus, area, nbr_elem, nbr_face,
        ihl, r0, r1, r2, r3, kdiff, face_proj, face_lift,
    )
    result = pl.pallas_call(
        fault_kernel,
        in_specs=[anywhere, pl.BlockSpec(memory_space=pltpu.VMEM)] + [anywhere] * len(FAULT_SHAPES),
        out_specs=anywhere,
        out_shape=shape((NB, NQ, E_DEV), F32),
        input_output_aliases={0: 0},
        scratch_shapes=[
            pltpu.VMEM((64, LANES), F32), pltpu.VMEM((96, 48), BF),
            pltpu.VMEM((NB, 8, E_DEV), F32), pltpu.VMEM((2 * SLOTS, E_DEV), BF),
            *[pltpu.VMEM(n, t) for n, t in zip(FAULT_SHAPES, FAULT_TYPES)],
            pltpu.SemaphoreType.DMA((len(FAULT_SHAPES) + 1,)),
        ],
        compiler_params=small,
        name="fault",
    )(
        base, theirs, face_lift, fault_minus_elem, fault_send_elem, sent, keep, fault_minus_face,
        fault_live, fault_send_face,
    )
    return jnp.transpose(result, (1, 0, 2))


def solution(mesh):
    both = ("strike", "depth")
    split_1, split_2, split_3 = P(None, both), P(None, None, both), P(None, None, None, both)
    in_specs = (
        split_2, split_3, P(), split_2, split_1, split_2, split_2, split_1, P(), P(),
        split_1, split_1, P(both), split_1,
        *[P(both, None)] * 5, P(both, None, None), P(both, None, None),
    )
    return jax.shard_map(
        per_device, mesh=mesh, in_specs=in_specs, out_specs=split_2, check_vma=False
    )
```

```python
import jax
import jax.numpy as jnp
from jax import lax
from jax.experimental import pallas as pl
from jax.experimental.pallas import tpu as pltpu
from jax.sharding import PartitionSpec as P

NQ = 27
NE = 9
MECH = 3
NB = 20
NP = 16
ORDER = 4
NEWTON = 4
ETA = 1.0
AFRIC = 0.5
E_DEV = 512
BND = 128
SLOTS = 2048
DEVICES = 128
NBP = 24
LANES = 128
CHUNKS = E_DEV // LANES
PAIR = 2
WIDE = PAIR * LANES
ROWS = 224
TILES = 13
F32 = jnp.float32
BF = jnp.bfloat16
VMEM = 56 * 1024 * 1024
VMEM_SMALL = 24 * 1024 * 1024
FAULT_ROWS = (0, 3, 6)


def split(x):
    hi = x.astype(BF)
    return hi, (x - hi.astype(F32)).astype(BF)


def pad_rows(x, rows):
    extra = rows - x.shape[0]
    if extra == 0:
        return x
    return jnp.concatenate([x, jnp.zeros((extra,) + x.shape[1:], x.dtype)], axis=0)


def stack3(x):
    hi, lo = split(x)
    return jnp.concatenate([hi, hi, lo], axis=0)


def left3(scratch, parts, depth, rows):
    scratch[...] = jnp.zeros(scratch.shape, F32)
    for row, col, value in parts:
        scratch[row : row + value.shape[0], col : col + value.shape[1]] = value
    whole = scratch[0:depth, :]
    hi = whole.astype(BF).astype(F32)
    lo = whole - hi
    tall = jnp.concatenate([hi, lo, hi], axis=0)
    tall = pad_rows(tall, -(-tall.shape[0] // 128) * 128)
    return jnp.transpose(tall, (1, 0))[0:rows, 0 : 3 * depth].astype(BF)


def dot(a, b):
    return lax.dot_general(a, b, (((1,), (0,)), ((), ())), preferred_element_type=F32)


def dot_nt(a, b):
    return lax.dot_general(a, b, (((1,), (1,)), ((), ())), preferred_element_type=F32)


def one_hot(index, rows, base=0):
    row = lax.broadcasted_iota(jnp.int32, (rows, LANES), 0).astype(jnp.int16)
    index = jnp.broadcast_to(index - base, (16, index.shape[1])).astype(jnp.int16)
    out = []
    for t in range(index.shape[1] // LANES):
        here = jnp.concatenate([index[:, t * LANES : (t + 1) * LANES]] * (rows // 16), axis=0)
        out.append(jnp.where(row == here, jnp.ones((), BF), jnp.zeros((), BF)))
    return jnp.concatenate(out, axis=1)


def one_hot_t(index, columns):
    column = lax.broadcasted_iota(jnp.int32, (16, columns), 1).astype(jnp.int16)
    column = jnp.concatenate([column] * (LANES // 16), axis=0)
    out = []
    for t in range(index.shape[1] // LANES):
        here = jnp.broadcast_to(index[:, t * LANES : (t + 1) * LANES], (LANES, LANES))
        here = jnp.transpose(here, (1, 0)).astype(jnp.int16)
        here = jnp.concatenate([here] * (columns // LANES), axis=1)
        out.append(jnp.where(column == here, jnp.ones((), BF), jnp.zeros((), BF)))
    return jnp.concatenate(out, axis=0)


def fetches(sources, held, sems):
    copies = [
        pltpu.make_async_copy(source, place, sems.at[n])
        for n, (source, place) in enumerate(zip(sources, held))
    ]
    for copy in copies:
        copy.start()
    return copies


def swap_blocks(x):
    x = pltpu.roll(x, 0, 1, stride=16, stride_axis=0)
    lane = lax.broadcasted_iota(jnp.int32, (8, LANES), 1)
    sub = lax.broadcasted_iota(jnp.int32, (8, LANES), 0)
    down = jnp.bitwise_and(lane // 16 - sub, 7)
    across = jnp.bitwise_and(lane + 16 * sub, LANES - 1)
    tiles = []
    for t in range(x.shape[0] // 8):
        y = jnp.take_along_axis(x[8 * t : 8 * t + 8], down, axis=0, mode="promise_in_bounds")
        tiles.append(jnp.take_along_axis(y, across, axis=1, mode="promise_in_bounds"))
    return jnp.concatenate(tiles, axis=0)


def to_blocks(x):
    return swap_blocks(
        jnp.concatenate([x[:, t * LANES : (t + 1) * LANES] for t in range(SLOTS // LANES)], axis=0)
    )


def to_slots(x):
    x = swap_blocks(x)
    return jnp.concatenate([x[8 * t : 8 * t + 8] for t in range(SLOTS // LANES)], axis=1)


def stress_of(get, star_ref, kd, rows=range(NE)):
    fields = [get(j) for j in range(NE)]
    out = []
    for i in rows:
        mixed = []
        for d in range(3):
            t = star_ref[i, 0, d : d + 1, :] * fields[0]
            for j in range(1, NE):
                t = t + star_ref[i, j, d : d + 1, :] * fields[j]
            mixed.append(t)
        out.append(dot(kd, stack3(pad_rows(jnp.concatenate(mixed, axis=0), 80)))[0:NBP])
    return out


def predict_kernel(
    dofs, star, couple, omega, wc, kdiff, srow,
    integ, ihl, fhl, send0, send1, send2, send3,
    term, mat, kdw,
):
    c = pl.program_id(0)

    @pl.when(c == 0)
    def _():
        kdw[...] = left3(mat, [(d * NBP, 0, kdiff[d]) for d in range(3)], 80, 32)
        term[...] = jnp.zeros(term.shape, F32)

    kd = kdw[...]
    step = 1.0 / (1.0 + wc[...].astype(F32))
    term[:, 0:NB, :] = jnp.transpose(dofs[...], (1, 0, 2))
    for q in range(NQ):
        integ[q] = step * term[q]

    def derive(cols, power):
        acc = stress_of(lambda j: term[j, :, cols], star.at[:, :, :, cols], kd)
        for q in range(6):
            old = [term[NE + 6 * l + q, :, cols] for l in range(MECH)]
            relax = couple[0, q : q + 1, cols] * old[0]
            for l in range(1, MECH):
                relax = relax + couple[l, q : q + 1, cols] * old[l]
            new = acc[q] - relax
            term[q, :, cols] = new
            integ[q, :, cols] += power * new
            for l in range(MECH):
                new = omega[l : l + 1, cols] * (acc[q] - old[l])
                term[NE + 6 * l + q, :, cols] = new
                integ[NE + 6 * l + q, :, cols] += power * new
        for q in range(6, NE):
            term[q, :, cols] = acc[q]
            integ[q, :, cols] += power * acc[q]

    def turn(order, power):
        power = power * step / (order + 2).astype(F32)
        for half in range(PAIR):
            cols = slice(half * LANES, (half + 1) * LANES)
            derive(cols, power[:, cols])
        return power

    lax.fori_loop(0, ORDER - 1, turn, step)

    here = pl.ds(pl.multiple_of(c * WIDE, WIDE), WIDE)
    flat = pad_rows(integ[0:NE].reshape(NE * NBP, WIDE), ROWS)
    hi, lo = split(flat)
    ihl[0:ROWS, here] = hi
    ihl[ROWS : 2 * ROWS, here] = lo
    hi, lo = split(pad_rows(jnp.concatenate([integ[r] for r in FAULT_ROWS], axis=0), 80))
    fhl[0:80, here] = hi
    fhl[80:160, here] = lo

    @pl.when(c == CHUNKS // PAIR - 1)
    def _():
        rows = []
        for axis, k in (("strike", 0), ("depth", 2)):
            even = lax.axis_index(axis) % 2 == 0
            ahead, behind = srow[k : k + 1, :], srow[k + 1 : k + 2, :]
            rows += [jnp.where(even, ahead, behind), jnp.where(even, behind, ahead)]
        rows = jnp.concatenate(rows, axis=1)
        got = dot(ihl[...], one_hot(rows, E_DEV))
        got = got[0:ROWS] + got[ROWS : 2 * ROWS]
        for k, ref in enumerate((send0, send1, send2, send3)):
            for j in range(NE):
                ref[j] = got[j * NBP : j * NBP + NB, k * BND : (k + 1) * BND]


def fault_values(fhl, fpw, elem, face):
    count = elem.shape[1]
    x = dot(fhl[...], one_hot(elem, E_DEV))
    right = []
    for r in range(3):
        h = pad_rows(x[r * NBP : (r + 1) * NBP], 32).astype(BF)
        l = pad_rows(x[80 + r * NBP : 80 + (r + 1) * NBP], 32).astype(BF)
        right.append(jnp.concatenate([h, h, l], axis=0))
    points = dot(fpw[...], jnp.concatenate(right, axis=1))
    values = []
    for r in range(3):
        cols = slice(r * count, (r + 1) * count)
        v = points[0:NP, cols]
        for g in range(1, 4):
            v = jnp.where(face == g, points[g * NP : (g + 1) * NP, cols], v)
        values.append(v)
    return values


SLOT_SHAPES = ((4, NP, NB), (160, E_DEV), *[(1, SLOTS)] * 5, (1, NP, SLOTS), (1, NP, SLOTS))
SLOT_TYPES = (F32, BF, *[jnp.int32] * 5, F32, F32)


def slot_kernel(*refs):
    count = len(SLOT_SHAPES)
    sources, (out_to, keep_to, mat, fpw, out, keep) = refs[:count], refs[count : count + 6]
    held, sems = refs[count + 6 : -1], refs[-1]
    fetch = fetches(sources, held, sems)
    proj, fhl, fse, fsf, fme, fmf, live, load, state = held
    fetch[0].wait()
    fpw[...] = left3(mat, [(0, g * NP, proj[g].T) for g in range(4)], 32, 64)
    for copy in fetch[1:]:
        copy.wait()

    def place(tile, x):
        out[pl.ds(tile, DEVICES, stride=TILES), :] = to_blocks(x)

    def place_points(n, x):
        for g in range(2):
            place(2 * n + g, x[8 * g : 8 * g + 8])

    place(12, jnp.broadcast_to(live[...].astype(F32), (8, SLOTS)))
    place_points(4, load[0])
    place_points(5, state[0])
    values = fault_values(
        fhl, fpw, jnp.concatenate([fse[...], fme[...]], axis=1), jnp.concatenate([fsf[...], fmf[...]], axis=1)
    )
    plus, minus = [v[:, 0:SLOTS] for v in values], [v[:, SLOTS : 2 * SLOTS] for v in values]
    for n, x in enumerate((plus[1] + plus[2], plus[0], minus[1] - minus[2], minus[0])):
        place_points(n, x)
    for n, x in enumerate((plus[1], minus[1])):
        for g in range(2):
            at = (2 * n + g) * LANES
            keep[:, at : at + LANES] = to_blocks(x[8 * g : 8 * g + 8])
    writes = fetches((out, keep), (out_to, keep_to), sems)
    for copy in writes:
        copy.wait()


def element_kernel(
    integ, dofs, star, couple, omega, fminus, fplus, area, nelem, nface, ihl, rim0, rim1, rim2, rim3,
    kdiff, proj, lift, base, mat, kdw, fpw, ltw, plw, rhl, change,
):
    c = pl.program_id(0)

    def put_rim(k, fields):
        flat = jnp.concatenate([pad_rows(x, NBP) for x in fields], axis=0)
        hi, lo = split(pad_rows(flat, ROWS))
        rhl[0:ROWS, k * BND : (k + 1) * BND] = hi
        rhl[ROWS : 2 * ROWS, k * BND : (k + 1) * BND] = lo

    @pl.when(c == 0)
    def _():
        kdw[...] = left3(mat, [(d * NBP, 0, kdiff[d]) for d in range(3)], 80, 32)
        fpw[...] = left3(mat, [(0, g * NP, proj[g].T) for g in range(4)], 32, 64)
        ltw[...] = left3(mat, [(f * NP, 0, lift[f]) for f in range(4)], 64, 32)
        both = [
            lax.dot_general(
                proj[f], lift[f], (((0,), (0,)), ((), ())),
                precision=lax.Precision.HIGHEST, preferred_element_type=F32,
            )
            for f in range(4)
        ]
        plw[...] = left3(mat, [(0, f * NBP, both[f]) for f in range(4)], 32, 96)
        for k, first, second, axis in ((0, rim0, rim1, "strike"), (2, rim2, rim3, "depth")):
            at = lax.axis_index(axis)
            even = (at % 2 == 0).astype(F32)
            odd = 1.0 - even
            before = (at > 0).astype(F32)
            after = (at < lax.axis_size(axis) - 1).astype(F32)
            for side, one, two in ((k, odd * before, even * before), (k + 1, even * after, odd * after)):
                put_rim(side, [one * first[j] + two * second[j] for j in range(NE)])
    def spread(ref):
        return jnp.concatenate([ref[f : f + 1, :] for f in range(4)], axis=1)

    def gather():
        elem = spread(nelem)
        return dot(ihl[...], one_hot(elem, E_DEV)) + dot(rhl[...], one_hot(elem, 4 * BND, E_DEV))

    def project(got):
        right = []
        for j in range(NE):
            hi = pad_rows(got[j * NBP : (j + 1) * NBP], 32).astype(BF)
            lo = pad_rows(got[ROWS + j * NBP : ROWS + (j + 1) * NBP], 32).astype(BF)
            right.append(jnp.concatenate([hi, hi, lo], axis=0))
        return dot(fpw[...], jnp.concatenate(right, axis=1))

    def choose(points):
        face, scale = spread(nface), spread(area)
        out = []
        for j in range(NE):
            cols = slice(j * E_DEV, (j + 1) * E_DEV)
            v = points[0:NP, cols]
            for g in range(1, 4):
                v = jnp.where(face == g, points[g * NP : (g + 1) * NP, cols], v)
            v = v * scale
            out.append(jnp.concatenate([v[:, f * LANES : (f + 1) * LANES] for f in range(4)], axis=0))
        return out

    kd = kdw[...]
    got = gather()
    acc = stress_of(lambda j: integ[j], star, kd)
    folded = dot(plw[...], jnp.concatenate([stack3(pad_rows(integ[j], 32)) for j in range(NE)], axis=1))
    points = project(got)
    for q in range(6):
        old = [integ[NE + 6 * l + q] for l in range(MECH)]
        relax = couple[0, q : q + 1, :] * old[0]
        for l in range(1, MECH):
            relax = relax + couple[l, q : q + 1, :] * old[l]
        for l in range(MECH):
            change[NE + 6 * l + q] = omega[l : l + 1, :] * (acc[q] - old[l])
        change[q] = acc[q] - relax
    for q in range(6, NE):
        change[q] = acc[q]
    total = [None] * NE
    for j in range(NE):
        cols = slice(j * LANES, (j + 1) * LANES)
        w = area[0:1, :] * folded[0:NBP, cols]
        for f in range(1, 4):
            w = w + area[f : f + 1, :] * folded[f * NBP : (f + 1) * NBP, cols]
        for i in range(NE):
            t = fminus[i, j : j + 1, :] * w
            total[i] = t if j == 0 else total[i] + t
    for i in range(NE):
        change[i] += total[i]
    lifted = dot(ltw[...], jnp.concatenate([stack3(v) for v in choose(points)], axis=1))
    for i in range(NE):
        t = change[i]
        for j in range(NE):
            t = t + fplus[i, j : j + 1, :] * lifted[0:NBP, j * LANES : (j + 1) * LANES]
        change[i] = t
    base[...] = dofs[...] + jnp.transpose(change[:, 0:NB, :], (1, 0, 2))


def inverse_of(x):
    guess = pl.reciprocal(x, approx=True)
    return guess * (2.0 - x * guess)


def friction(trial, pressure, load, state):
    sigma = load * (1.0 + 0.5 * jnp.tanh(0.5 * pressure))
    half = AFRIC * sigma
    steep = half * state
    size = jnp.abs(trial)
    slip = size * inverse_of(ETA + steep)
    for turn in range(NEWTON - 1):
        scaled = state * slip
        square = 1.0 + scaled * scaled
        inverse = lax.rsqrt(square)
        resid = size - ETA * slip - half * jnp.log(scaled + square * inverse)
        slip = slip + resid * inverse_of(ETA + steep * inverse)
    slip = jnp.where(trial < 0.0, -slip, slip)
    return trial - ETA * slip, slip


FAULT_SHAPES = (
    (4, NP, NB), (1, SLOTS), (1, SLOTS), (DEVICES * TILES, LANES), (DEVICES, 4 * LANES), *[(1, SLOTS)] * 3,
)
FAULT_TYPES = (F32, jnp.int32, jnp.int32, F32, F32, *[jnp.int32] * 3)


def fault_kernel(
    base_in, theirs, *refs
):
    del base_in
    count = len(FAULT_SHAPES)
    sources, (base, mat, lfw, slab, spots) = refs[:count], refs[count : count + 5]
    held = refs[count + 5 : -1]
    sem = refs[-1].at[count]
    fetch = fetches(sources, held, refs[-1])
    lift, fme, fse, mine, keep, fmf, live, fsf = held
    window = base.at[:, 0:8, :]
    read_slab = pltpu.make_async_copy(window, slab, sem)
    read_slab.start()
    fetch[0].wait()
    lfw[...] = left3(mat, [(0, f * NBP, lift[f]) for f in range(4)], 16, 96)
    for n, elem in enumerate((fme, fse)):
        fetch[1 + n].wait()
        spots[n * SLOTS : (n + 1) * SLOTS, :] = one_hot_t(elem[...], E_DEV)
    for copy in fetch[3:]:
        copy.wait()

    def tile(ref, n):
        return ref[pl.ds(n, DEVICES, stride=TILES), :]

    def pair(ref, n):
        return jnp.concatenate([tile(ref, 2 * n), tile(ref, 2 * n + 1)], axis=1)

    def side(one, other, load, state, kept, sign, alive, face, rows):
        pull, slip = friction(0.5 * (pair(theirs, other[0]) + pair(mine, one[0])), pair(mine, one[1]) + pair(theirs, other[1]), load, state)
        right = []
        for t in (pull - kept, sign * slip):
            x = jnp.concatenate([to_slots(t[:, 0:LANES]), to_slots(t[:, LANES:256])], axis=0)
            right.append(stack3(x))
        added = dot(lfw[...], jnp.concatenate(right, axis=1))
        sums = []
        for k in range(2):
            at = slice(k * SLOTS, (k + 1) * SLOTS)
            y = added[0:NBP, at]
            for f in range(1, 4):
                y = jnp.where(face == f, added[f * NBP : (f + 1) * NBP, at], y)
            sums.append(y * alive)
        hi, lo = split(jnp.concatenate(sums, axis=0))
        return dot(jnp.concatenate([hi, lo], axis=0), spots[rows, :])

    minus = side(
        (2, 3), (0, 1), pair(mine, 4), pair(mine, 5), keep[:, 256:512], -0.5,
        live[...].astype(F32), fmf[...], slice(0, SLOTS),
    )
    far = to_slots(tile(theirs, 12))[0:1]
    plus = side(
        (0, 1), (2, 3), pair(theirs, 4), pair(theirs, 5), keep[:, 0:256], 0.5,
        far, fsf[...], slice(SLOTS, 2 * SLOTS),
    )
    both = minus + plus
    delta = both[0:48] + both[48:96]
    read_slab.wait()
    for b in range(NB):
        for k in range(2):
            row = slice(FAULT_ROWS[1 + k], FAULT_ROWS[1 + k] + 1)
            slab[b, row, :] = slab[b, row, :] + delta[k * NBP + b : k * NBP + b + 1, :]
    write = pltpu.make_async_copy(slab, window, sem)
    write.start()
    write.wait()


def whole(shape):
    return pl.BlockSpec(shape, lambda *i: (0,) * len(shape))


def lanes(*lead, width=LANES):
    return pl.BlockSpec(lead + (width,), lambda c: (0,) * len(lead) + (c,))


def wide(*lead):
    return lanes(*lead, width=WIDE)


def per_device(
    dofs, star, kdiff, couple, omega, flux_minus, flux_plus, area, face_proj, face_lift,
    nbr_elem, nbr_face, weight_class, send_rows, fault_send_elem, fault_send_face,
    fault_minus_elem, fault_minus_face, fault_live, normal_load, state,
):
    shape = jax.ShapeDtypeStruct
    wc = weight_class.reshape(1, E_DEV)
    dofs = jnp.transpose(dofs, (1, 0, 2))
    star = jnp.transpose(star, (1, 2, 0, 3))
    face_proj = jnp.transpose(face_proj, (0, 2, 1))
    rim = whole((NE, NB, BND))
    anywhere = pl.BlockSpec(memory_space=pl.ANY)
    outside = pl.BlockSpec(memory_space=pltpu.HBM)
    params = pltpu.CompilerParams(vmem_limit_bytes=VMEM)
    small = pltpu.CompilerParams(vmem_limit_bytes=VMEM_SMALL)
    integ, ihl, fhl, s0, s1, s2, s3 = pl.pallas_call(
        predict_kernel,
        grid=(CHUNKS // PAIR,),
        in_specs=[
            wide(NB, NQ), wide(NE, NE, 3), wide(MECH, 6), wide(MECH), wide(1),
            whole((3, NB, NB)), whole((4, BND)),
        ],
        out_specs=[
            wide(NQ, NBP), whole((2 * ROWS, E_DEV)), whole((160, E_DEV)), rim, rim, rim, rim,
        ],
        out_shape=[
            shape((NQ, NBP, E_DEV), F32), shape((2 * ROWS, E_DEV), BF), shape((160, E_DEV), BF),
            *[pltpu.HBM((NE, NB, BND), F32)] * 4,
        ],
        scratch_shapes=[
            pltpu.VMEM((NQ, NBP, WIDE), F32), pltpu.VMEM((80, LANES), F32),
            pltpu.VMEM((32, 240), BF),
        ],
        compiler_params=params,
        name="predict",
    )(dofs, star, couple, omega, wc, kdiff, send_rows)
    out, keep = pl.pallas_call(
        slot_kernel,
        in_specs=[anywhere] * len(SLOT_SHAPES),
        out_specs=[anywhere] * 2,
        out_shape=[shape((DEVICES * TILES, LANES), F32), shape((DEVICES, 4 * LANES), F32)],
        scratch_shapes=[
            pltpu.VMEM((64, LANES), F32), pltpu.VMEM((64, 96), BF),
            pltpu.VMEM((DEVICES * TILES, LANES), F32), pltpu.VMEM((DEVICES, 4 * LANES), F32),
            *[pltpu.VMEM(n, t) for n, t in zip(SLOT_SHAPES, SLOT_TYPES)],
            pltpu.SemaphoreType.DMA((len(SLOT_SHAPES),)),
        ],
        compiler_params=params,
        name="slots",
    )(
        face_proj, fhl, fault_send_elem, fault_send_face, fault_minus_elem, fault_minus_face,
        fault_live, normal_load, state,
    )
    ns, nd = lax.axis_size("strike"), lax.axis_size("depth")

    def swap(x, axis, n, first):
        ends = [(i, (i + 1) % n) for i in range(first, n, 2)]
        return lax.ppermute(x, axis, ends + [(j, i) for i, j in ends])

    r0 = swap(s0, "strike", ns, 0)
    r1 = swap(s1, "strike", ns, 1)
    r2 = swap(s2, "depth", nd, 0)
    r3 = swap(s3, "depth", nd, 1)
    r0, r1, r2, r3, sent = lax.optimization_barrier((r0, r1, r2, r3, out))
    theirs = lax.all_to_all(
        sent.reshape(DEVICES, 1, TILES * LANES), ("strike", "depth"), split_axis=0, concat_axis=0, tiled=True
    ).reshape(DEVICES * TILES, LANES)
    base = pl.pallas_call(
        element_kernel,
        grid=(CHUNKS,),
        in_specs=[
            lanes(NQ, NBP), lanes(NB, NQ), lanes(NE, NE, 3), lanes(MECH, 6), lanes(MECH),
            lanes(NE, NE), lanes(NE, NE), lanes(4), lanes(4), lanes(4),
            whole((2 * ROWS, E_DEV)), rim, rim, rim, rim,
            whole((3, NB, NB)), whole((4, NP, NB)), whole((4, NP, NB)),
        ],
        out_specs=lanes(NB, NQ),
        out_shape=pltpu.HBM((NB, NQ, E_DEV), F32),
        scratch_shapes=[
            pltpu.VMEM((80, LANES), F32),
            pltpu.VMEM((32, 240), BF), pltpu.VMEM((64, 96), BF), pltpu.VMEM((32, 192), BF),
            pltpu.VMEM((96, 96), BF), pltpu.VMEM((2 * ROWS, 4 * BND), BF),
            pltpu.VMEM((NQ, NBP, LANES), F32),
        ],
        compiler_params=params,
        name="elements",
    )(
        integ, dofs, star, couple, omega, flux_minus, flux_plus, area, nbr_elem, nbr_face,
        ihl, r0, r1, r2, r3, kdiff, face_proj, face_lift,
    )
    result = pl.pallas_call(
        fault_kernel,
        in_specs=[outside, pl.BlockSpec(memory_space=pltpu.VMEM)] + [outside] * len(FAULT_SHAPES),
        out_specs=outside,
        out_shape=shape((NB, NQ, E_DEV), F32),
        input_output_aliases={0: 0},
        scratch_shapes=[
            pltpu.VMEM((64, LANES), F32), pltpu.VMEM((96, 48), BF),
            pltpu.VMEM((NB, 8, E_DEV), F32), pltpu.VMEM((2 * SLOTS, E_DEV), BF),
            *[pltpu.VMEM(n, t) for n, t in zip(FAULT_SHAPES, FAULT_TYPES)],
            pltpu.SemaphoreType.DMA((len(FAULT_SHAPES) + 1,)),
        ],
        compiler_params=small,
        name="fault",
    )(
        base, pltpu.with_memory_space_constraint(theirs, pltpu.VMEM),
        *[
            pltpu.with_memory_space_constraint(x, pltpu.HBM)
            for x in (
                face_lift, fault_minus_elem, fault_send_elem, sent, keep, fault_minus_face, fault_live,
                fault_send_face,
            )
        ],
    )
    return jnp.transpose(result, (1, 0, 2))


def solution(mesh):
    both = ("strike", "depth")
    split_1, split_2, split_3 = P(None, both), P(None, None, both), P(None, None, None, both)
    in_specs = (
        split_2, split_3, P(), split_2, split_1, split_2, split_2, split_1, P(), P(),
        split_1, split_1, P(both), split_1,
        *[P(both, None)] * 5, P(both, None, None), P(both, None, None),
    )
    return jax.shard_map(
        per_device, mesh=mesh, in_specs=in_specs, out_specs=split_2, check_vma=False
    )
```

```python
import jax
import jax.numpy as jnp
from jax import lax
from jax.experimental import pallas as pl
from jax.experimental.pallas import tpu as pltpu
from jax.sharding import PartitionSpec as P

NQ = 27
NE = 9
MECH = 3
NB = 20
NP = 16
ORDER = 4
NEWTON = 4
ETA = 1.0
AFRIC = 0.5
E_DEV = 512
BND = 128
SLOTS = 2048
DEVICES = 128
NBP = 24
LANES = 128
CHUNKS = E_DEV // LANES
PAIR = 2
WIDE = PAIR * LANES
ROWS = 224
TILES = 13
F32 = jnp.float32
BF = jnp.bfloat16
VMEM = 56 * 1024 * 1024
VMEM_SMALL = 24 * 1024 * 1024
FAULT_ROWS = (0, 3, 6)


def split(x):
    hi = x.astype(BF)
    return hi, (x - hi.astype(F32)).astype(BF)


def pad_rows(x, rows):
    extra = rows - x.shape[0]
    if extra == 0:
        return x
    return jnp.concatenate([x, jnp.zeros((extra,) + x.shape[1:], x.dtype)], axis=0)


def stack3(x):
    hi, lo = split(x)
    return jnp.concatenate([hi, hi, lo], axis=0)


def left3(scratch, parts, depth, rows):
    scratch[...] = jnp.zeros(scratch.shape, F32)
    for row, col, value in parts:
        scratch[row : row + value.shape[0], col : col + value.shape[1]] = value
    whole = scratch[0:depth, :]
    hi = whole.astype(BF).astype(F32)
    lo = whole - hi
    tall = jnp.concatenate([hi, lo, hi], axis=0)
    tall = pad_rows(tall, -(-tall.shape[0] // 128) * 128)
    return jnp.transpose(tall, (1, 0))[0:rows, 0 : 3 * depth].astype(BF)


def dot(a, b):
    return lax.dot_general(a, b, (((1,), (0,)), ((), ())), preferred_element_type=F32)


def dot_nt(a, b):
    return lax.dot_general(a, b, (((1,), (1,)), ((), ())), preferred_element_type=F32)


def one_hot(index, rows, base=0):
    row = lax.broadcasted_iota(jnp.int32, (rows, LANES), 0).astype(jnp.int16)
    index = jnp.broadcast_to(index - base, (16, index.shape[1])).astype(jnp.int16)
    out = []
    for t in range(index.shape[1] // LANES):
        here = jnp.concatenate([index[:, t * LANES : (t + 1) * LANES]] * (rows // 16), axis=0)
        out.append(jnp.where(row == here, jnp.ones((), BF), jnp.zeros((), BF)))
    return jnp.concatenate(out, axis=1)


def one_hot_t(index, columns):
    column = lax.broadcasted_iota(jnp.int32, (16, columns), 1).astype(jnp.int16)
    column = jnp.concatenate([column] * (LANES // 16), axis=0)
    out = []
    for t in range(index.shape[1] // LANES):
        here = jnp.broadcast_to(index[:, t * LANES : (t + 1) * LANES], (LANES, LANES))
        here = jnp.transpose(here, (1, 0)).astype(jnp.int16)
        here = jnp.concatenate([here] * (columns // LANES), axis=1)
        out.append(jnp.where(column == here, jnp.ones((), BF), jnp.zeros((), BF)))
    return jnp.concatenate(out, axis=0)


def fetches(sources, held, sems):
    copies = [
        pltpu.make_async_copy(source, place, sems.at[n])
        for n, (source, place) in enumerate(zip(sources, held))
    ]
    for copy in copies:
        copy.start()
    return copies


def swap_blocks(x):
    x = pltpu.roll(x, 0, 1, stride=16, stride_axis=0)
    lane = lax.broadcasted_iota(jnp.int32, (8, LANES), 1)
    sub = lax.broadcasted_iota(jnp.int32, (8, LANES), 0)
    down = jnp.bitwise_and(lane // 16 - sub, 7)
    across = jnp.bitwise_and(lane + 16 * sub, LANES - 1)
    tiles = []
    for t in range(x.shape[0] // 8):
        y = jnp.take_along_axis(x[8 * t : 8 * t + 8], down, axis=0, mode="promise_in_bounds")
        tiles.append(jnp.take_along_axis(y, across, axis=1, mode="promise_in_bounds"))
    return jnp.concatenate(tiles, axis=0)


def to_blocks(x):
    return swap_blocks(
        jnp.concatenate([x[:, t * LANES : (t + 1) * LANES] for t in range(SLOTS // LANES)], axis=0)
    )


def to_slots(x):
    x = swap_blocks(x)
    return jnp.concatenate([x[8 * t : 8 * t + 8] for t in range(SLOTS // LANES)], axis=1)


def stress_of(get, star_ref, kd, rows=range(NE)):
    fields = [get(j) for j in range(NE)]
    out = []
    for i in rows:
        mixed = []
        for d in range(3):
            t = star_ref[i, 0, d : d + 1, :] * fields[0]
            for j in range(1, NE):
                t = t + star_ref[i, j, d : d + 1, :] * fields[j]
            mixed.append(t)
        out.append(dot(kd, stack3(pad_rows(jnp.concatenate(mixed, axis=0), 80)))[0:NBP])
    return out


def predict_kernel(
    dofs, star, couple, omega, wc, kdiff, srow,
    integ, ihl, fhl, send0, send1, send2, send3,
    term, mat, kdw,
):
    c = pl.program_id(0)

    @pl.when(c == 0)
    def _():
        kdw[...] = left3(mat, [(d * NBP, 0, kdiff[d]) for d in range(3)], 80, 32)
        term[...] = jnp.zeros(term.shape, F32)

    kd = kdw[...]
    step = 1.0 / (1.0 + wc[...].astype(F32))
    term[:, 0:NB, :] = jnp.transpose(dofs[...], (1, 0, 2))
    for q in range(NQ):
        integ[q] = step * term[q]

    def derive(cols, power):
        acc = stress_of(lambda j: term[j, :, cols], star.at[:, :, :, cols], kd)
        for q in range(6):
            old = [term[NE + 6 * l + q, :, cols] for l in range(MECH)]
            relax = couple[0, q : q + 1, cols] * old[0]
            for l in range(1, MECH):
                relax = relax + couple[l, q : q + 1, cols] * old[l]
            new = acc[q] - relax
            term[q, :, cols] = new
            integ[q, :, cols] += power * new
            for l in range(MECH):
                new = omega[l : l + 1, cols] * (acc[q] - old[l])
                term[NE + 6 * l + q, :, cols] = new
                integ[NE + 6 * l + q, :, cols] += power * new
        for q in range(6, NE):
            term[q, :, cols] = acc[q]
            integ[q, :, cols] += power * acc[q]

    def turn(order, power):
        power = power * step / (order + 2).astype(F32)
        for half in range(PAIR):
            cols = slice(half * LANES, (half + 1) * LANES)
            derive(cols, power[:, cols])
        return power

    lax.fori_loop(0, ORDER - 1, turn, step)

    here = pl.ds(pl.multiple_of(c * WIDE, WIDE), WIDE)
    flat = pad_rows(integ[0:NE].reshape(NE * NBP, WIDE), ROWS)
    hi, lo = split(flat)
    ihl[0:ROWS, here] = hi
    ihl[ROWS : 2 * ROWS, here] = lo
    hi, lo = split(pad_rows(jnp.concatenate([integ[r] for r in FAULT_ROWS], axis=0), 80))
    fhl[0:80, here] = hi
    fhl[80:160, here] = lo

    @pl.when(c == CHUNKS // PAIR - 1)
    def _():
        rows = []
        for axis, k in (("strike", 0), ("depth", 2)):
            even = lax.axis_index(axis) % 2 == 0
            ahead, behind = srow[k : k + 1, :], srow[k + 1 : k + 2, :]
            rows += [jnp.where(even, ahead, behind), jnp.where(even, behind, ahead)]
        rows = jnp.concatenate(rows, axis=1)
        got = dot(ihl[...], one_hot(rows, E_DEV))
        got = got[0:ROWS] + got[ROWS : 2 * ROWS]
        for k, ref in enumerate((send0, send1, send2, send3)):
            for j in range(NE):
                ref[j] = got[j * NBP : j * NBP + NB, k * BND : (k + 1) * BND]


def fault_values(fhl, fpw, elem, face):
    count = elem.shape[1]
    x = dot(fhl[...], one_hot(elem, E_DEV))
    right = []
    for r in range(3):
        h = pad_rows(x[r * NBP : (r + 1) * NBP], 32).astype(BF)
        l = pad_rows(x[80 + r * NBP : 80 + (r + 1) * NBP], 32).astype(BF)
        right.append(jnp.concatenate([h, h, l], axis=0))
    points = dot(fpw[...], jnp.concatenate(right, axis=1))
    values = []
    for r in range(3):
        cols = slice(r * count, (r + 1) * count)
        v = points[0:NP, cols]
        for g in range(1, 4):
            v = jnp.where(face == g, points[g * NP : (g + 1) * NP, cols], v)
        values.append(v)
    return values


SLOT_SHAPES = ((4, NP, NB), (160, E_DEV), *[(1, SLOTS)] * 5, (1, NP, SLOTS), (1, NP, SLOTS))
SLOT_TYPES = (F32, BF, *[jnp.int32] * 5, F32, F32)


def slot_kernel(*refs):
    count = len(SLOT_SHAPES)
    sources, (out_to, keep_to, mat, fpw, out, keep) = refs[:count], refs[count : count + 6]
    held, sems = refs[count + 6 : -1], refs[-1]
    fetch = fetches(sources, held, sems)
    proj, fhl, fse, fsf, fme, fmf, live, load, state = held
    for copy in fetch:
        copy.wait()
    fpw[...] = left3(mat, [(0, g * NP, proj[g].T) for g in range(4)], 32, 64)

    def place(tile, x):
        out[pl.ds(tile, DEVICES, stride=TILES), :] = to_blocks(x)

    def place_points(n, x):
        for g in range(2):
            place(2 * n + g, x[8 * g : 8 * g + 8])

    place(12, jnp.broadcast_to(live[...].astype(F32), (8, SLOTS)))
    place_points(4, load[0])
    place_points(5, state[0])
    values = fault_values(
        fhl, fpw, jnp.concatenate([fse[...], fme[...]], axis=1), jnp.concatenate([fsf[...], fmf[...]], axis=1)
    )
    plus, minus = [v[:, 0:SLOTS] for v in values], [v[:, SLOTS : 2 * SLOTS] for v in values]
    for n, x in enumerate((plus[1] + plus[2], plus[0], minus[1] - minus[2], minus[0])):
        place_points(n, x)
    for n, x in enumerate((plus[1], minus[1])):
        for g in range(2):
            at = (2 * n + g) * LANES
            keep[:, at : at + LANES] = to_blocks(x[8 * g : 8 * g + 8])
    writes = fetches((out, keep), (out_to, keep_to), sems)
    for copy in writes:
        copy.wait()


def element_kernel(
    integ, dofs, star, couple, omega, fminus, fplus, area, nelem, nface, ihl, rim0, rim1, rim2, rim3,
    kdiff, proj, lift, base, mat, kdw, fpw, ltw, plw, rhl, change,
):
    c = pl.program_id(0)

    def put_rim(k, fields):
        flat = jnp.concatenate([pad_rows(x, NBP) for x in fields], axis=0)
        hi, lo = split(pad_rows(flat, ROWS))
        rhl[0:ROWS, k * BND : (k + 1) * BND] = hi
        rhl[ROWS : 2 * ROWS, k * BND : (k + 1) * BND] = lo

    @pl.when(c == 0)
    def _():
        kdw[...] = left3(mat, [(d * NBP, 0, kdiff[d]) for d in range(3)], 80, 32)
        fpw[...] = left3(mat, [(0, g * NP, proj[g].T) for g in range(4)], 32, 64)
        ltw[...] = left3(mat, [(f * NP, 0, lift[f]) for f in range(4)], 64, 32)
        both = [
            lax.dot_general(
                proj[f], lift[f], (((0,), (0,)), ((), ())),
                precision=lax.Precision.HIGHEST, preferred_element_type=F32,
            )
            for f in range(4)
        ]
        plw[...] = left3(mat, [(0, f * NBP, both[f]) for f in range(4)], 32, 96)
        for k, first, second, axis in ((0, rim0, rim1, "strike"), (2, rim2, rim3, "depth")):
            at = lax.axis_index(axis)
            even = (at % 2 == 0).astype(F32)
            odd = 1.0 - even
            before = (at > 0).astype(F32)
            after = (at < lax.axis_size(axis) - 1).astype(F32)
            for side, one, two in ((k, odd * before, even * before), (k + 1, even * after, odd * after)):
                put_rim(side, [one * first[j] + two * second[j] for j in range(NE)])
    def spread(ref):
        return jnp.concatenate([ref[f : f + 1, :] for f in range(4)], axis=1)

    def gather():
        elem = spread(nelem)
        return dot(ihl[...], one_hot(elem, E_DEV)) + dot(rhl[...], one_hot(elem, 4 * BND, E_DEV))

    def project(got):
        right = []
        for j in range(NE):
            hi = pad_rows(got[j * NBP : (j + 1) * NBP], 32).astype(BF)
            lo = pad_rows(got[ROWS + j * NBP : ROWS + (j + 1) * NBP], 32).astype(BF)
            right.append(jnp.concatenate([hi, hi, lo], axis=0))
        return dot(fpw[...], jnp.concatenate(right, axis=1))

    def choose(points):
        face, scale = spread(nface), spread(area)
        out = []
        for j in range(NE):
            cols = slice(j * E_DEV, (j + 1) * E_DEV)
            v = points[0:NP, cols]
            for g in range(1, 4):
                v = jnp.where(face == g, points[g * NP : (g + 1) * NP, cols], v)
            v = v * scale
            out.append(jnp.concatenate([v[:, f * LANES : (f + 1) * LANES] for f in range(4)], axis=0))
        return out

    kd = kdw[...]
    got = gather()
    acc = stress_of(lambda j: integ[j], star, kd)
    folded = dot(plw[...], jnp.concatenate([stack3(pad_rows(integ[j], 32)) for j in range(NE)], axis=1))
    points = project(got)
    for q in range(6):
        old = [integ[NE + 6 * l + q] for l in range(MECH)]
        relax = couple[0, q : q + 1, :] * old[0]
        for l in range(1, MECH):
            relax = relax + couple[l, q : q + 1, :] * old[l]
        for l in range(MECH):
            change[NE + 6 * l + q] = omega[l : l + 1, :] * (acc[q] - old[l])
        change[q] = acc[q] - relax
    for q in range(6, NE):
        change[q] = acc[q]
    total = [None] * NE
    for j in range(NE):
        cols = slice(j * LANES, (j + 1) * LANES)
        w = area[0:1, :] * folded[0:NBP, cols]
        for f in range(1, 4):
            w = w + area[f : f + 1, :] * folded[f * NBP : (f + 1) * NBP, cols]
        for i in range(NE):
            t = fminus[i, j : j + 1, :] * w
            total[i] = t if j == 0 else total[i] + t
    for i in range(NE):
        change[i] += total[i]
    lifted = dot(ltw[...], jnp.concatenate([stack3(v) for v in choose(points)], axis=1))
    for i in range(NE):
        t = change[i]
        for j in range(NE):
            t = t + fplus[i, j : j + 1, :] * lifted[0:NBP, j * LANES : (j + 1) * LANES]
        change[i] = t
    base[...] = dofs[...] + jnp.transpose(change[:, 0:NB, :], (1, 0, 2))


def inverse_of(x):
    guess = pl.reciprocal(x, approx=True)
    return guess * (2.0 - x * guess)


def friction(trial, pressure, load, state):
    sigma = load * (1.0 + 0.5 * jnp.tanh(0.5 * pressure))
    half = AFRIC * sigma
    steep = half * state
    size = jnp.abs(trial)
    slip = size * inverse_of(ETA + steep)
    for turn in range(NEWTON - 1):
        scaled = state * slip
        square = 1.0 + scaled * scaled
        inverse = lax.rsqrt(square)
        resid = size - ETA * slip - half * jnp.log(scaled + square * inverse)
        slip = slip + resid * inverse_of(ETA + steep * inverse)
    slip = jnp.where(trial < 0.0, -slip, slip)
    return trial - ETA * slip, slip


FAULT_SHAPES = (
    (4, NP, NB), (1, SLOTS), (1, SLOTS), (DEVICES * TILES, LANES), (DEVICES, 4 * LANES), *[(1, SLOTS)] * 3,
)
FAULT_TYPES = (F32, jnp.int32, jnp.int32, F32, F32, *[jnp.int32] * 3)


def fault_kernel(
    base_in, theirs, *refs
):
    del base_in
    count = len(FAULT_SHAPES)
    sources, (base, mat, lfw, slab, spots) = refs[:count], refs[count : count + 5]
    held = refs[count + 5 : -1]
    sem = refs[-1].at[count]
    fetch = fetches(sources, held, refs[-1])
    lift, fme, fse, mine, keep, fmf, live, fsf = held
    window = base.at[:, 0:8, :]
    read_slab = pltpu.make_async_copy(window, slab, sem)
    read_slab.start()
    for copy in fetch[:3]:
        copy.wait()
    lfw[...] = left3(mat, [(0, f * NBP, lift[f]) for f in range(4)], 16, 96)
    for n, elem in enumerate((fme, fse)):
        spots[n * SLOTS : (n + 1) * SLOTS, :] = one_hot_t(elem[...], E_DEV)
    for copy in fetch[3:]:
        copy.wait()

    def tile(ref, n):
        return ref[pl.ds(n, DEVICES, stride=TILES), :]

    def pair(ref, n):
        return jnp.concatenate([tile(ref, 2 * n), tile(ref, 2 * n + 1)], axis=1)

    def side(one, other, load, state, kept, sign, alive, face, rows):
        pull, slip = friction(0.5 * (pair(theirs, other[0]) + pair(mine, one[0])), pair(mine, one[1]) + pair(theirs, other[1]), load, state)
        right = []
        for t in (pull - kept, sign * slip):
            x = jnp.concatenate([to_slots(t[:, 0:LANES]), to_slots(t[:, LANES:256])], axis=0)
            right.append(stack3(x))
        added = dot(lfw[...], jnp.concatenate(right, axis=1))
        sums = []
        for k in range(2):
            at = slice(k * SLOTS, (k + 1) * SLOTS)
            y = added[0:NBP, at]
            for f in range(1, 4):
                y = jnp.where(face == f, added[f * NBP : (f + 1) * NBP, at], y)
            sums.append(y * alive)
        hi, lo = split(jnp.concatenate(sums, axis=0))
        return dot(jnp.concatenate([hi, lo], axis=0), spots[rows, :])

    minus = side(
        (2, 3), (0, 1), pair(mine, 4), pair(mine, 5), keep[:, 256:512], -0.5,
        live[...].astype(F32), fmf[...], slice(0, SLOTS),
    )
    far = to_slots(tile(theirs, 12))[0:1]
    plus = side(
        (0, 1), (2, 3), pair(theirs, 4), pair(theirs, 5), keep[:, 0:256], 0.5,
        far, fsf[...], slice(SLOTS, 2 * SLOTS),
    )
    both = minus + plus
    delta = both[0:48] + both[48:96]
    read_slab.wait()
    for b in range(NB):
        for k in range(2):
            row = slice(FAULT_ROWS[1 + k], FAULT_ROWS[1 + k] + 1)
            slab[b, row, :] = slab[b, row, :] + delta[k * NBP + b : k * NBP + b + 1, :]
    write = pltpu.make_async_copy(slab, window, sem)
    write.start()
    write.wait()


def whole(shape):
    return pl.BlockSpec(shape, lambda *i: (0,) * len(shape))


def lanes(*lead, width=LANES):
    return pl.BlockSpec(lead + (width,), lambda c: (0,) * len(lead) + (c,))


def wide(*lead):
    return lanes(*lead, width=WIDE)


def per_device(
    dofs, star, kdiff, couple, omega, flux_minus, flux_plus, area, face_proj, face_lift,
    nbr_elem, nbr_face, weight_class, send_rows, fault_send_elem, fault_send_face,
    fault_minus_elem, fault_minus_face, fault_live, normal_load, state,
):
    shape = jax.ShapeDtypeStruct
    wc = weight_class.reshape(1, E_DEV)
    dofs = jnp.transpose(dofs, (1, 0, 2))
    star = jnp.transpose(star, (1, 2, 0, 3))
    face_proj = jnp.transpose(face_proj, (0, 2, 1))
    rim = whole((NE, NB, BND))
    anywhere = pl.BlockSpec(memory_space=pl.ANY)
    outside = pl.BlockSpec(memory_space=pltpu.HBM)
    params = pltpu.CompilerParams(vmem_limit_bytes=VMEM)
    small = pltpu.CompilerParams(vmem_limit_bytes=VMEM_SMALL)
    integ, ihl, fhl, s0, s1, s2, s3 = pl.pallas_call(
        predict_kernel,
        grid=(CHUNKS // PAIR,),
        in_specs=[
            wide(NB, NQ), wide(NE, NE, 3), wide(MECH, 6), wide(MECH), wide(1),
            whole((3, NB, NB)), whole((4, BND)),
        ],
        out_specs=[
            wide(NQ, NBP), whole((2 * ROWS, E_DEV)), whole((160, E_DEV)), rim, rim, rim, rim,
        ],
        out_shape=[
            shape((NQ, NBP, E_DEV), F32), shape((2 * ROWS, E_DEV), BF), shape((160, E_DEV), BF),
            *[pltpu.HBM((NE, NB, BND), F32)] * 4,
        ],
        scratch_shapes=[
            pltpu.VMEM((NQ, NBP, WIDE), F32), pltpu.VMEM((80, LANES), F32),
            pltpu.VMEM((32, 240), BF),
        ],
        compiler_params=params,
        name="predict",
    )(dofs, star, couple, omega, wc, kdiff, send_rows)
    out, keep = pl.pallas_call(
        slot_kernel,
        in_specs=[anywhere] * len(SLOT_SHAPES),
        out_specs=[anywhere] * 2,
        out_shape=[shape((DEVICES * TILES, LANES), F32), shape((DEVICES, 4 * LANES), F32)],
        scratch_shapes=[
            pltpu.VMEM((64, LANES), F32), pltpu.VMEM((64, 96), BF),
            pltpu.VMEM((DEVICES * TILES, LANES), F32), pltpu.VMEM((DEVICES, 4 * LANES), F32),
            *[pltpu.VMEM(n, t) for n, t in zip(SLOT_SHAPES, SLOT_TYPES)],
            pltpu.SemaphoreType.DMA((len(SLOT_SHAPES),)),
        ],
        compiler_params=params,
        name="slots",
    )(
        face_proj, fhl, fault_send_elem, fault_send_face, fault_minus_elem, fault_minus_face,
        fault_live, normal_load, state,
    )
    ns, nd = lax.axis_size("strike"), lax.axis_size("depth")

    def swap(x, axis, n, first):
        ends = [(i, (i + 1) % n) for i in range(first, n, 2)]
        return lax.ppermute(x, axis, ends + [(j, i) for i, j in ends])

    r0 = swap(s0, "strike", ns, 0)
    r1 = swap(s1, "strike", ns, 1)
    r2 = swap(s2, "depth", nd, 0)
    r3 = swap(s3, "depth", nd, 1)
    r0, r1, r2, r3, sent = lax.optimization_barrier((r0, r1, r2, r3, out))
    theirs = lax.all_to_all(
        sent.reshape(DEVICES, 1, TILES * LANES), ("strike", "depth"), split_axis=0, concat_axis=0, tiled=True
    ).reshape(DEVICES * TILES, LANES)
    base = pl.pallas_call(
        element_kernel,
        grid=(CHUNKS,),
        in_specs=[
            lanes(NQ, NBP), lanes(NB, NQ), lanes(NE, NE, 3), lanes(MECH, 6), lanes(MECH),
            lanes(NE, NE), lanes(NE, NE), lanes(4), lanes(4), lanes(4),
            whole((2 * ROWS, E_DEV)), rim, rim, rim, rim,
            whole((3, NB, NB)), whole((4, NP, NB)), whole((4, NP, NB)),
        ],
        out_specs=lanes(NB, NQ),
        out_shape=pltpu.HBM((NB, NQ, E_DEV), F32),
        scratch_shapes=[
            pltpu.VMEM((80, LANES), F32),
            pltpu.VMEM((32, 240), BF), pltpu.VMEM((64, 96), BF), pltpu.VMEM((32, 192), BF),
            pltpu.VMEM((96, 96), BF), pltpu.VMEM((2 * ROWS, 4 * BND), BF),
            pltpu.VMEM((NQ, NBP, LANES), F32),
        ],
        compiler_params=params,
        name="elements",
    )(
        integ, dofs, star, couple, omega, flux_minus, flux_plus, area, nbr_elem, nbr_face,
        ihl, r0, r1, r2, r3, kdiff, face_proj, face_lift,
    )
    result = pl.pallas_call(
        fault_kernel,
        in_specs=[outside, pl.BlockSpec(memory_space=pltpu.VMEM)] + [outside] * len(FAULT_SHAPES),
        out_specs=outside,
        out_shape=shape((NB, NQ, E_DEV), F32),
        input_output_aliases={0: 0},
        scratch_shapes=[
            pltpu.VMEM((64, LANES), F32), pltpu.VMEM((96, 48), BF),
            pltpu.VMEM((NB, 8, E_DEV), F32), pltpu.VMEM((2 * SLOTS, E_DEV), BF),
            *[pltpu.VMEM(n, t) for n, t in zip(FAULT_SHAPES, FAULT_TYPES)],
            pltpu.SemaphoreType.DMA((len(FAULT_SHAPES) + 1,)),
        ],
        compiler_params=small,
        name="fault",
    )(
        base, pltpu.with_memory_space_constraint(theirs, pltpu.VMEM),
        *[
            pltpu.with_memory_space_constraint(x, pltpu.HBM)
            for x in (
                face_lift, fault_minus_elem, fault_send_elem, sent, keep, fault_minus_face, fault_live,
                fault_send_face,
            )
        ],
    )
    return jnp.transpose(result, (1, 0, 2))


def solution(mesh):
    both = ("strike", "depth")
    split_1, split_2, split_3 = P(None, both), P(None, None, both), P(None, None, None, both)
    in_specs = (
        split_2, split_3, P(), split_2, split_1, split_2, split_2, split_1, P(), P(),
        split_1, split_1, P(both), split_1,
        *[P(both, None)] * 5, P(both, None, None), P(both, None, None),
    )
    return jax.shard_map(
        per_device, mesh=mesh, in_specs=in_specs, out_specs=split_2, check_vma=False
    )
```
